32 devices in a mesh: dp: 8 (over z, x), seq: 4 (over y, core).
Axes of the slice: x: 2, y: 2, z: 4, core: 2. Of those that a mesh axis runs over, the one named last changes fastest.
Arguments:
- tokens: bfloat16 [2, 16, 1024, 1536], P(None, 'dp', 'seq'), may hold values from -6 to 6
- cotangent: bfloat16 [2, 16, 1024, 1536], P(None, 'dp', 'seq'), may hold values from -6 to 6
- lengths: int32 [2, 16], P(None, 'dp'), may hold values from 256 to 1024, as said below
- buckets: int32 [2047], replicated, may hold values from 0 to 31, as said below
- gain_one: bfloat16 [1536], P('dp'), may hold values from 0.25 to 1.75
- gain_two: bfloat16 [1536], P('dp'), may hold values from 0.25 to 1.75
- table: bfloat16 [32, 12], P('dp'), may hold values from -3 to 3
- w_query: bfloat16 [1536, 768], P('dp'), may hold values from -0.078125 to 0.078125
- w_key: bfloat16 [1536, 768], P('dp'), may hold values from -0.078125 to 0.078125
- w_value: bfloat16 [1536, 768], P('dp'), may hold values from -0.15625 to 0.15625
- w_out: bfloat16 [768, 1536], P(None, 'dp'), may hold values from -1.75 to 1.75
- w_gate: bfloat16 [1536, 3968], P('dp'), may hold values from -0.15625 to 0.15625
- w_up: bfloat16 [1536, 3968], P('dp'), may hold values from -0.15625 to 0.15625
- w_down: bfloat16 [3968, 1536], P(None, 'dp'), may hold values from -0.09375 to 0.09375
Outputs:
- output: bfloat16 [2, 16, 1024, 1536], P(None, 'dp', 'seq')
- input_grad: float32 [2, 16, 1024, 1536], P(None, 'dp', 'seq')
- grad_gain_one: float32 [1536], P('dp')
- grad_gain_two: float32 [1536], P('dp')
- grad_table: float32 [32, 12], P('dp')
- grad_query: float32 [1536, 768], P('dp')
- grad_key: float32 [1536, 768], P('dp')
- grad_value: float32 [1536, 768], P('dp')
- grad_out: float32 [768, 1536], P(None, 'dp')
- grad_gate: float32 [1536, 3968], P('dp')
- grad_up: float32 [1536, 3968], P('dp')
- grad_down: float32 [3968, 1536], P(None, 'dp')
The draws below stay inside these ranges and needn't reach their ends.
Inputs may be any that keep to these rules, and one draw needn't show every extreme that they name: `lengths`: among the 4 rows that one dp index holds over all micro-batches, one is 1024 long. `buckets`: entry 1023 + o is the bucket of the offset o = key position - query position: 0 at o = 0, below 16 for o < 0, 16 or more for o > 0, never falling as |o| grows on either side.
All inputs are finite; a program needn't handle non-finite values.
Results may differ from the reference program's by a relative error of at most 0.014.
The reference program's roundings to bfloat16 on the way count: a program that leaves them out, or rounds other values in their place, can miss the bound.
Values may be sent and summed in bfloat16 or wider, within the bound.
A program may use at most 320 MiB of HBM per device.

```python
import jax
import jax.numpy as jnp
from jax import lax

D = 1536
HEADS = 12
HD = 64
FF = 3968
BUCKETS = 32
ROW_LEN = 1024
ROWS = 2
MICRO = 2
BATCH = 16


def draw_lengths(key, part):
    key = jax.random.fold_in(key, 11)
    key_lengths, key_pick = jax.random.split(key)
    groups = BATCH // ROWS
    spread = jax.random.randint(key_lengths, (groups, MICRO * ROWS), ROW_LEN // 4, ROW_LEN + 1)
    chosen = jax.random.randint(key_pick, (groups, 1), 0, MICRO * ROWS)
    filled = jnp.where(jnp.arange(MICRO * ROWS)[None, :] == chosen, ROW_LEN, spread)
    return filled.reshape(groups, MICRO, ROWS).transpose(1, 0, 2).reshape(MICRO, BATCH).astype(jnp.int32)


def draw_buckets(key, part):
    key = jax.random.fold_in(key, 23)
    halves = BUCKETS // 2
    levels = jnp.arange(halves - 1)
    widths = jax.random.randint(key, (halves - 1,), 1, 1 + 2 ** (levels // 2))
    limits = jnp.cumsum(widths)
    offsets = jnp.arange(2 * ROW_LEN - 1) - (ROW_LEN - 1)
    magnitude = jnp.abs(offsets)
    counted = jnp.sum((magnitude[:, None] >= limits[None, :]).astype(jnp.int32), axis=1)
    return (jnp.where(offsets > 0, halves, 0) + counted).astype(jnp.int32)


def block_scale(rng, shape, shards, smallest, high):
    def one(axis_at, shards_of):
        steps = jax.random.uniform(jax.random.fold_in(jax.random.fold_in(rng, 6), axis_at), (shards_of,), jnp.float32, smallest / len(shards), high / len(shards))
        return jnp.repeat(jnp.exp(steps), shape[axis_at] // shards_of).reshape((-1,) + (1,) * (len(shape) - axis_at - 1))

    level = one(*shards[0])
    for cut in shards[1:]:
        level = level * one(*cut)
    return level


def scatter_about(rng, shape, scale, reach, shards=(), dtype=jnp.bfloat16):
    level = block_scale(rng, shape, shards, -0.22, 0.18) if shards else 1.0
    array = jax.random.normal(rng, shape, jnp.float32) * scale * level
    return jnp.minimum(jnp.maximum(array, -reach), reach).astype(dtype)


def setup_inputs(seed: int = 0) -> dict:
    streams_of = jax.random.split(jax.random.key(seed), 15)
    tokens = scatter_about(streams_of[0], (MICRO, BATCH, ROW_LEN, D), 1.0, 6.0, ((1, 8), (2, 4)))
    cotangent = scatter_about(streams_of[1], (MICRO, BATCH, ROW_LEN, D), 1.0, 6.0, ((1, 8), (2, 4)))
    lengths = draw_lengths(jax.random.fold_in(streams_of[14], 71), 0)
    buckets = draw_buckets(jax.random.fold_in(streams_of[14], 71), 0)
    gain_one = jnp.clip(1.0 + 0.15 * jax.random.normal(streams_of[4], (D,), jnp.float32), 0.25, 1.75).astype(jnp.bfloat16)
    gain_two = jnp.clip(1.0 + 0.15 * jax.random.normal(streams_of[5], (D,), jnp.float32), 0.25, 1.75).astype(jnp.bfloat16)
    table = scatter_about(streams_of[6], (BUCKETS, HEADS), 0.5, 3.0, ((0, 8),))
    w_query = scatter_about(streams_of[7], (D, HEADS * HD), (4 * D) ** -0.5, 0.078125, ((0, 8),))
    w_key = scatter_about(streams_of[8], (D, HEADS * HD), (4 * D) ** -0.5, 0.078125, ((0, 8),))
    w_value = scatter_about(streams_of[9], (D, HEADS * HD), D ** -0.5, 0.15625, ((0, 8),))
    w_out = scatter_about(streams_of[10], (HEADS * HD, D), HEADS ** -0.5, 1.75, ((1, 8),))
    w_gate = scatter_about(streams_of[11], (D, FF), D ** -0.5, 0.15625, ((0, 8),))
    w_up = scatter_about(streams_of[12], (D, FF), D ** -0.5, 0.15625, ((0, 8),))
    w_down = scatter_about(streams_of[13], (FF, D), FF ** -0.5, 0.09375, ((1, 8),))
    return {"tokens": tokens, "cotangent": cotangent, "lengths": lengths, "buckets": buckets, "gain_one": gain_one, "gain_two": gain_two, "table": table, "w_query": w_query, "w_key": w_key, "w_value": w_value, "w_out": w_out, "w_gate": w_gate, "w_up": w_up, "w_down": w_down}


@jax.custom_vjp
def low(v):
    return lax.optimization_barrier(v.astype(jnp.bfloat16)).astype(jnp.float32)

@jax.custom_vjp
def low_back(v):
    return v

def low_keep(v):
    return (low(v), None)

def low_pass(kept, grad):
    return (grad,)

def back_keep(v):
    return (v, None)

def back_low(kept, grad):
    return (low(grad),)
low.defvjp(low_keep, low_pass)
low_back.defvjp(back_keep, back_low)
eps = 1e-06
highest = lax.Precision.HIGHEST

def rms_scale(values, gain):
    return values * lax.rsqrt(lax.optimization_barrier(jnp.mean(values * values, axis=-1, keepdims=True)) + eps) * gain

def layer(params, rows_in, row_lengths, bucket_index):
    gain_one, gain_two, table, w_query, w_key, w_value, w_out, w_gate, w_up, w_down = params
    count, seq_len, width = rows_in.shape
    heads = table.shape[1]
    normed = low(rms_scale(rows_in, gain_one))

    def project(weight):
        made = jnp.einsum('rld,de->rle', normed, weight, precision=highest)
        return low_back(low(made)).reshape(count, seq_len, heads, -1)
    query = project(w_query)
    key = project(w_key)
    value = project(w_value)
    raw = low_back(jnp.einsum('rqhe,rkhe->rhqk', query, key, precision=highest))
    bias = jnp.transpose(table[bucket_index], (2, 0, 1))
    valid = jnp.arange(seq_len)[None, :] < row_lengths[:, None]
    scores = jnp.where(valid[:, None, None, :], raw + bias[None], -1e+30)
    probs = low(jax.nn.softmax(scores, axis=-1))
    mixed = jnp.einsum('rhqk,rkhe->rqhe', probs, value, precision=highest)
    mixed = low_back(low(mixed)).reshape(count, seq_len, -1)
    resid = rows_in + low_back(jnp.einsum('rle,ed->rld', mixed, w_out, precision=highest))
    normed_two = low(rms_scale(resid, gain_two))
    gate = low_back(jnp.einsum('rld,df->rlf', normed_two, w_gate, precision=highest))
    up = low_back(jnp.einsum('rld,df->rlf', normed_two, w_up, precision=highest))
    hidden = low(jax.nn.gelu(gate, approximate=True) * up)
    return resid + low_back(jnp.einsum('rlf,fd->rld', hidden, w_down, precision=highest))

def reference(tokens, cotangent, lengths, buckets, gain_one, gain_two, table, w_query, w_key, w_value, w_out, w_gate, w_up, w_down):
    params = tuple((weight.astype(jnp.float32) for weight in (gain_one, gain_two, table, w_query, w_key, w_value, w_out, w_gate, w_up, w_down)))
    places = jnp.arange(ROW_LEN)
    bucket_index = buckets[places[None, :] - places[:, None] + ROW_LEN - 1]
    pairs = MICRO * BATCH // 2
    inputs = tokens.astype(jnp.float32).reshape(pairs, 2, ROW_LEN, D)
    cotangents = cotangent.astype(jnp.float32).reshape(pairs, 2, ROW_LEN, D)
    row_lengths = lengths.reshape(pairs, 2)

    def one_pair(totals, item):
        rows_in, rows_cot, pair_lengths = item
        result, pull = jax.vjp(lambda weights, values: layer(weights, values, pair_lengths, bucket_index), params, rows_in)
        grads, input_grad = pull(rows_cot)
        totals = jax.tree.map(jnp.add, totals, grads)
        return (totals, (result.astype(jnp.bfloat16), input_grad.astype(jnp.float32)))
    zeros = tuple((jnp.zeros_like(weight) for weight in params))
    totals, (results, input_grads) = lax.scan(one_pair, zeros, (inputs, cotangents, row_lengths))
    totals = tuple((total.astype(jnp.float32) for total in totals))
    return (results.reshape(MICRO, BATCH, ROW_LEN, D), input_grads.reshape(MICRO, BATCH, ROW_LEN, D), totals[0], totals[1], totals[2], totals[3], totals[4], totals[5], totals[6], totals[7], totals[8], totals[9])
```

```python
import functools

import jax
import jax.numpy as jnp
from jax import lax
from jax.experimental import pallas as pl
from jax.experimental.pallas import tpu as pltpu
from jax.sharding import PartitionSpec as P

eps = 1e-06
masked_value = -1e30
highest = lax.Precision.HIGHEST
gelu_scale = 0.7978845608028654
gelu_cubic = 0.044715
LANES = 128
VMEM_LIMIT = 56 * 1024 * 1024
NT = (((1,), (1,)), ((), ()))
NN = (((1,), (0,)), ((), ()))
TN = (((0,), (0,)), ((), ()))


def dot32(a, b, dims):
    return lax.dot_general(a, b, dims, preferred_element_type=jnp.float32)


def toeplitz_strip(diag_row, span):
    wide = jnp.broadcast_to(diag_row, (LANES, span))
    return pltpu.roll(wide, span - (LANES - 1), 1, stride=1, stride_axis=0)


def with_mask_lane(key_pair, lanes, here, spare, length):
    rows = lax.broadcasted_iota(jnp.int32, key_pair.shape, 0)
    mask = jnp.where(rows < length, 0.0, masked_value).astype(key_pair.dtype)
    zero = jnp.zeros_like(key_pair)
    return jnp.where(here, key_pair, jnp.where(lanes == spare, mask, zero))


def attend_kernel(head_dim, block, len_ref, diag_ref, q_ref, k_ref, v_ref, mixed_ref, lse_ref, strip, keys):
    step = pl.program_id(1)
    seq_len = k_ref.shape[0]
    span = diag_ref.shape[-1]
    length = len_ref[0]
    per = LANES // head_dim
    lanes_k = lax.broadcasted_iota(jnp.int32, (seq_len, LANES), 1)
    lanes_q = lax.broadcasted_iota(jnp.int32, (block, LANES), 1)

    @pl.when(step == 0)
    def _():
        for head in range(per):
            strip[head] = toeplitz_strip(diag_ref[head], span)
            here = lanes_k // head_dim == head
            spare = ((head + 1) % per) * head_dim
            keys[head] = with_mask_lane(k_ref[...], lanes_k, here, spare, length)

    mixed = None
    for head in range(per):
        here = lanes_q // head_dim == head
        spare = ((head + 1) % per) * head_dim
        one = (lanes_q == spare).astype(q_ref.dtype)
        query = jnp.where(here, q_ref[...], one)
        raw = dot32(query, keys[head], NT)
        parts = []
        for sub in range(block // LANES):
            offset = seq_len - LANES - (step * block + sub * LANES)
            offset = pl.multiple_of(offset, LANES)
            parts.append(raw[sub * LANES : (sub + 1) * LANES] + strip[head, :, pl.ds(offset, seq_len)])
        scores = jnp.concatenate(parts, axis=0)
        top = jnp.max(scores, axis=1, keepdims=True)
        expo = jnp.exp(scores - top)
        total = jnp.sum(expo, axis=1, keepdims=True)
        made = dot32(expo.astype(jnp.bfloat16), v_ref[...], NN) / total
        mixed = made if mixed is None else jnp.where(here, made, mixed)
        lse = jnp.broadcast_to(top + jnp.log(total), (block, LANES))
        lse_ref[head] = lse.T[:1]
    mixed_ref[...] = mixed.astype(mixed_ref.dtype)


def attend(qkv, diag, length, head_dim, block=256):
    seq_len, cols = qkv.shape[0], qkv.shape[1] // 3
    pairs = cols // LANES
    per = LANES // head_dim
    span = diag.shape[-1]
    flops = 2 * 2 * seq_len * seq_len * LANES * 2 * cols // head_dim
    return pl.pallas_call(
        functools.partial(attend_kernel, head_dim, block),
        grid=(pairs, seq_len // block),
        in_specs=[
            pl.BlockSpec(memory_space=pltpu.SMEM),
            pl.BlockSpec((per, 1, span), lambda p, b: (p, 0, 0)),
            pl.BlockSpec((block, LANES), lambda p, b: (b, p)),
            pl.BlockSpec((seq_len, LANES), lambda p, b: (0, pairs + p)),
            pl.BlockSpec((seq_len, LANES), lambda p, b: (0, 2 * pairs + p)),
        ],
        out_specs=[
            pl.BlockSpec((block, LANES), lambda p, b: (b, p)),
            pl.BlockSpec((per, 1, block), lambda p, b: (p, 0, b)),
        ],
        out_shape=[
            jax.ShapeDtypeStruct((seq_len, cols), jnp.bfloat16),
            jax.ShapeDtypeStruct((cols // head_dim, 1, seq_len), jnp.float32),
        ],
        scratch_shapes=[
            pltpu.VMEM((per, LANES, span), jnp.float32),
            pltpu.VMEM((per, seq_len, LANES), jnp.bfloat16),
        ],
        compiler_params=pltpu.CompilerParams(vmem_limit_bytes=VMEM_LIMIT),
        cost_estimate=pl.CostEstimate(flops=flops, bytes_accessed=8 * seq_len * cols, transcendentals=0),
        name="attend",
    )(length, diag, qkv, qkv, qkv)


def attend_back_kernel(
    head_dim, block, len_ref, diag_ref, q_ref, k_ref, v_ref, do_ref, lse_ref,
    dq_ref, dk_ref, dv_ref, dd_ref, strip, keys, acc_bias, acc_k, acc_v,
):
    step = pl.program_id(1)
    steps = pl.num_programs(1)
    seq_len = k_ref.shape[0]
    span = diag_ref.shape[-1]
    length = len_ref[0]
    per = LANES // head_dim
    lanes_k = lax.broadcasted_iota(jnp.int32, (seq_len, LANES), 1)
    lanes_q = lax.broadcasted_iota(jnp.int32, (block, LANES), 1)
    subs = block // LANES

    @pl.when(step == 0)
    def _():
        for head in range(per):
            strip[head] = toeplitz_strip(diag_ref[head], span).T
            here = lanes_k // head_dim == head
            spare = ((head + 1) % per) * head_dim
            keys[head] = with_mask_lane(k_ref[...], lanes_k, here, spare, length)
        acc_bias[...] = jnp.zeros_like(acc_bias)
        acc_k[...] = jnp.zeros_like(acc_k)
        acc_v[...] = jnp.zeros_like(acc_v)

    grad_query = None
    for head in range(per):
        here = lanes_q // head_dim == head
        spare = ((head + 1) % per) * head_dim
        zero = jnp.zeros_like(q_ref[...])
        one = (lanes_q == spare).astype(q_ref.dtype)
        query = jnp.where(here, q_ref[...], zero)
        grad = jnp.where(here, do_ref[...], zero)
        raw = dot32(keys[head], query + one, NT)
        grad_probs = dot32(v_ref[...], grad, NT)
        parts = []
        offsets = []
        for sub in range(subs):
            offset = seq_len - LANES - (step * block + sub * LANES)
            offset = pl.multiple_of(offset, LANES)
            offsets.append(offset)
            parts.append(raw[:, sub * LANES : (sub + 1) * LANES] + strip[head, pl.ds(offset, seq_len), :])
        scores = jnp.concatenate(parts, axis=1)
        probs = jnp.exp(scores - lse_ref[head])
        product = probs * grad_probs
        inner = jnp.sum(product, axis=0, keepdims=True)
        grad_scores = product - probs * inner
        for sub in range(subs):
            rows = pl.ds(offsets[sub], seq_len)
            acc_bias[head, rows, :] += grad_scores[:, sub * LANES : (sub + 1) * LANES]
        rounded = grad_scores.astype(jnp.bfloat16)
        acc_v[...] += dot32(probs.astype(jnp.bfloat16), grad, NN)
        acc_k[...] += dot32(rounded, query, NN)
        made = dot32(rounded, k_ref[...], TN)
        grad_query = made if grad_query is None else jnp.where(here, made, grad_query)
    dq_ref[...] = grad_query.astype(dq_ref.dtype)

    @pl.when(step == steps - 1)
    def _():
        dk_ref[...] = acc_k[...].astype(dk_ref.dtype)
        dv_ref[...] = acc_v[...].astype(dv_ref.dtype)
        row = lax.broadcasted_iota(jnp.int32, (LANES, LANES), 0)
        col = lax.broadcasted_iota(jnp.int32, (LANES, LANES), 1)
        flip = (row + col == LANES - 1).astype(jnp.float32)
        for head in range(per):
            turned = lax.dot_general(
                flip, acc_bias[head], NT, precision=lax.Precision.HIGHEST, preferred_element_type=jnp.float32
            )
            aligned = pltpu.roll(turned, 0, 1, stride=1, stride_axis=0)
            dd_ref[head] = jnp.sum(aligned, axis=0, keepdims=True)


def attend_back(qkv, grad_mixed, lse, diag, length, head_dim, block=256):
    seq_len, cols = qkv.shape[0], qkv.shape[1] // 3
    pairs = cols // LANES
    per = LANES // head_dim
    span = diag.shape[-1]
    flops = 5 * 2 * seq_len * seq_len * LANES * 2 * cols // head_dim
    whole = lambda p, b: (0, p)
    part = lambda p, b: (b, p)
    flat = jax.ShapeDtypeStruct((seq_len, cols), jnp.bfloat16)
    return pl.pallas_call(
        functools.partial(attend_back_kernel, head_dim, block),
        grid=(pairs, seq_len // block),
        in_specs=[
            pl.BlockSpec(memory_space=pltpu.SMEM),
            pl.BlockSpec((per, 1, span), lambda p, b: (p, 0, 0)),
            pl.BlockSpec((block, LANES), part),
            pl.BlockSpec((seq_len, LANES), lambda p, b: (0, pairs + p)),
            pl.BlockSpec((seq_len, LANES), lambda p, b: (0, 2 * pairs + p)),
            pl.BlockSpec((block, LANES), part),
            pl.BlockSpec((per, 1, block), lambda p, b: (p, 0, b)),
        ],
        out_specs=[
            pl.BlockSpec((block, LANES), part),
            pl.BlockSpec((seq_len, LANES), whole),
            pl.BlockSpec((seq_len, LANES), whole),
            pl.BlockSpec((per, 1, span), lambda p, b: (p, 0, 0)),
        ],
        out_shape=[flat, flat, flat, jax.ShapeDtypeStruct(diag.shape, jnp.float32)],
        scratch_shapes=[
            pltpu.VMEM((per, span, LANES), jnp.float32),
            pltpu.VMEM((per, seq_len, LANES), jnp.bfloat16),
            pltpu.VMEM((per, span, LANES), jnp.float32),
            pltpu.VMEM((seq_len, LANES), jnp.float32),
            pltpu.VMEM((seq_len, LANES), jnp.float32),
        ],
        compiler_params=pltpu.CompilerParams(vmem_limit_bytes=VMEM_LIMIT),
        cost_estimate=pl.CostEstimate(flops=flops, bytes_accessed=16 * seq_len * cols, transcendentals=0),
        name="attend_back",
    )(length, diag, qkv, qkv, qkv, grad_mixed, lse)


def gated_kernel(width, a_ref, d_ref, g_ref, e_ref):
    gate = dot32(a_ref[...], g_ref[:, :width], NN)
    up = dot32(a_ref[...], g_ref[:, width : 2 * width], NN)
    grad = dot32(d_ref[...], g_ref[:, 2 * width :], NN)
    square = gate * gate
    inner = gelu_scale * gate * (1.0 + gelu_cubic * square)
    turn = jnp.tanh(inner)
    half = 0.5 * (1.0 + turn)
    act = gate * half
    slope = half + 0.5 * gate * (1.0 - turn * turn) * gelu_scale * (1.0 + 3.0 * gelu_cubic * square)
    e_ref[:, :width] = (grad * up * slope).astype(e_ref.dtype)
    e_ref[:, width : 2 * width] = (grad * act).astype(e_ref.dtype)
    e_ref[:, 2 * width :] = (act * up).astype(e_ref.dtype)


def gated_chunk(normed, down_in, weights, tile=256):
    tokens, width = normed.shape[0], weights.shape[1] // 3
    depth = normed.shape[1]
    return pl.pallas_call(
        functools.partial(gated_kernel, width),
        grid=(tokens // tile,),
        in_specs=[
            pl.BlockSpec((tile, depth), lambda t: (t, 0)),
            pl.BlockSpec((tile, depth), lambda t: (t, 0)),
            pl.BlockSpec((depth, 3 * width), lambda t: (0, 0)),
        ],
        out_specs=pl.BlockSpec((tile, 3 * width), lambda t: (t, 0)),
        out_shape=jax.ShapeDtypeStruct((tokens, 3 * width), jnp.bfloat16),
        compiler_params=pltpu.CompilerParams(vmem_limit_bytes=VMEM_LIMIT),
        cost_estimate=pl.CostEstimate(
            flops=6 * tokens * depth * width, bytes_accessed=2 * (2 * tokens * depth + 6 * depth * width), transcendentals=0
        ),
        name="gated_chunk",
    )(normed, down_in, weights)


def back_kernel(count, *refs):
    total = None
    for index in range(count):
        made = dot32(refs[index][...], refs[count + index][...], NT)
        total = made if total is None else total + made
    refs[-1][...] = total.astype(refs[-1].dtype)


def back_sum(pieces, weights, start, width, block_at, half, dtype, tile=256):
    count = len(pieces)
    rows, _, _ = pieces[0].shape
    depth = weights[0].shape[0]
    tile = min(tile, half)
    steps = half // tile

    def body_of(start_ref, *refs):
        back_kernel(count, *refs)

    return pl.pallas_call(
        body_of,
        grid_spec=pltpu.PrefetchScalarGridSpec(
            num_scalar_prefetch=1,
            grid=(rows, steps),
            in_specs=[pl.BlockSpec((None, tile, width), lambda r, t, s: (r, s[0] * steps + t, block_at))] * count
            + [pl.BlockSpec((depth, width), lambda r, t, s: (0, block_at))] * count,
            out_specs=pl.BlockSpec((None, tile, depth), lambda r, t, s: (r, t, 0)),
        ),
        out_shape=jax.ShapeDtypeStruct((rows, half, depth), dtype),
        compiler_params=pltpu.CompilerParams(vmem_limit_bytes=VMEM_LIMIT),
        cost_estimate=pl.CostEstimate(
            flops=2 * rows * half * depth * width * count,
            bytes_accessed=2 * count * width * (rows * half + depth) + 4 * rows * half * depth,
            transcendentals=0,
        ),
        name="back_sum",
    )(start, *pieces, *weights)


def ring_order(count):
    if count % 4 or count < 8:
        return list(range(count))
    long, short = 4, count // 4
    walk = []
    for line in range(long):
        columns = range(1, short) if line % 2 == 0 else range(short - 1, 0, -1)
        walk += [line * short + column for column in columns]
    return walk + [line * short for line in range(long - 1, -1, -1)]


class Ring:
    def __init__(self, count):
        order = ring_order(count)
        place = [0] * count
        for at, index in enumerate(order):
            place[index] = at
        self.count = count
        self.order = jnp.array(order, jnp.int32)
        self.here = jnp.array(place, jnp.int32)[lax.axis_index("dp")]
        self.ahead = [(order[i], order[(i + 1) % count]) for i in range(count)]
        self.behind = [(order[i], order[(i - 1) % count]) for i in range(count)]

    def owner(self, shift):
        return self.order[(self.here + shift) % self.count]

    def send(self, block, forward):
        return lax.ppermute(block, "dp", self.ahead if forward else self.behind)

    def gather(self, shard):
        rows, cols = shard.shape
        cut = cols // 2
        far = self.count // 2
        whole = jnp.zeros((self.count * rows, cols), shard.dtype)

        def put(whole, block, shift, column=0):
            return lax.dynamic_update_slice(whole, block, (self.owner(shift) * rows, column))

        whole = put(whole, shard, 0)
        ahead = behind = shard
        for step in range(1, far):
            ahead, behind = self.send(ahead, True), self.send(behind, False)
            whole = put(put(whole, ahead, -step), behind, step)
        last = (ahead, behind)
        ahead, behind = self.send(ahead[:, :cut], True), self.send(behind[:, cut:], False)
        whole = put(put(whole, ahead, -far), behind, far, cut)
        return whole, last

    def scatter(self, local, cols):
        cut = cols // 2
        far = self.count // 2
        most = local(self.owner(far))
        ahead, behind = self.send(most[:, :cut], True), self.send(most[:, cut:], False)
        for step in range(far - 1, 0, -1):
            mine = local(self.owner(step))
            other = local(self.owner(-step))
            if step == far - 1:
                ahead = jnp.concatenate([add_low(mine[:, :cut], ahead), mine[:, cut:]], axis=1)
                behind = jnp.concatenate([other[:, :cut], add_low(other[:, cut:], behind)], axis=1)
            else:
                ahead, behind = add_low(mine, ahead), add_low(other, behind)
            ahead, behind = self.send(ahead, True), self.send(behind, False)
        return local(self.owner(0)).astype(jnp.float32) + ahead.astype(jnp.float32) + behind.astype(jnp.float32)


def add_low(a, b):
    return (a.astype(jnp.float32) + b.astype(jnp.float32)).astype(jnp.bfloat16)


def body(
    tokens, cotangent, lengths, buckets, gain_one, gain_two, table,
    w_query, w_key, w_value, w_out, w_gate, w_up, w_down,
):
    micro, rows, local, width = tokens.shape
    seq_devices = lax.axis_size("seq")
    dp_devices = lax.axis_size("dp")
    seq_rank = lax.axis_index("seq")
    core = seq_rank % 2
    plane = seq_rank // 2
    planes = seq_devices // 2
    heads = table.shape[1]
    shard_rows, inner = w_query.shape
    head_dim = inner // heads
    half_inner = inner // 2
    hidden_units = w_gate.shape[1]
    pair_local = 2 * local
    seq_len = local * seq_devices
    first = core == 0
    core_pairs = [(i, i ^ 1) for i in range(seq_devices)]
    plane_groups = [[2 * p + c for p in range(planes)] for c in range(2)]
    ring = Ring(dp_devices)

    def swap_core(value):
        return lax.ppermute(value, "seq", core_pairs)

    def both_cores(own, other, axis):
        return jnp.concatenate([jnp.where(first, own, other), jnp.where(first, other, own)], axis=axis)

    def own_half(value, axis):
        return lax.dynamic_slice_in_dim(value, core * local, local, axis)

    def other_half(value, axis):
        return lax.dynamic_slice_in_dim(value, (1 - core) * local, local, axis)

    def core_columns(weight, split):
        low, high = weight[:, :split], weight[:, split:]
        high = jnp.pad(high, ((0, 0), (0, split - high.shape[1])))
        return jnp.where(first, low, high)

    chunk = 512
    chunks = -(-(hidden_units // 2) // chunk)
    split = chunks * chunk
    if split > hidden_units:
        split = hidden_units
    attn_shard = jnp.concatenate(
        [core_columns(w, half_inner) for w in (w_query, w_key, w_value, w_out.T)], axis=1
    )
    up_parts = [core_columns(w, split) for w in (w_gate, w_up, w_down.T)]
    chunk_shards = [
        jnp.concatenate([w[:, n * chunk : (n + 1) * chunk] for w in up_parts], axis=1) for n in range(chunks)
    ]

    small = jnp.concatenate([gain_one, gain_two, table.reshape(-1)])[None]
    small = lax.all_gather(small, "dp", axis=0, tiled=True).astype(jnp.float32)
    gain_first = small[:, :shard_rows].reshape(-1)
    gain_second = small[:, shard_rows : 2 * shard_rows].reshape(-1)
    full_table = small[:, 2 * shard_rows :].reshape(-1, heads)

    attn_weights, last = ring.gather(attn_shard)
    qkv_weights = attn_weights[:, : 3 * half_inner]
    out_own = attn_weights[:, 3 * half_inner :]
    out_other = swap_core(out_own)
    out_pair = jnp.concatenate([out_own, out_other], axis=1)

    chunk_weights = []
    for shard in chunk_shards:
        shard, last = lax.optimization_barrier((shard, last))
        gathered, last = ring.gather(shard)
        chunk_weights.append(gathered)

    tokens_other = swap_core(tokens)
    cotangent_other = swap_core(cotangent)
    tokens_pair = both_cores(tokens, tokens_other, 2)
    down_in = both_cores(cotangent, cotangent_other, 2)

    core_heads = heads // 2
    head_splits = planes // rows
    item_heads = core_heads // head_splits
    item_cols = item_heads * head_dim
    padded_cols = -(-item_cols // LANES) * LANES
    padded_heads = padded_cols // head_dim
    item_row = plane // head_splits
    item_group = plane % head_splits
    head_start = core * core_heads + item_group * item_heads
    item_table = lax.dynamic_slice_in_dim(full_table, head_start, item_heads, 1)
    item_table = jnp.pad(item_table, ((0, 0), (0, padded_heads - item_heads)))
    levels = full_table.shape[0]
    bucket_hot = (buckets[:, None] == jnp.arange(levels)[None, :]).astype(jnp.float32)
    bucket_hot = jnp.pad(bucket_hot, ((0, 1), (0, 0)))
    diag = jnp.dot(item_table.T, bucket_hot.T, precision=highest)[:, None, :]

    def to_items(value, parts):
        if planes == 2 and rows == 2:
            mine = lax.dynamic_index_in_dim(value, plane, 0, keepdims=False)
            sent = lax.dynamic_index_in_dim(value, 1 - plane, 0, keepdims=False)
            got = lax.ppermute(sent, "seq", [(i, i ^ 2) for i in range(4)])
            low = plane == 0
            return jnp.concatenate([jnp.where(low, mine, got), jnp.where(low, got, mine)], axis=0)
        value = value.reshape(rows, pair_local, parts, head_splits, item_cols)
        value = value.transpose(0, 3, 1, 2, 4).reshape(planes, pair_local, parts * item_cols)
        value = lax.all_to_all(value, "seq", 0, 0, tiled=True, axis_index_groups=plane_groups)
        value = value.reshape(seq_len, parts, item_cols)
        value = jnp.pad(value, ((0, 0), (0, 0), (0, padded_cols - item_cols)))
        return value.reshape(seq_len, parts * padded_cols)

    def from_items(values):
        parts = len(values)
        if planes == 2 and rows == 2:
            value = jnp.concatenate(values, axis=1)
            mine = lax.dynamic_slice_in_dim(value, plane * pair_local, pair_local, 0)
            sent = lax.dynamic_slice_in_dim(value, (1 - plane) * pair_local, pair_local, 0)
            got = lax.ppermute(sent, "seq", [(i, i ^ 2) for i in range(4)])
            low = plane == 0
            return jnp.stack([jnp.where(low, mine, got), jnp.where(low, got, mine)])
        value = jnp.concatenate([v[:, :item_cols] for v in values], axis=1)
        value = value.reshape(planes, pair_local, parts * item_cols)
        value = lax.all_to_all(value, "seq", 0, 0, tiled=True, axis_index_groups=plane_groups)
        value = value.reshape(rows, head_splits, pair_local, parts, item_cols).transpose(0, 2, 3, 1, 4)
        return value.reshape(rows, pair_local, parts * half_inner)

    normed, roots, qkvs, lses, mixes, resids, normed_twos, item_lens = [], [], [], [], [], [], [], []
    for step in range(micro):
        rows_in = tokens_pair[step].astype(jnp.float32)
        root = lax.rsqrt(jnp.mean(rows_in * rows_in, axis=-1, keepdims=True) + eps)
        roots.append(root)
        normed.append((rows_in * root * gain_first).astype(jnp.bfloat16))
    for step in range(micro):
        made = jnp.einsum("rld,de->rle", normed[step], qkv_weights, preferred_element_type=jnp.float32)
        qkvs.append(to_items(made.astype(jnp.bfloat16), 3))
    for step in range(micro):
        item_len = lax.dynamic_slice_in_dim(lengths[step], item_row, 1, 0)
        item_lens.append(item_len)
        mixed, lse = attend(qkvs[step], diag, item_len, head_dim)
        lses.append(lse)
        mixed_own = from_items([mixed])
        mixes.append(mixed_own)
        mixed_pair = jnp.concatenate([mixed_own, swap_core(mixed_own)], axis=2)
        resid = tokens_pair[step].astype(jnp.float32) + jnp.einsum(
            "rle,de->rld", mixed_pair, out_pair, preferred_element_type=jnp.float32
        )
        root = lax.rsqrt(jnp.mean(resid * resid, axis=-1, keepdims=True) + eps)
        normed_twos.append((resid * root * gain_second).astype(jnp.bfloat16))
        resids.append(own_half(resid, 1))

    pair_tokens = rows * pair_local
    flat = lambda value: value.reshape(-1, value.shape[-1])
    normed_two_all = jnp.concatenate([flat(v) for v in normed_twos])
    down_all = flat(down_in)
    pieces = [[None] * chunks for _ in range(micro)]
    chunk_totals = []
    for n in range(chunks):
        for step in range(micro):
            rowsl = slice(step * pair_tokens, (step + 1) * pair_tokens)
            pieces[step][n] = gated_chunk(flat(normed_twos[step]), down_all[rowsl], chunk_weights[n])
        joined = jnp.concatenate([pieces[step][n] for step in range(micro)])
        grad_gu = jnp.einsum("td,tf->df", normed_two_all, joined[:, : 2 * chunk], preferred_element_type=jnp.float32)
        grad_dn = jnp.einsum("td,tf->df", down_all, joined[:, 2 * chunk :], preferred_element_type=jnp.float32)
        grad_gu, grad_dn = grad_gu.astype(jnp.bfloat16), grad_dn.astype(jnp.bfloat16)

        def local_term(index, grad_gu=grad_gu, grad_dn=grad_dn):
            return jnp.concatenate(
                [lax.dynamic_slice_in_dim(g, index * shard_rows, shard_rows, 0) for g in (grad_gu, grad_dn)], axis=1
            )

        chunk_totals.append(ring.scatter(local_term, 3 * chunk))

    pieces = [[p.reshape(rows, pair_local, 3 * chunk) for p in per] for per in pieces]
    core_at = core.astype(jnp.int32)[None]
    grad_resids, grads_mixed, attn_ins = [], [], []
    gain_two_sum = jnp.zeros((width,), jnp.float32)
    for step in range(micro):
        sent = back_sum(pieces[step], chunk_weights, 1 - core_at, 2 * chunk, 0, local, jnp.bfloat16)
        got = swap_core(sent)
        kept = back_sum(pieces[step], chunk_weights, core_at, 2 * chunk, 0, local, jnp.float32)
        grad_normed = kept + got.astype(jnp.float32)
        resid = resids[step]
        root = lax.rsqrt(jnp.mean(resid * resid, axis=-1, keepdims=True) + eps)
        gain_two_sum = gain_two_sum + jnp.sum(grad_normed * resid * root, axis=(0, 1))
        scaled = grad_normed * gain_second
        shared = jnp.mean(scaled * resid, axis=-1, keepdims=True) * root * root * root
        grad_resid = cotangent[step].astype(jnp.float32) + scaled * root - resid * shared
        grad_resids.append(grad_resid)
        attn_in = grad_resid.astype(jnp.bfloat16)
        attn_ins.append(attn_in)
        made_own = jnp.einsum("rld,de->rle", attn_in, out_own, preferred_element_type=jnp.float32).astype(jnp.bfloat16)
        made_other = jnp.einsum("rld,de->rle", attn_in, out_other, preferred_element_type=jnp.float32).astype(
            jnp.bfloat16
        )
        grads_mixed.append(both_cores(made_own, swap_core(made_other), 1))

    outputs = []
    for step in range(micro):
        sent = back_sum(pieces[step], chunk_weights, 1 - core_at, chunk, 2, local, jnp.bfloat16)
        got = swap_core(sent)
        kept = back_sum(pieces[step], chunk_weights, core_at, chunk, 2, local, jnp.float32)
        outputs.append((resids[step] + kept + got.astype(jnp.float32)).astype(jnp.bfloat16))

    grads_qkv = []
    diag_sum = 0.0
    for step in range(micro):
        grad_items = to_items(grads_mixed[step], 1)
        grad_q, grad_k, grad_v, grad_diag = attend_back(
            qkvs[step], grad_items, lses[step], diag, item_lens[step], head_dim
        )
        diag_sum = diag_sum + grad_diag[:item_heads, 0]
        grads_qkv.append(from_items([grad_q, grad_k, grad_v]))
    item_grad = jnp.dot(diag_sum, bucket_hot, precision=highest)
    grad_table = lax.dynamic_update_slice(jnp.zeros((heads, levels), jnp.float32), item_grad, (head_start, 0))

    input_grads = []
    gain_one_sum = jnp.zeros((width,), jnp.float32)
    for step in range(micro):
        made = jnp.einsum("rle,de->rld", other_half(grads_qkv[step], 1), qkv_weights, preferred_element_type=jnp.float32)
        got = swap_core(made.astype(jnp.bfloat16))
        kept = jnp.einsum("rle,de->rld", own_half(grads_qkv[step], 1), qkv_weights, preferred_element_type=jnp.float32)
        grad_normed = kept + got.astype(jnp.float32)
        rows_in = tokens[step].astype(jnp.float32)
        root = own_half(roots[step], 1)
        gain_one_sum = gain_one_sum + jnp.sum(grad_normed * rows_in * root, axis=(0, 1))
        scaled = grad_normed * gain_first
        shared = jnp.mean(scaled * rows_in, axis=-1, keepdims=True) * root * root * root
        input_grads.append(grad_resids[step] + scaled * root - rows_in * shared)

    normed_all = jnp.concatenate([flat(v) for v in normed])
    grads_all = jnp.concatenate([flat(v) for v in grads_qkv])
    mixed_all = jnp.concatenate([flat(v) for v in mixes])
    attn_all = jnp.stack(attn_ins)
    attn_all = flat(both_cores(attn_all, swap_core(attn_all), 2))
    grad_attn = jnp.einsum("td,te->de", normed_all, grads_all, preferred_element_type=jnp.float32).astype(jnp.bfloat16)
    grad_o = jnp.einsum("td,te->de", attn_all, mixed_all, preferred_element_type=jnp.float32).astype(jnp.bfloat16)

    def attn_term(index):
        return jnp.concatenate(
            [lax.dynamic_slice_in_dim(g, index * shard_rows, shard_rows, 0) for g in (grad_attn, grad_o)], axis=1
        )

    attn_total = ring.scatter(attn_term, 4 * half_inner)

    def finish(total):
        if planes == 2:
            low = total.astype(jnp.bfloat16)
            got = lax.ppermute(low, "seq", [(i, i ^ 2) for i in range(4)])
            total = low.astype(jnp.float32) + got.astype(jnp.float32)
        else:
            total = lax.psum(total, "seq", axis_index_groups=plane_groups)
        return total, swap_core(total)

    def whole_columns(own, other, size):
        low, high = jnp.where(first, own, other), jnp.where(first, other, own)
        return jnp.concatenate([low, high[:, : size - low.shape[1]]], axis=1)

    own, other = finish(attn_total)
    parts = [slice(i * half_inner, (i + 1) * half_inner) for i in range(4)]
    grad_query, grad_key, grad_value, grad_out = [whole_columns(own[:, p], other[:, p], inner) for p in parts]
    done = [finish(total) for total in chunk_totals]
    parts = [slice(i * chunk, (i + 1) * chunk) for i in range(3)]
    grad_gate, grad_up, grad_down = [
        whole_columns(
            jnp.concatenate([own[:, p] for own, _ in done], axis=1),
            jnp.concatenate([other[:, p] for _, other in done], axis=1),
            hidden_units,
        )
        for p in parts
    ]

    dp_rank = lax.axis_index("dp")
    small = lax.psum(
        jnp.concatenate([gain_one_sum, gain_two_sum, grad_table.T.reshape(-1)]), ("dp", "seq")
    )
    grad_gain_one = lax.dynamic_slice_in_dim(small, dp_rank * shard_rows, shard_rows, 0)
    grad_gain_two = lax.dynamic_slice_in_dim(small, width + dp_rank * shard_rows, shard_rows, 0)
    table_part = levels // dp_devices
    grad_table = lax.dynamic_slice_in_dim(small[2 * width :].reshape(levels, heads), dp_rank * table_part, table_part, 0)

    return (
        jnp.stack(outputs), jnp.stack(input_grads), grad_gain_one, grad_gain_two, grad_table,
        grad_query, grad_key, grad_value, grad_out.T, grad_gate, grad_up, grad_down.T,
    )


def solution(mesh):
    weight, turned = P("dp", None), P(None, "dp")
    return jax.shard_map(
        body,
        mesh=mesh,
        in_specs=(
            P(None, "dp", "seq", None), P(None, "dp", "seq", None), P(None, "dp"), P(), P("dp"), P("dp"),
            weight, weight, weight, weight, turned, weight, weight, turned,
        ),
        out_specs=(
            P(None, "dp", "seq", None), P(None, "dp", "seq", None), P("dp"), P("dp"),
            weight, weight, weight, weight, turned, weight, weight, turned,
        ),
        check_vma=False,
    )
```

```python
import functools

import jax
import jax.numpy as jnp
from jax import lax
from jax.experimental import pallas as pl
from jax.experimental.pallas import tpu as pltpu
from jax.sharding import PartitionSpec as P

eps = 1e-06
masked_value = -1e30
highest = lax.Precision.HIGHEST
gelu_scale = 0.7978845608028654
gelu_cubic = 0.044715
LANES = 128
VMEM_LIMIT = 56 * 1024 * 1024
NT = (((1,), (1,)), ((), ()))
NN = (((1,), (0,)), ((), ()))
TN = (((0,), (0,)), ((), ()))


def dot32(a, b, dims):
    return lax.dot_general(a, b, dims, preferred_element_type=jnp.float32)


def toeplitz_strip(diag_row, span):
    wide = jnp.broadcast_to(diag_row, (LANES, span))
    return pltpu.roll(wide, span - (LANES - 1), 1, stride=1, stride_axis=0)


def with_mask_lane(key_pair, lanes, here, spare, length):
    rows = lax.broadcasted_iota(jnp.int32, key_pair.shape, 0)
    mask = jnp.where(rows < length, 0.0, masked_value).astype(key_pair.dtype)
    zero = jnp.zeros_like(key_pair)
    return jnp.where(here, key_pair, jnp.where(lanes == spare, mask, zero))


def attend_kernel(head_dim, block, len_ref, diag_ref, q_ref, k_ref, v_ref, mixed_ref, lse_ref, strip, keys):
    step = pl.program_id(1)
    seq_len = k_ref.shape[0]
    span = diag_ref.shape[-1]
    length = len_ref[0]
    per = LANES // head_dim
    lanes_k = lax.broadcasted_iota(jnp.int32, (seq_len, LANES), 1)
    lanes_q = lax.broadcasted_iota(jnp.int32, (block, LANES), 1)

    @pl.when(step == 0)
    def _():
        for head in range(per):
            strip[head] = toeplitz_strip(diag_ref[head], span)
            here = lanes_k // head_dim == head
            spare = ((head + 1) % per) * head_dim
            keys[head] = with_mask_lane(k_ref[...], lanes_k, here, spare, length)

    mixed = None
    for head in range(per):
        here = lanes_q // head_dim == head
        spare = ((head + 1) % per) * head_dim
        one = (lanes_q == spare).astype(q_ref.dtype)
        query = jnp.where(here, q_ref[...], one)
        raw = dot32(query, keys[head], NT)
        parts = []
        for sub in range(block // LANES):
            offset = seq_len - LANES - (step * block + sub * LANES)
            offset = pl.multiple_of(offset, LANES)
            parts.append(raw[sub * LANES : (sub + 1) * LANES] + strip[head, :, pl.ds(offset, seq_len)])
        scores = jnp.concatenate(parts, axis=0)
        top = jnp.max(scores, axis=1, keepdims=True)
        expo = jnp.exp(scores - top)
        total = jnp.sum(expo, axis=1, keepdims=True)
        made = dot32(expo.astype(jnp.bfloat16), v_ref[...], NN) / total
        mixed = made if mixed is None else jnp.where(here, made, mixed)
        lse = jnp.broadcast_to(top + jnp.log(total), (block, LANES))
        lse_ref[head] = lse.T[:1]
    mixed_ref[...] = mixed.astype(mixed_ref.dtype)


def attend(qkv, diag, length, head_dim, block=256):
    seq_len, cols = qkv.shape[0], qkv.shape[1] // 3
    pairs = cols // LANES
    per = LANES // head_dim
    span = diag.shape[-1]
    flops = 2 * 2 * seq_len * seq_len * LANES * 2 * cols // head_dim
    return pl.pallas_call(
        functools.partial(attend_kernel, head_dim, block),
        grid=(pairs, seq_len // block),
        in_specs=[
            pl.BlockSpec(memory_space=pltpu.SMEM),
            pl.BlockSpec((per, 1, span), lambda p, b: (p, 0, 0)),
            pl.BlockSpec((block, LANES), lambda p, b: (b, p)),
            pl.BlockSpec((seq_len, LANES), lambda p, b: (0, pairs + p)),
            pl.BlockSpec((seq_len, LANES), lambda p, b: (0, 2 * pairs + p)),
        ],
        out_specs=[
            pl.BlockSpec((block, LANES), lambda p, b: (b, p)),
            pl.BlockSpec((per, 1, block), lambda p, b: (p, 0, b)),
        ],
        out_shape=[
            jax.ShapeDtypeStruct((seq_len, cols), jnp.bfloat16),
            jax.ShapeDtypeStruct((cols // head_dim, 1, seq_len), jnp.float32),
        ],
        scratch_shapes=[
            pltpu.VMEM((per, LANES, span), jnp.float32),
            pltpu.VMEM((per, seq_len, LANES), jnp.bfloat16),
        ],
        compiler_params=pltpu.CompilerParams(vmem_limit_bytes=VMEM_LIMIT),
        cost_estimate=pl.CostEstimate(flops=flops, bytes_accessed=8 * seq_len * cols, transcendentals=0),
        name="attend",
    )(length, diag, qkv, qkv, qkv)


def attend_back_kernel(
    head_dim, block, len_ref, diag_ref, q_ref, k_ref, v_ref, do_ref, lse_ref,
    dq_ref, dk_ref, dv_ref, dd_ref, strip, keys, acc_bias, acc_k, acc_v,
):
    step = pl.program_id(1)
    steps = pl.num_programs(1)
    seq_len = k_ref.shape[0]
    span = diag_ref.shape[-1]
    length = len_ref[0]
    per = LANES // head_dim
    lanes_k = lax.broadcasted_iota(jnp.int32, (seq_len, LANES), 1)
    lanes_q = lax.broadcasted_iota(jnp.int32, (block, LANES), 1)
    subs = block // LANES

    @pl.when(step == 0)
    def _():
        for head in range(per):
            strip[head] = toeplitz_strip(diag_ref[head], span).T
            here = lanes_k // head_dim == head
            spare = ((head + 1) % per) * head_dim
            keys[head] = with_mask_lane(k_ref[...], lanes_k, here, spare, length)
        acc_bias[...] = jnp.zeros_like(acc_bias)
        acc_k[...] = jnp.zeros_like(acc_k)
        acc_v[...] = jnp.zeros_like(acc_v)

    grad_query = None
    for head in range(per):
        here = lanes_q // head_dim == head
        spare = ((head + 1) % per) * head_dim
        zero = jnp.zeros_like(q_ref[...])
        one = (lanes_q == spare).astype(q_ref.dtype)
        query = jnp.where(here, q_ref[...], zero)
        grad = jnp.where(here, do_ref[...], zero)
        raw = dot32(keys[head], query + one, NT)
        grad_probs = dot32(v_ref[...], grad, NT)
        parts = []
        offsets = []
        for sub in range(subs):
            offset = seq_len - LANES - (step * block + sub * LANES)
            offset = pl.multiple_of(offset, LANES)
            offsets.append(offset)
            parts.append(raw[:, sub * LANES : (sub + 1) * LANES] + strip[head, pl.ds(offset, seq_len), :])
        scores = jnp.concatenate(parts, axis=1)
        probs = jnp.exp(scores - lse_ref[head])
        product = probs * grad_probs
        inner = jnp.sum(product, axis=0, keepdims=True)
        grad_scores = product - probs * inner
        for sub in range(subs):
            rows = pl.ds(offsets[sub], seq_len)
            acc_bias[head, rows, :] += grad_scores[:, sub * LANES : (sub + 1) * LANES]
        rounded = grad_scores.astype(jnp.bfloat16)
        acc_v[...] += dot32(probs.astype(jnp.bfloat16), grad, NN)
        acc_k[...] += dot32(rounded, query, NN)
        made = dot32(rounded, k_ref[...], TN)
        grad_query = made if grad_query is None else jnp.where(here, made, grad_query)
    dq_ref[...] = grad_query.astype(dq_ref.dtype)

    @pl.when(step == steps - 1)
    def _():
        dk_ref[...] = acc_k[...].astype(dk_ref.dtype)
        dv_ref[...] = acc_v[...].astype(dv_ref.dtype)
        row = lax.broadcasted_iota(jnp.int32, (LANES, LANES), 0)
        col = lax.broadcasted_iota(jnp.int32, (LANES, LANES), 1)
        flip = (row + col == LANES - 1).astype(jnp.float32)
        for head in range(per):
            turned = lax.dot_general(
                flip, acc_bias[head], NT, precision=lax.Precision.HIGHEST, preferred_element_type=jnp.float32
            )
            aligned = pltpu.roll(turned, 0, 1, stride=1, stride_axis=0)
            dd_ref[head] = jnp.sum(aligned, axis=0, keepdims=True)


def attend_back(qkv, grad_mixed, lse, diag, length, head_dim, block=256):
    seq_len, cols = qkv.shape[0], qkv.shape[1] // 3
    pairs = cols // LANES
    per = LANES // head_dim
    span = diag.shape[-1]
    flops = 5 * 2 * seq_len * seq_len * LANES * 2 * cols // head_dim
    whole = lambda p, b: (0, p)
    part = lambda p, b: (b, p)
    flat = jax.ShapeDtypeStruct((seq_len, cols), jnp.bfloat16)
    return pl.pallas_call(
        functools.partial(attend_back_kernel, head_dim, block),
        grid=(pairs, seq_len // block),
        in_specs=[
            pl.BlockSpec(memory_space=pltpu.SMEM),
            pl.BlockSpec((per, 1, span), lambda p, b: (p, 0, 0)),
            pl.BlockSpec((block, LANES), part),
            pl.BlockSpec((seq_len, LANES), lambda p, b: (0, pairs + p)),
            pl.BlockSpec((seq_len, LANES), lambda p, b: (0, 2 * pairs + p)),
            pl.BlockSpec((block, LANES), part),
            pl.BlockSpec((per, 1, block), lambda p, b: (p, 0, b)),
        ],
        out_specs=[
            pl.BlockSpec((block, LANES), part),
            pl.BlockSpec((seq_len, LANES), whole),
            pl.BlockSpec((seq_len, LANES), whole),
            pl.BlockSpec((per, 1, span), lambda p, b: (p, 0, 0)),
        ],
        out_shape=[flat, flat, flat, jax.ShapeDtypeStruct(diag.shape, jnp.float32)],
        scratch_shapes=[
            pltpu.VMEM((per, span, LANES), jnp.float32),
            pltpu.VMEM((per, seq_len, LANES), jnp.bfloat16),
            pltpu.VMEM((per, span, LANES), jnp.float32),
            pltpu.VMEM((seq_len, LANES), jnp.float32),
            pltpu.VMEM((seq_len, LANES), jnp.float32),
        ],
        compiler_params=pltpu.CompilerParams(vmem_limit_bytes=VMEM_LIMIT),
        cost_estimate=pl.CostEstimate(flops=flops, bytes_accessed=16 * seq_len * cols, transcendentals=0),
        name="attend_back",
    )(length, diag, qkv, qkv, qkv, grad_mixed, lse)


def gated_values(gate, up, grad):
    square = gate * gate
    turn = jnp.tanh(gelu_scale * gate * (1.0 + gelu_cubic * square))
    half = 0.5 * (1.0 + turn)
    act = gate * half
    slope = half + 0.5 * gate * (1.0 - turn * turn) * gelu_scale * (1.0 + 3.0 * gelu_cubic * square)
    low = jnp.bfloat16
    return (grad * up * slope).astype(low), (grad * act).astype(low), (act * up).astype(low)


def ring_order(count):
    if count % 4 or count < 8:
        return list(range(count))
    long, short = 4, count // 4
    walk = []
    for line in range(long):
        columns = range(1, short) if line % 2 == 0 else range(short - 1, 0, -1)
        walk += [line * short + column for column in columns]
    return walk + [line * short for line in range(long - 1, -1, -1)]


MESH = pl.DeviceIdType.MESH


def pick(options, at):
    value = jnp.int32(options[0])
    for index in range(1, len(options)):
        value = jnp.where(at == index, jnp.int32(options[index]), value)
    return value


class Links:
    def __init__(self, count, planes):
        order = ring_order(count)
        place = [0] * count
        for at, index in enumerate(order):
            place[index] = at
        self.count, self.order, self.planes = count, order, planes
        self.place = pick(place, lax.axis_index("dp"))
        seq = lax.axis_index("seq")
        self.core = seq % 2
        self.plane = seq // 2
        self.sibling = {"seq": self.plane * 2 + 1 - self.core}
        self.across = {"seq": (1 - self.plane) * 2 + self.core}
        self.ahead = {"dp": self.owner(1)}
        self.behind = {"dp": self.owner(-1)}

    def owner(self, shift):
        return pick(self.order, lax.rem(self.place + shift + self.count, self.count))

    def greet(self):
        barrier = pltpu.get_barrier_semaphore()
        friends = [self.ahead, self.behind, self.sibling] + ([self.across] if self.planes == 2 else [])
        for friend in friends:
            pl.semaphore_signal(barrier, inc=1, device_id=friend, device_id_type=MESH)
        pl.semaphore_wait(barrier, len(friends))


class Gather:
    def __init__(self, links, shard, whole, sems, rows):
        self.links, self.shard, self.whole, self.sems, self.rows = links, shard, whole, sems, rows
        self.far = links.count // 2
        self.shared = links.planes == 2
        self.third = rows // 3
        self.size = 2 * self.third if self.shared else rows
        self.cut = -(-(self.size // 2) // 16) * 16

    def base(self, shift):
        start = self.links.owner(shift) * self.rows
        if self.shared:
            start = start + self.links.plane * self.third
        return pl.multiple_of(start, 16)

    def ring_copy(self, step, forward):
        shift = (1 - step) if forward else (step - 1)
        offset, size = 0, self.size
        if step == self.far:
            offset, size = (0, self.cut) if forward else (self.cut, self.size - self.cut)
        place = self.whole.at[pl.ds(pl.multiple_of(self.base(shift) + offset, 16), size)]
        source = place
        if step == 1:
            first = self.links.plane * self.third if self.shared else 0
            source = self.shard.at[pl.ds(pl.multiple_of(first + offset, 16), size)]
        return pltpu.make_async_remote_copy(
            src_ref=source,
            dst_ref=place,
            send_sem=self.sems.at[0 if forward else 1, step],
            recv_sem=self.sems.at[2 if forward else 3, step],
            device_id=self.links.ahead if forward else self.links.behind,
            device_id_type=MESH,
        )

    def recv_copy(self, step, forward):
        shift = -step if forward else step
        offset, size = 0, self.size
        if step == self.far:
            offset, size = (0, self.cut) if forward else (self.cut, self.size - self.cut)
        place = self.whole.at[pl.ds(pl.multiple_of(self.base(shift) + offset, 16), size)]
        return pltpu.make_async_remote_copy(
            src_ref=place,
            dst_ref=place,
            send_sem=self.sems.at[0 if forward else 1, step],
            recv_sem=self.sems.at[2 if forward else 3, step],
            device_id=self.links.ahead if forward else self.links.behind,
            device_id_type=MESH,
        )

    def across_copy(self, slot, shift, receive):
        plane = 1 - self.links.plane if receive else self.links.plane
        start = self.links.owner(shift) * self.rows + plane * 2 * self.third
        place = self.whole.at[pl.ds(pl.multiple_of(start, 16), self.third)]
        return pltpu.make_async_remote_copy(
            src_ref=place,
            dst_ref=place,
            send_sem=self.sems.at[4, slot],
            recv_sem=self.sems.at[5, slot],
            device_id=self.links.across,
            device_id_type=MESH,
        )

    def start(self):
        self.ring_copy(1, True).start()
        self.ring_copy(1, False).start()

    def advance(self, step):
        last = step == self.far
        for forward in (True, False):
            self.recv_copy(step, forward).wait_recv()
            if not last:
                self.ring_copy(step + 1, forward).start()
            if self.shared and not last:
                slot = 2 * step - 2 + (0 if forward else 1)
                self.across_copy(slot, -step if forward else step, False).start()
        if self.shared and last:
            self.across_copy(2 * step - 2, step, False).start()

    def slots(self):
        shifts = []
        for step in range(1, self.far):
            shifts += [(2 * step - 2, -step), (2 * step - 1, step)]
        return shifts + [(2 * self.far - 2, self.far)]

    def finish(self):
        for step in range(1, self.far + 1):
            self.ring_copy(step, True).wait_send()
            self.ring_copy(step, False).wait_send()
        if self.shared:
            for slot, shift in self.slots():
                self.across_copy(slot, shift, False).wait_send()
                self.across_copy(slot, shift, True).wait_recv()


def gather_kernel(count, planes, rows, shard, small, tokens, cotangent, whole, smalls, tokens_there, cotangent_there, sems, sems_small, sems_core, own):
    links = Links(count, planes)
    keep = pltpu.make_async_copy(shard, whole.at[pl.ds(pl.multiple_of(links.owner(0) * rows, 16), rows)], own.at[0])
    keep_small = pltpu.make_async_copy(small, smalls.at[pl.ds(pl.multiple_of(links.owner(0) * 16, 16), 16)], own.at[1])
    keep.start()
    keep_small.start()
    links.greet()
    large = Gather(links, shard, whole, sems, rows)
    little = SmallGather(links, small, smalls, sems_small)
    little.start()
    large.start()
    swaps = []
    for at, (source, target) in enumerate(((tokens, tokens_there), (cotangent, cotangent_there))):
        swaps.append(
            pltpu.make_async_remote_copy(
                src_ref=source, dst_ref=target, send_sem=sems_core.at[at, 0], recv_sem=sems_core.at[at, 1],
                device_id=links.sibling, device_id_type=MESH,
            )
        )
        swaps[-1].start()
    for step in range(1, large.far + 1):
        little.advance(step)
        large.advance(step)
    for swap in swaps:
        swap.wait()
    little.finish()
    large.finish()
    keep.wait()
    keep_small.wait()


class SmallGather(Gather):
    def __init__(self, links, shard, whole, sems):
        self.links, self.shard, self.whole, self.sems, self.rows = links, shard, whole, sems, 16
        self.far, self.shared, self.size, self.cut = links.count // 2, False, 16, 16

    def start(self):
        self.ring_copy(1, True).start()
        self.ring_copy(1, False).start()

    def advance(self, step):
        self.recv_copy(step, True).wait_recv()
        if step < self.far:
            self.ring_copy(step + 1, True).start()
            self.recv_copy(step, False).wait_recv()
            if step + 1 < self.far:
                self.ring_copy(step + 1, False).start()

    def finish(self):
        for step in range(1, self.far + 1):
            self.ring_copy(step, True).wait_send()
            if step < self.far:
                self.ring_copy(step, False).wait_send()


def gather_first(shard, small, tokens, cotangent, count, planes):
    rows, cols = shard.shape
    anywhere = pl.BlockSpec(memory_space=pl.ANY)
    return pl.pallas_call(
        functools.partial(gather_kernel, count, planes, rows),
        in_specs=[anywhere] * 4,
        out_specs=[anywhere] * 4,
        out_shape=[
            jax.ShapeDtypeStruct((count * rows, cols), shard.dtype),
            jax.ShapeDtypeStruct((count * 16, small.shape[1]), small.dtype),
            jax.ShapeDtypeStruct(tokens.shape, tokens.dtype),
            jax.ShapeDtypeStruct(cotangent.shape, cotangent.dtype),
        ],
        scratch_shapes=[
            pltpu.SemaphoreType.DMA((6, count)),
            pltpu.SemaphoreType.DMA((4, count)),
            pltpu.SemaphoreType.DMA((2, 2)),
            pltpu.SemaphoreType.DMA((2,)),
        ],
        compiler_params=pltpu.CompilerParams(collective_id=0, has_side_effects=True),
        name="gather_first",
    )(shard, small, tokens, cotangent)


class Scatter:
    def __init__(self, links, grads, inbox, totals, mine, came, made, total, send_sems, recv_sems, near_sems, total_sems, rows):
        self.links, self.grads, self.inbox, self.totals = links, grads, inbox, totals
        self.mine, self.came, self.made, self.total = mine, came, made, total
        self.send_sems, self.recv_sems, self.near_sems, self.total_sems = send_sems, recv_sems, near_sems, total_sems
        self.rows = rows
        self.far = links.count // 2
        self.cut = -(-(rows // 2) // 16) * 16
        self.spaces = made.shape[0]

    def part(self, step, way):
        if step > 1:
            return 0, self.rows
        return (0, self.cut) if way == 0 else (self.cut, self.rows - self.cut)

    def term(self, chunk, shift, offset, size):
        start = self.links.owner(shift) * self.rows + offset
        return self.grads.at[chunk, pl.ds(pl.multiple_of(start, 16), size)]

    def hop(self, chunk, step, way):
        offset, size = self.part(step, way)
        if step == 1:
            source = self.term(chunk, self.far, offset, size)
        else:
            source = self.made.at[lax.rem(chunk, self.spaces), way, pl.ds(offset, size)]
        return pltpu.make_async_remote_copy(
            src_ref=source,
            dst_ref=self.inbox.at[chunk, way, step - 1, pl.ds(offset, size)],
            send_sem=self.send_sems.at[chunk, way, step - 1],
            recv_sem=self.recv_sems.at[chunk, way, step - 1],
            device_id=self.links.behind if way else self.links.ahead,
            device_id_type=MESH,
        )

    def near(self, chunk, step, way):
        offset, size = self.part(step, way)
        space = lax.rem(chunk, self.spaces)
        shift = (step - self.far) if way else (self.far - step)
        copies = [
            pltpu.make_async_copy(
                self.inbox.at[chunk, way, step - 1, pl.ds(offset, size)],
                self.came.at[space, way, pl.ds(offset, size)],
                self.near_sems.at[space, way, 0],
            )
        ]
        if step < self.far or way == 0:
            copies.append(
                pltpu.make_async_copy(
                    self.term(chunk, shift, 0, self.rows), self.mine.at[space, way], self.near_sems.at[space, way, 1]
                )
            )
        return copies

    def start(self, chunk):
        for way in range(2):
            self.hop(chunk, 1, way).start()

    def fetch(self, chunk, step):
        for way in range(2):
            self.hop(chunk, step, way).wait_recv()
            for copy in self.near(chunk, step, way):
                copy.start()

    def pass_on(self, chunk, step):
        space = lax.rem(chunk, self.spaces)
        for way in range(2):
            for copy in self.near(chunk, step, way):
                copy.wait()
            self.hop(chunk, step, way).wait_send()
            offset, size = self.part(step, way)
            rows = pl.ds(offset, size)
            if size < self.rows:
                other = pl.ds(0 if way else size, self.rows - size)
                self.made[space, way, other] = self.mine[space, way, other]
            self.made[space, way, rows] = add_low(self.mine[space, way, rows], self.came[space, way, rows])
            self.hop(chunk, step + 1, way).start()

    def total_copy(self, chunk):
        return pltpu.make_async_copy(self.total, self.totals.at[chunk], self.total_sems.at[0])

    def close(self, chunk):
        space = lax.rem(chunk, self.spaces)
        for way in range(2):
            for copy in self.near(chunk, self.far, way):
                copy.wait()
            self.hop(chunk, self.far, way).wait_send()

        @pl.when(chunk > 0)
        def _():
            self.total_copy(chunk - 1).wait()

        total = self.mine[space, 0].astype(jnp.float32) + self.came[space, 0].astype(jnp.float32)
        self.total[...] = total + self.came[space, 1].astype(jnp.float32)
        self.total_copy(chunk).start()


def feed_kernel(plan, *refs):
    count, planes, rows, chunks, early, tile, block, groups = plan
    late = chunks - early
    (normed, down, *rest) = refs
    ready, shards = rest[:early], rest[early:chunks]
    rest = rest[chunks:]
    back_kept, back_got, out_kept, out_got, totals, pieces, grads, inbox = rest[:8]
    wholes = rest[8 : 8 + late]
    (
        a_all, b_all, weights, piece, stage, mine, came, made, total, out_stage,
        in_sems, piece_sems, stage_sems, fetch_sems, keep_sems, give_sems, take_sems,
        send_sems, recv_sems, near_sems, total_sems, own_sems, *gather_sems,
    ) = rest[8 + late :]
    tokens, depth = a_all.shape
    width = weights.shape[2] // 3
    tiles, blocks = tokens // tile, depth // block
    per = tiles + blocks
    front = chunks * per
    links = Links(count, planes)
    far = count // 2

    loads = [pltpu.make_async_copy(normed, a_all, in_sems.at[chunks]), pltpu.make_async_copy(down, b_all, in_sems.at[chunks + 1])]
    loads += [pltpu.make_async_copy(ready[n], weights.at[n], in_sems.at[n]) for n in range(early)]
    keeps = []
    for n in range(late):
        place = wholes[n].at[pl.ds(pl.multiple_of(links.owner(0) * rows, 16), rows)]
        keeps.append(pltpu.make_async_copy(shards[n], place, own_sems.at[n]))
    for copy in loads + keeps:
        copy.start()
    links.greet()
    gathers = [Gather(links, shards[n], wholes[n], gather_sems[n], rows) for n in range(late)]
    scatter = Scatter(
        links, grads, inbox, totals, mine, came, made, total, send_sems, recv_sems, near_sems, total_sems, rows
    )
    loads[0].wait()
    loads[1].wait()

    gap_gather = max(1, 16 // far)
    gap = max(2, 20 // far)

    def load_weights(n):
        source = ready[n] if n < early else wholes[n - early]
        return pltpu.make_async_copy(source, weights.at[n], in_sems.at[n])

    def piece_copy(n, t):
        place = pl.ds(pl.multiple_of(t * tile, 16), tile)
        return pltpu.make_async_copy(piece.at[place], pieces.at[n, place], piece_sems.at[t])

    def stage_copy(n, b):
        slot = lax.rem(b, 2)
        place = pl.ds(pl.multiple_of(b * block, 16), block)
        return pltpu.make_async_copy(stage.at[slot], grads.at[n, place], stage_sems.at[slot])

    def back_rows(g, half):
        start = (2 * g + half) * tile
        return pl.ds(pl.multiple_of(start, 16), tile)

    def fetch_copy(n, t):
        half = jnp.where(lax.rem(t, 2) == 0, 1 - links.core, links.core)
        slot = lax.rem(t, 2)
        target = pl.ds(pl.multiple_of((slot * chunks + n) * tile, 16), tile)
        return pltpu.make_async_copy(pieces.at[n, back_rows(t // 2, half)], piece.at[target], fetch_sems.at[slot, n])

    def give_copy(kind, g):
        target = (back_got, out_got)[kind]
        return pltpu.make_async_remote_copy(
            src_ref=out_stage.at[kind, 0], dst_ref=target.at[g], send_sem=give_sems.at[kind], recv_sem=take_sems.at[kind, g],
            device_id=links.sibling, device_id_type=MESH,
        )

    def keep_copy(kind, g):
        target = (back_kept, out_kept)[kind]
        return pltpu.make_async_copy(out_stage.at[kind, 1], target.at[g], keep_sems.at[kind])

    items_back = 4 * groups
    last_event = front + 1 + gap * far
    total_items = max(front + items_back, last_event + 1)

    def item(i, carry):
        n, j = i // per, lax.rem(i, per)

        for k in range(late):
            base = k * per
            for step in range(far + 2):

                @pl.when(i == base + step * gap_gather)
                def _(k=k, step=step):
                    if step == 0:
                        gathers[k].start()
                    elif step <= far:
                        gathers[k].advance(step)
                    else:
                        gathers[k].finish()
                        keeps[k].wait()
                        load_weights(early + k).start()

        def event(offset, act):
            past = i - per - offset

            @pl.when((past >= 0) & (past < front) & (lax.rem(past + per * 64, per) == 0))
            def _():
                act(past // per)

        def begin(chunk):
            for b in (blocks - 2, blocks - 1):
                stage_copy(chunk, b).wait()
            scatter.start(chunk)

        event(0, begin)
        for step in range(1, far + 1):
            event(step * gap - 1, lambda chunk, step=step: scatter.fetch(chunk, step))
            if step < far:
                event(step * gap, lambda chunk, step=step: scatter.pass_on(chunk, step))
            else:
                event(step * gap, scatter.close)

        @pl.when((i < front) & (j == 0))
        def _():
            for m in range(chunks):

                @pl.when(n == m)
                def _(m=m):
                    load_weights(m).wait()

        @pl.when((i < front) & (j < tiles))
        def _():
            @pl.when(n > 0)
            def _():
                piece_copy(n - 1, j).wait()

            place = pl.ds(pl.multiple_of(j * tile, 16), tile)
            a, d = a_all[place], b_all[place]
            gate = dot32(a, weights[n, :, :width], NN)
            up = dot32(a, weights[n, :, width : 2 * width], NN)
            grad = dot32(d, weights[n, :, 2 * width :], NN)
            d_gate, d_up, hidden = gated_values(gate, up, grad)
            piece[place, :width] = d_gate
            piece[place, width : 2 * width] = d_up
            piece[place, 2 * width :] = hidden
            piece_copy(n, j).start()

        @pl.when((i < front) & (j >= tiles))
        def _():
            b = j - tiles

            @pl.when(b >= 2)
            def _():
                stage_copy(n, b - 2).wait()

            place = pl.ds(pl.multiple_of(b * block, LANES), block)
            slot = lax.rem(b, 2)
            first = dot32(a_all[:, place], piece[:, : 2 * width], TN)
            stage[slot, :, : 2 * width] = first.astype(stage.dtype)
            second = dot32(b_all[:, place], piece[:, 2 * width :], TN)
            stage[slot, :, 2 * width :] = second.astype(stage.dtype)
            stage_copy(n, b).start()

        @pl.when(i == front)
        def _():
            for t in range(tiles):
                piece_copy(chunks - 1, t).wait()
            for m in range(chunks):
                fetch_copy(m, 0).start()

        at = i - front
        t, kind_at = at // 2, lax.rem(at + 2 * per, 2)
        for kind in range(2):

            @pl.when((at >= 0) & (at < items_back) & (kind_at == kind))
            def _(kind=kind):
                slot, g = lax.rem(t, 2), t // 2
                if kind == 0:
                    for m in range(chunks):
                        fetch_copy(m, t).wait()

                    @pl.when(t + 1 < 2 * groups)
                    def _():
                        for m in range(chunks):
                            fetch_copy(m, t + 1).start()

                columns = slice(0, 2 * width) if kind == 0 else slice(2 * width, 3 * width)
                made_sum = None
                for m in range(chunks):
                    place = pl.ds(pl.multiple_of((slot * chunks + m) * tile, 16), tile)
                    term = dot32(piece[place, columns], weights[m, :, columns], NT)
                    made_sum = term if made_sum is None else made_sum + term

                @pl.when((t >= 2) & (slot == 0))
                def _():
                    give_copy(kind, g - 1).wait_send()

                @pl.when((t >= 2) & (slot == 1))
                def _():
                    keep_copy(kind, g - 1).wait()

                out_stage[kind, slot] = made_sum.astype(out_stage.dtype)

                @pl.when(slot == 0)
                def _():
                    give_copy(kind, g).start()

                @pl.when(slot == 1)
                def _():
                    keep_copy(kind, g).start()

        return carry

    lax.fori_loop(0, total_items, item, 0)
    scatter.total_copy(chunks - 1).wait()
    for kind in range(2):
        give_copy(kind, groups - 1).wait_send()
        keep_copy(kind, groups - 1).wait()
        for g in range(groups):
            give_copy(kind, g).wait_recv()


def feed(normed, down, ready, shards, count, planes, tile):
    tokens, depth = normed.shape
    rows, cols = shards[0].shape
    early, chunks = len(ready), len(ready) + len(shards)
    far = count // 2
    block = 384
    groups = tokens // (2 * tile)
    spaces = 2 if far <= 4 else chunks
    plan = (count, planes, rows, chunks, early, tile, block, groups)
    anywhere = pl.BlockSpec(memory_space=pl.ANY)
    low, wide = jnp.bfloat16, jnp.float32
    part = jax.ShapeDtypeStruct((groups, tile, depth), low)
    shapes = [part] * 4 + [
        jax.ShapeDtypeStruct((chunks, rows, cols), wide),
        jax.ShapeDtypeStruct((chunks, tokens, cols), low),
        jax.ShapeDtypeStruct((chunks, depth, cols), low),
        jax.ShapeDtypeStruct((chunks, 2, far, rows, cols), low),
    ]
    shapes += [jax.ShapeDtypeStruct((depth, cols), low)] * len(shards)
    dma = pltpu.SemaphoreType.DMA
    made = pl.pallas_call(
        functools.partial(feed_kernel, plan),
        in_specs=[anywhere] * (2 + chunks),
        out_specs=[anywhere] * len(shapes),
        out_shape=shapes,
        scratch_shapes=[
            pltpu.VMEM((tokens, depth), low),
            pltpu.VMEM((tokens, depth), low),
            pltpu.VMEM((chunks, depth, cols), low),
            pltpu.VMEM((tokens, cols), low),
            pltpu.VMEM((2, block, cols), low),
            pltpu.VMEM((spaces, 2, rows, cols), low),
            pltpu.VMEM((spaces, 2, rows, cols), low),
            pltpu.VMEM((spaces, 2, rows, cols), low),
            pltpu.VMEM((rows, cols), wide),
            pltpu.VMEM((2, 2, tile, depth), low),
            dma((chunks + 2,)),
            dma((tokens // tile,)),
            dma((2,)),
            dma((2, chunks)),
            dma((2,)),
            dma((2,)),
            dma((2, groups)),
            dma((chunks, 2, far)),
            dma((chunks, 2, far)),
            dma((spaces, 2, 2)),
            dma((1,)),
            dma((len(shards),)),
        ]
        + [dma((6, count))] * len(shards),
        compiler_params=pltpu.CompilerParams(
            collective_id=1, has_side_effects=True, vmem_limit_bytes=62 * 1024 * 1024
        ),
        cost_estimate=pl.CostEstimate(
            flops=18 * tokens * depth * cols // 3 * chunks, bytes_accessed=10 * tokens * depth, transcendentals=0
        ),
        name="feed",
    )(normed, down, *ready, *shards)
    return made[:5]


class Ring:
    def __init__(self, count):
        order = ring_order(count)
        place = [0] * count
        for at, index in enumerate(order):
            place[index] = at
        self.count = count
        self.order = jnp.array(order, jnp.int32)
        self.here = jnp.array(place, jnp.int32)[lax.axis_index("dp")]
        self.ahead = [(order[i], order[(i + 1) % count]) for i in range(count)]
        self.behind = [(order[i], order[(i - 1) % count]) for i in range(count)]

    def owner(self, shift):
        return self.order[(self.here + shift) % self.count]

    def send(self, block, forward):
        return lax.ppermute(block, "dp", self.ahead if forward else self.behind)

    def gather(self, shard):
        rows, cols = shard.shape
        cut = cols // 2
        far = self.count // 2
        whole = jnp.zeros((self.count * rows, cols), shard.dtype)

        def put(whole, block, shift, column=0):
            return lax.dynamic_update_slice(whole, block, (self.owner(shift) * rows, column))

        whole = put(whole, shard, 0)
        ahead = behind = shard
        for step in range(1, far):
            ahead, behind = self.send(ahead, True), self.send(behind, False)
            whole = put(put(whole, ahead, -step), behind, step)
        last = (ahead, behind)
        ahead, behind = self.send(ahead[:, :cut], True), self.send(behind[:, cut:], False)
        whole = put(put(whole, ahead, -far), behind, far, cut)
        return whole, last

    def scatter(self, local, cols):
        cut = cols // 2
        far = self.count // 2
        most = local(self.owner(far))
        ahead, behind = self.send(most[:, :cut], True), self.send(most[:, cut:], False)
        for step in range(far - 1, 0, -1):
            mine = local(self.owner(step))
            other = local(self.owner(-step))
            if step == far - 1:
                ahead = jnp.concatenate([add_low(mine[:, :cut], ahead), mine[:, cut:]], axis=1)
                behind = jnp.concatenate([other[:, :cut], add_low(other[:, cut:], behind)], axis=1)
            else:
                ahead, behind = add_low(mine, ahead), add_low(other, behind)
            ahead, behind = self.send(ahead, True), self.send(behind, False)
        return local(self.owner(0)).astype(jnp.float32) + ahead.astype(jnp.float32) + behind.astype(jnp.float32)


def add_low(a, b):
    return (a.astype(jnp.float32) + b.astype(jnp.float32)).astype(jnp.bfloat16)


def body(
    tokens, cotangent, lengths, buckets, gain_one, gain_two, table,
    w_query, w_key, w_value, w_out, w_gate, w_up, w_down,
):
    micro, rows, local, width = tokens.shape
    seq_devices = lax.axis_size("seq")
    dp_devices = lax.axis_size("dp")
    seq_rank = lax.axis_index("seq")
    core = seq_rank % 2
    plane = seq_rank // 2
    planes = seq_devices // 2
    heads = table.shape[1]
    shard_rows, inner = w_query.shape
    head_dim = inner // heads
    half_inner = inner // 2
    hidden_units = w_gate.shape[1]
    pair_local = 2 * local
    seq_len = local * seq_devices
    first = core == 0
    core_pairs = [(i, i ^ 1) for i in range(seq_devices)]
    plane_groups = [[2 * p + c for p in range(planes)] for c in range(2)]
    ring = Ring(dp_devices)

    def swap_core(value):
        return lax.ppermute(value, "seq", core_pairs)

    def both_cores(own, other, axis):
        return jnp.concatenate([jnp.where(first, own, other), jnp.where(first, other, own)], axis=axis)

    def own_half(value, axis):
        return lax.dynamic_slice_in_dim(value, core * local, local, axis)

    def other_half(value, axis):
        return lax.dynamic_slice_in_dim(value, (1 - core) * local, local, axis)

    def core_columns(weight, split):
        low, high = weight[:, :split], weight[:, split:]
        high = jnp.pad(high, ((0, 0), (0, split - high.shape[1])))
        return jnp.where(first, low, high)

    chunk = 512
    chunks = -(-(hidden_units // 2) // chunk)
    split = chunks * chunk
    if split > hidden_units:
        split = hidden_units
    attn_shard = jnp.concatenate(
        [core_columns(w, half_inner) for w in (w_query, w_key, w_value, w_out.T)], axis=1
    )
    up_parts = [core_columns(w, split) for w in (w_gate, w_up, w_down.T)]
    chunk_shards = [
        jnp.concatenate([w[:, n * chunk : (n + 1) * chunk] for w in up_parts], axis=1) for n in range(chunks)
    ]

    small = jnp.concatenate([gain_one, gain_two, table.reshape(-1)])
    small = jnp.pad(small, (0, -small.shape[0] % LANES))
    small = jnp.pad(small[None], ((0, 15), (0, 0)))
    attn_weights, small, tokens_other, cotangent_other = gather_first(
        attn_shard, small, tokens, cotangent, dp_devices, planes
    )
    small = small.reshape(dp_devices, 16, -1)[:, 0].astype(jnp.float32)
    gain_first = small[:, :shard_rows].reshape(-1)
    gain_second = small[:, shard_rows : 2 * shard_rows].reshape(-1)
    full_table = small[:, 2 * shard_rows : 2 * shard_rows + table.size].reshape(-1, heads)
    last = attn_weights
    qkv_weights = attn_weights[:, : 3 * half_inner]
    out_own = attn_weights[:, 3 * half_inner :]
    out_other = swap_core(out_own)
    out_pair = jnp.concatenate([out_own, out_other], axis=1)

    early = min(2, chunks - 1)
    ready = []
    for shard in chunk_shards[:early]:
        shard, last = lax.optimization_barrier((shard, last))
        ready.append(lax.all_gather(shard, "dp", axis=0, tiled=True))

    tokens_pair = both_cores(tokens, tokens_other, 2)
    down_in = both_cores(cotangent, cotangent_other, 2)

    core_heads = heads // 2
    head_splits = planes // rows
    item_heads = core_heads // head_splits
    item_cols = item_heads * head_dim
    padded_cols = -(-item_cols // LANES) * LANES
    padded_heads = padded_cols // head_dim
    item_row = plane // head_splits
    item_group = plane % head_splits
    head_start = core * core_heads + item_group * item_heads
    item_table = lax.dynamic_slice_in_dim(full_table, head_start, item_heads, 1)
    item_table = jnp.pad(item_table, ((0, 0), (0, padded_heads - item_heads)))
    levels = full_table.shape[0]
    bucket_hot = (buckets[:, None] == jnp.arange(levels)[None, :]).astype(jnp.float32)
    bucket_hot = jnp.pad(bucket_hot, ((0, 1), (0, 0)))
    diag = jnp.dot(item_table.T, bucket_hot.T, precision=highest)[:, None, :]

    def to_items(value, parts):
        if planes == 2 and rows == 2:
            mine = lax.dynamic_index_in_dim(value, plane, 0, keepdims=False)
            sent = lax.dynamic_index_in_dim(value, 1 - plane, 0, keepdims=False)
            got = lax.ppermute(sent, "seq", [(i, i ^ 2) for i in range(4)])
            low = plane == 0
            return jnp.concatenate([jnp.where(low, mine, got), jnp.where(low, got, mine)], axis=0)
        value = value.reshape(rows, pair_local, parts, head_splits, item_cols)
        value = value.transpose(0, 3, 1, 2, 4).reshape(planes, pair_local, parts * item_cols)
        value = lax.all_to_all(value, "seq", 0, 0, tiled=True, axis_index_groups=plane_groups)
        value = value.reshape(seq_len, parts, item_cols)
        value = jnp.pad(value, ((0, 0), (0, 0), (0, padded_cols - item_cols)))
        return value.reshape(seq_len, parts * padded_cols)

    def from_items(values):
        parts = len(values)
        if planes == 2 and rows == 2:
            value = jnp.concatenate(values, axis=1)
            mine = lax.dynamic_slice_in_dim(value, plane * pair_local, pair_local, 0)
            sent = lax.dynamic_slice_in_dim(value, (1 - plane) * pair_local, pair_local, 0)
            got = lax.ppermute(sent, "seq", [(i, i ^ 2) for i in range(4)])
            low = plane == 0
            return jnp.stack([jnp.where(low, mine, got), jnp.where(low, got, mine)])
        value = jnp.concatenate([v[:, :item_cols] for v in values], axis=1)
        value = value.reshape(planes, pair_local, parts * item_cols)
        value = lax.all_to_all(value, "seq", 0, 0, tiled=True, axis_index_groups=plane_groups)
        value = value.reshape(rows, head_splits, pair_local, parts, item_cols).transpose(0, 2, 3, 1, 4)
        return value.reshape(rows, pair_local, parts * half_inner)

    normed, roots, qkvs, lses, mixes, resids, normed_twos, item_lens = [], [], [], [], [], [], [], []
    for step in range(micro):
        rows_in = tokens_pair[step].astype(jnp.float32)
        root = lax.rsqrt(jnp.mean(rows_in * rows_in, axis=-1, keepdims=True) + eps)
        roots.append(root)
        normed.append((rows_in * root * gain_first).astype(jnp.bfloat16))
    for step in range(micro):
        made = jnp.einsum("rld,de->rle", normed[step], qkv_weights, preferred_element_type=jnp.float32)
        qkvs.append(to_items(made.astype(jnp.bfloat16), 3))
    for step in range(micro):
        item_len = lax.dynamic_slice_in_dim(lengths[step], item_row, 1, 0)
        item_lens.append(item_len)
        mixed, lse = attend(qkvs[step], diag, item_len, head_dim)
        lses.append(lse)
        mixed_own = from_items([mixed])
        mixes.append(mixed_own)
        mixed_pair = jnp.concatenate([mixed_own, swap_core(mixed_own)], axis=2)
        resid = tokens_pair[step].astype(jnp.float32) + jnp.einsum(
            "rle,de->rld", mixed_pair, out_pair, preferred_element_type=jnp.float32
        )
        root = lax.rsqrt(jnp.mean(resid * resid, axis=-1, keepdims=True) + eps)
        normed_twos.append((resid * root * gain_second).astype(jnp.bfloat16))
        resids.append(own_half(resid, 1))

    flat = lambda value: value.reshape(-1, value.shape[-1])
    normed_two_all = jnp.concatenate([flat(v) for v in normed_twos])
    down_all = flat(down_in)
    back_kept, back_got, out_kept, out_got, chunk_totals = feed(
        normed_two_all, down_all, ready, chunk_shards[early:], dp_devices, planes, local
    )
    back_kept, back_got, out_kept, out_got = [
        v.reshape(micro, rows, local, width).astype(jnp.float32) for v in (back_kept, back_got, out_kept, out_got)
    ]

    grad_resids, grads_mixed, attn_ins = [], [], []
    gain_two_sum = jnp.zeros((width,), jnp.float32)
    for step in range(micro):
        grad_normed = back_kept[step] + back_got[step]
        resid = resids[step]
        root = lax.rsqrt(jnp.mean(resid * resid, axis=-1, keepdims=True) + eps)
        gain_two_sum = gain_two_sum + jnp.sum(grad_normed * resid * root, axis=(0, 1))
        scaled = grad_normed * gain_second
        shared = jnp.mean(scaled * resid, axis=-1, keepdims=True) * root * root * root
        grad_resid = cotangent[step].astype(jnp.float32) + scaled * root - resid * shared
        grad_resids.append(grad_resid)
        attn_in = grad_resid.astype(jnp.bfloat16)
        attn_ins.append(attn_in)
        made_own = jnp.einsum("rld,de->rle", attn_in, out_own, preferred_element_type=jnp.float32).astype(jnp.bfloat16)
        made_other = jnp.einsum("rld,de->rle", attn_in, out_other, preferred_element_type=jnp.float32).astype(
            jnp.bfloat16
        )
        grads_mixed.append(both_cores(made_own, swap_core(made_other), 1))

    outputs = []
    for step in range(micro):
        outputs.append((resids[step] + out_kept[step] + out_got[step]).astype(jnp.bfloat16))

    grads_qkv = []
    diag_sum = 0.0
    for step in range(micro):
        grad_items = to_items(grads_mixed[step], 1)
        grad_q, grad_k, grad_v, grad_diag = attend_back(
            qkvs[step], grad_items, lses[step], diag, item_lens[step], head_dim
        )
        diag_sum = diag_sum + grad_diag[:item_heads, 0]
        grads_qkv.append(from_items([grad_q, grad_k, grad_v]))
    item_grad = jnp.dot(diag_sum, bucket_hot, precision=highest)
    grad_table = lax.dynamic_update_slice(jnp.zeros((heads, levels), jnp.float32), item_grad, (head_start, 0))

    input_grads = []
    gain_one_sum = jnp.zeros((width,), jnp.float32)
    for step in range(micro):
        made = jnp.einsum("rle,de->rld", other_half(grads_qkv[step], 1), qkv_weights, preferred_element_type=jnp.float32)
        got = swap_core(made.astype(jnp.bfloat16))
        kept = jnp.einsum("rle,de->rld", own_half(grads_qkv[step], 1), qkv_weights, preferred_element_type=jnp.float32)
        grad_normed = kept + got.astype(jnp.float32)
        rows_in = tokens[step].astype(jnp.float32)
        root = own_half(roots[step], 1)
        gain_one_sum = gain_one_sum + jnp.sum(grad_normed * rows_in * root, axis=(0, 1))
        scaled = grad_normed * gain_first
        shared = jnp.mean(scaled * rows_in, axis=-1, keepdims=True) * root * root * root
        input_grads.append(grad_resids[step] + scaled * root - rows_in * shared)

    normed_all = jnp.concatenate([flat(v) for v in normed])
    grads_all = jnp.concatenate([flat(v) for v in grads_qkv])
    mixed_all = jnp.concatenate([flat(v) for v in mixes])
    attn_all = jnp.stack(attn_ins)
    attn_all = flat(both_cores(attn_all, swap_core(attn_all), 2))
    grad_attn = jnp.einsum("td,te->de", normed_all, grads_all, preferred_element_type=jnp.float32).astype(jnp.bfloat16)
    grad_o = jnp.einsum("td,te->de", attn_all, mixed_all, preferred_element_type=jnp.float32).astype(jnp.bfloat16)

    def attn_term(index):
        return jnp.concatenate(
            [lax.dynamic_slice_in_dim(g, index * shard_rows, shard_rows, 0) for g in (grad_attn, grad_o)], axis=1
        )

    attn_total = ring.scatter(attn_term, 4 * half_inner)

    def finish(total):
        if planes == 2:
            low = total.astype(jnp.bfloat16)
            got = lax.ppermute(low, "seq", [(i, i ^ 2) for i in range(4)])
            total = low.astype(jnp.float32) + got.astype(jnp.float32)
        else:
            total = lax.psum(total, "seq", axis_index_groups=plane_groups)
        return total, swap_core(total)

    def whole_columns(own, other, size):
        low, high = jnp.where(first, own, other), jnp.where(first, other, own)
        return jnp.concatenate([low, high[:, : size - low.shape[1]]], axis=1)

    own, other = finish(attn_total)
    parts = [slice(i * half_inner, (i + 1) * half_inner) for i in range(4)]
    grad_query, grad_key, grad_value, grad_out = [whole_columns(own[:, p], other[:, p], inner) for p in parts]
    done = [finish(chunk_totals[n]) for n in range(chunks)]
    parts = [slice(i * chunk, (i + 1) * chunk) for i in range(3)]
    grad_gate, grad_up, grad_down = [
        whole_columns(
            jnp.concatenate([own[:, p] for own, _ in done], axis=1),
            jnp.concatenate([other[:, p] for _, other in done], axis=1),
            hidden_units,
        )
        for p in parts
    ]

    dp_rank = lax.axis_index("dp")
    small = lax.psum(
        jnp.concatenate([gain_one_sum, gain_two_sum, grad_table.T.reshape(-1)]), ("dp", "seq")
    )
    grad_gain_one = lax.dynamic_slice_in_dim(small, dp_rank * shard_rows, shard_rows, 0)
    grad_gain_two = lax.dynamic_slice_in_dim(small, width + dp_rank * shard_rows, shard_rows, 0)
    table_part = levels // dp_devices
    grad_table = lax.dynamic_slice_in_dim(small[2 * width :].reshape(levels, heads), dp_rank * table_part, table_part, 0)

    return (
        jnp.stack(outputs), jnp.stack(input_grads), grad_gain_one, grad_gain_two, grad_table,
        grad_query, grad_key, grad_value, grad_out.T, grad_gate, grad_up, grad_down.T,
    )


def solution(mesh):
    weight, turned = P("dp", None), P(None, "dp")
    return jax.shard_map(
        body,
        mesh=mesh,
        in_specs=(
            P(None, "dp", "seq", None), P(None, "dp", "seq", None), P(None, "dp"), P(), P("dp"), P("dp"),
            weight, weight, weight, weight, turned, weight, weight, turned,
        ),
        out_specs=(
            P(None, "dp", "seq", None), P(None, "dp", "seq", None), P("dp"), P("dp"),
            weight, weight, weight, weight, turned, weight, weight, turned,
        ),
        check_vma=False,
    )
```

```python
import functools

import jax
import jax.numpy as jnp
from jax import lax
from jax.experimental import pallas as pl
from jax.experimental.pallas import tpu as pltpu
from jax.sharding import PartitionSpec as P

eps = 1e-06
masked_value = -1e30
highest = lax.Precision.HIGHEST
gelu_scale = 0.7978845608028654
gelu_cubic = 0.044715
LANES = 128
VMEM_LIMIT = 56 * 1024 * 1024
NT = (((1,), (1,)), ((), ()))
NN = (((1,), (0,)), ((), ()))
TN = (((0,), (0,)), ((), ()))


def dot32(a, b, dims):
    return lax.dot_general(a, b, dims, preferred_element_type=jnp.float32)


def toeplitz_strip(diag_row, span):
    wide = jnp.broadcast_to(diag_row, (LANES, span))
    return pltpu.roll(wide, span - (LANES - 1), 1, stride=1, stride_axis=0)


def with_mask_lane(key_pair, lanes, here, spare, length):
    rows = lax.broadcasted_iota(jnp.int32, key_pair.shape, 0)
    mask = jnp.where(rows < length, 0.0, masked_value).astype(key_pair.dtype)
    zero = jnp.zeros_like(key_pair)
    return jnp.where(here, key_pair, jnp.where(lanes == spare, mask, zero))


def attend_kernel(head_dim, block, len_ref, diag_ref, q_ref, k_ref, v_ref, mixed_ref, lse_ref, strip, keys):
    step = pl.program_id(1)
    seq_len = k_ref.shape[0]
    span = diag_ref.shape[-1]
    length = len_ref[0]
    per = LANES // head_dim
    lanes_k = lax.broadcasted_iota(jnp.int32, (seq_len, LANES), 1)
    lanes_q = lax.broadcasted_iota(jnp.int32, (block, LANES), 1)

    @pl.when(step == 0)
    def _():
        for head in range(per):
            strip[head] = toeplitz_strip(diag_ref[head], span)
            here = lanes_k // head_dim == head
            spare = ((head + 1) % per) * head_dim
            keys[head] = with_mask_lane(k_ref[...], lanes_k, here, spare, length)

    mixed = None
    for head in range(per):
        here = lanes_q // head_dim == head
        spare = ((head + 1) % per) * head_dim
        one = (lanes_q == spare).astype(q_ref.dtype)
        query = jnp.where(here, q_ref[...], one)
        raw = dot32(query, keys[head], NT)
        parts = []
        for sub in range(block // LANES):
            offset = seq_len - LANES - (step * block + sub * LANES)
            offset = pl.multiple_of(offset, LANES)
            parts.append(raw[sub * LANES : (sub + 1) * LANES] + strip[head, :, pl.ds(offset, seq_len)])
        scores = jnp.concatenate(parts, axis=0)
        top = jnp.max(scores, axis=1, keepdims=True)
        expo = jnp.exp(scores - top)
        total = jnp.sum(expo, axis=1, keepdims=True)
        made = dot32(expo.astype(jnp.bfloat16), v_ref[...], NN) / total
        mixed = made if mixed is None else jnp.where(here, made, mixed)
        lse = jnp.broadcast_to(top + jnp.log(total), (block, LANES))
        lse_ref[head] = lse.T[:1]
    mixed_ref[...] = mixed.astype(mixed_ref.dtype)


def attend(qkv, diag, length, head_dim, by_pair=False, block=256):
    seq_len, cols = qkv.shape[0], qkv.shape[1] // 3
    pairs = cols // LANES
    per = LANES // head_dim
    span = diag.shape[-1]
    at = (lambda part, p: 3 * p + part) if by_pair else (lambda part, p: part * pairs + p)
    flops = 2 * 2 * seq_len * seq_len * LANES * 2 * cols // head_dim
    return pl.pallas_call(
        functools.partial(attend_kernel, head_dim, block),
        grid=(pairs, seq_len // block),
        in_specs=[
            pl.BlockSpec(memory_space=pltpu.SMEM),
            pl.BlockSpec((per, 1, span), lambda p, b: (p, 0, 0)),
            pl.BlockSpec((block, LANES), lambda p, b: (b, at(0, p))),
            pl.BlockSpec((seq_len, LANES), lambda p, b: (0, at(1, p))),
            pl.BlockSpec((seq_len, LANES), lambda p, b: (0, at(2, p))),
        ],
        out_specs=[
            pl.BlockSpec((block, LANES), lambda p, b: (b, p)),
            pl.BlockSpec((per, 1, block), lambda p, b: (p, 0, b)),
        ],
        out_shape=[
            jax.ShapeDtypeStruct((seq_len, cols), jnp.bfloat16),
            jax.ShapeDtypeStruct((cols // head_dim, 1, seq_len), jnp.float32),
        ],
        scratch_shapes=[
            pltpu.VMEM((per, LANES, span), jnp.float32),
            pltpu.VMEM((per, seq_len, LANES), jnp.bfloat16),
        ],
        compiler_params=pltpu.CompilerParams(vmem_limit_bytes=VMEM_LIMIT),
        cost_estimate=pl.CostEstimate(flops=flops, bytes_accessed=8 * seq_len * cols, transcendentals=0),
        name="attend",
    )(length, diag, qkv, qkv, qkv)


def attend_back_kernel(
    head_dim, block, len_ref, diag_ref, q_ref, k_ref, v_ref, do_ref, lse_ref,
    dq_ref, dk_ref, dv_ref, dd_ref, strip, keys, acc_bias, acc_k, acc_v,
):
    step = pl.program_id(1)
    steps = pl.num_programs(1)
    seq_len = k_ref.shape[0]
    span = diag_ref.shape[-1]
    length = len_ref[0]
    per = LANES // head_dim
    lanes_k = lax.broadcasted_iota(jnp.int32, (seq_len, LANES), 1)
    lanes_q = lax.broadcasted_iota(jnp.int32, (block, LANES), 1)
    subs = block // LANES

    @pl.when(step == 0)
    def _():
        for head in range(per):
            strip[head] = toeplitz_strip(diag_ref[head], span).T
            here = lanes_k // head_dim == head
            spare = ((head + 1) % per) * head_dim
            keys[head] = with_mask_lane(k_ref[...], lanes_k, here, spare, length)
        acc_bias[...] = jnp.zeros_like(acc_bias)
        acc_k[...] = jnp.zeros_like(acc_k)
        acc_v[...] = jnp.zeros_like(acc_v)

    grad_query = None
    for head in range(per):
        here = lanes_q // head_dim == head
        spare = ((head + 1) % per) * head_dim
        zero = jnp.zeros_like(q_ref[...])
        one = (lanes_q == spare).astype(q_ref.dtype)
        query = jnp.where(here, q_ref[...], zero)
        grad = jnp.where(here, do_ref[...], zero)
        raw = dot32(keys[head], query + one, NT)
        grad_probs = dot32(v_ref[...], grad, NT)
        parts = []
        offsets = []
        for sub in range(subs):
            offset = seq_len - LANES - (step * block + sub * LANES)
            offset = pl.multiple_of(offset, LANES)
            offsets.append(offset)
            parts.append(raw[:, sub * LANES : (sub + 1) * LANES] + strip[head, pl.ds(offset, seq_len), :])
        scores = jnp.concatenate(parts, axis=1)
        probs = jnp.exp(scores - lse_ref[head])
        product = probs * grad_probs
        inner = jnp.sum(product, axis=0, keepdims=True)
        grad_scores = product - probs * inner
        for sub in range(subs):
            rows = pl.ds(offsets[sub], seq_len)
            acc_bias[head, rows, :] += grad_scores[:, sub * LANES : (sub + 1) * LANES]
        rounded = grad_scores.astype(jnp.bfloat16)
        acc_v[...] += dot32(probs.astype(jnp.bfloat16), grad, NN)
        acc_k[...] += dot32(rounded, query, NN)
        made = dot32(rounded, k_ref[...], TN)
        grad_query = made if grad_query is None else jnp.where(here, made, grad_query)
    dq_ref[...] = grad_query.astype(dq_ref.dtype)

    @pl.when(step == steps - 1)
    def _():
        dk_ref[...] = acc_k[...].astype(dk_ref.dtype)
        dv_ref[...] = acc_v[...].astype(dv_ref.dtype)
        row = lax.broadcasted_iota(jnp.int32, (LANES, LANES), 0)
        col = lax.broadcasted_iota(jnp.int32, (LANES, LANES), 1)
        flip = (row + col == LANES - 1).astype(jnp.float32)
        for head in range(per):
            turned = lax.dot_general(
                flip, acc_bias[head], NT, precision=lax.Precision.HIGHEST, preferred_element_type=jnp.float32
            )
            aligned = pltpu.roll(turned, 0, 1, stride=1, stride_axis=0)
            dd_ref[head] = jnp.sum(aligned, axis=0, keepdims=True)


def attend_back(qkv, grad_mixed, lse, diag, length, head_dim, block=256):
    seq_len, cols = qkv.shape[0], qkv.shape[1] // 3
    pairs = cols // LANES
    per = LANES // head_dim
    span = diag.shape[-1]
    flops = 5 * 2 * seq_len * seq_len * LANES * 2 * cols // head_dim
    whole = lambda p, b: (0, p)
    part = lambda p, b: (b, p)
    flat = jax.ShapeDtypeStruct((seq_len, cols), jnp.bfloat16)
    return pl.pallas_call(
        functools.partial(attend_back_kernel, head_dim, block),
        grid=(pairs, seq_len // block),
        in_specs=[
            pl.BlockSpec(memory_space=pltpu.SMEM),
            pl.BlockSpec((per, 1, span), lambda p, b: (p, 0, 0)),
            pl.BlockSpec((block, LANES), part),
            pl.BlockSpec((seq_len, LANES), lambda p, b: (0, pairs + p)),
            pl.BlockSpec((seq_len, LANES), lambda p, b: (0, 2 * pairs + p)),
            pl.BlockSpec((block, LANES), part),
            pl.BlockSpec((per, 1, block), lambda p, b: (p, 0, b)),
        ],
        out_specs=[
            pl.BlockSpec((block, LANES), part),
            pl.BlockSpec((seq_len, LANES), whole),
            pl.BlockSpec((seq_len, LANES), whole),
            pl.BlockSpec((per, 1, span), lambda p, b: (p, 0, 0)),
        ],
        out_shape=[flat, flat, flat, jax.ShapeDtypeStruct(diag.shape, jnp.float32)],
        scratch_shapes=[
            pltpu.VMEM((per, span, LANES), jnp.float32),
            pltpu.VMEM((per, seq_len, LANES), jnp.bfloat16),
            pltpu.VMEM((per, span, LANES), jnp.float32),
            pltpu.VMEM((seq_len, LANES), jnp.float32),
            pltpu.VMEM((seq_len, LANES), jnp.float32),
        ],
        compiler_params=pltpu.CompilerParams(vmem_limit_bytes=VMEM_LIMIT),
        cost_estimate=pl.CostEstimate(flops=flops, bytes_accessed=16 * seq_len * cols, transcendentals=0),
        name="attend_back",
    )(length, diag, qkv, qkv, qkv, grad_mixed, lse)


def gated_values(gate, up, grad):
    square = gate * gate
    turn = jnp.tanh(gelu_scale * gate * (1.0 + gelu_cubic * square))
    half = 0.5 * (1.0 + turn)
    act = gate * half
    slope = half + 0.5 * gate * (1.0 - turn * turn) * gelu_scale * (1.0 + 3.0 * gelu_cubic * square)
    low = jnp.bfloat16
    return (grad * up * slope).astype(low), (grad * act).astype(low), (act * up).astype(low)


def ring_order(count):
    if count % 4 or count < 8:
        return list(range(count))
    long, short = 4, count // 4
    walk = []
    for line in range(long):
        columns = range(1, short) if line % 2 == 0 else range(short - 1, 0, -1)
        walk += [line * short + column for column in columns]
    return walk + [line * short for line in range(long - 1, -1, -1)]


MESH = pl.DeviceIdType.MESH


def pick(options, at):
    value = jnp.int32(options[0])
    for index in range(1, len(options)):
        value = jnp.where(at == index, jnp.int32(options[index]), value)
    return value


class Links:
    def __init__(self, count, planes):
        order = ring_order(count)
        place = [0] * count
        for at, index in enumerate(order):
            place[index] = at
        self.count, self.order, self.planes = count, order, planes
        self.place = pick(place, lax.axis_index("dp"))
        seq = lax.axis_index("seq")
        self.core = seq % 2
        self.plane = seq // 2
        self.sibling = {"seq": self.plane * 2 + 1 - self.core}
        self.across = {"seq": (1 - self.plane) * 2 + self.core}
        self.ahead = {"dp": self.owner(1)}
        self.behind = {"dp": self.owner(-1)}

    def owner(self, shift):
        return pick(self.order, lax.rem(self.place + shift + self.count, self.count))

    def greet(self):
        barrier = pltpu.get_barrier_semaphore()
        friends = [self.ahead, self.behind, self.sibling] + ([self.across] if self.planes == 2 else [])
        for friend in friends:
            pl.semaphore_signal(barrier, inc=1, device_id=friend, device_id_type=MESH)
        pl.semaphore_wait(barrier, len(friends))


class Gather:
    def __init__(self, links, shard, whole, sems, rows):
        self.links, self.shard, self.whole, self.sems, self.rows = links, shard, whole, sems, rows
        self.far = links.count // 2
        self.shared = links.planes == 2
        self.third = rows // 3
        self.size = 2 * self.third if self.shared else rows
        self.cut = -(-(self.size // 2) // 16) * 16

    def base(self, shift):
        start = self.links.owner(shift) * self.rows
        if self.shared:
            start = start + self.links.plane * self.third
        return pl.multiple_of(start, 16)

    def ring_copy(self, step, forward):
        shift = (1 - step) if forward else (step - 1)
        offset, size = 0, self.size
        if step == self.far:
            offset, size = (0, self.cut) if forward else (self.cut, self.size - self.cut)
        place = self.whole.at[pl.ds(pl.multiple_of(self.base(shift) + offset, 16), size)]
        source = place
        if step == 1:
            first = self.links.plane * self.third if self.shared else 0
            source = self.shard.at[pl.ds(pl.multiple_of(first + offset, 16), size)]
        return pltpu.make_async_remote_copy(
            src_ref=source,
            dst_ref=place,
            send_sem=self.sems.at[0 if forward else 1, step],
            recv_sem=self.sems.at[2 if forward else 3, step],
            device_id=self.links.ahead if forward else self.links.behind,
            device_id_type=MESH,
        )

    def recv_copy(self, step, forward):
        shift = -step if forward else step
        offset, size = 0, self.size
        if step == self.far:
            offset, size = (0, self.cut) if forward else (self.cut, self.size - self.cut)
        place = self.whole.at[pl.ds(pl.multiple_of(self.base(shift) + offset, 16), size)]
        return pltpu.make_async_remote_copy(
            src_ref=place,
            dst_ref=place,
            send_sem=self.sems.at[0 if forward else 1, step],
            recv_sem=self.sems.at[2 if forward else 3, step],
            device_id=self.links.ahead if forward else self.links.behind,
            device_id_type=MESH,
        )

    def across_copy(self, slot, shift, receive):
        plane = 1 - self.links.plane if receive else self.links.plane
        start = self.links.owner(shift) * self.rows + plane * 2 * self.third
        place = self.whole.at[pl.ds(pl.multiple_of(start, 16), self.third)]
        return pltpu.make_async_remote_copy(
            src_ref=place,
            dst_ref=place,
            send_sem=self.sems.at[4, slot],
            recv_sem=self.sems.at[5, slot],
            device_id=self.links.across,
            device_id_type=MESH,
        )

    def start(self):
        self.ring_copy(1, True).start()
        self.ring_copy(1, False).start()

    def advance(self, step):
        last = step == self.far
        for forward in (True, False):
            self.recv_copy(step, forward).wait_recv()
            if not last:
                self.ring_copy(step + 1, forward).start()
            if self.shared and not last:
                slot = 2 * step - 2 + (0 if forward else 1)
                self.across_copy(slot, -step if forward else step, False).start()
        if self.shared and last:
            self.across_copy(2 * step - 2, step, False).start()

    def slots(self):
        shifts = []
        for step in range(1, self.far):
            shifts += [(2 * step - 2, -step), (2 * step - 1, step)]
        return shifts + [(2 * self.far - 2, self.far)]

    def finish(self):
        for step in range(1, self.far + 1):
            self.ring_copy(step, True).wait_send()
            self.ring_copy(step, False).wait_send()
        if self.shared:
            for slot, shift in self.slots():
                self.across_copy(slot, shift, False).wait_send()
                self.across_copy(slot, shift, True).wait_recv()


def gather_kernel(count, planes, rows, shard, small, tokens, cotangent, whole, smalls, tokens_there, cotangent_there, sems, sems_small, sems_core, own):
    links = Links(count, planes)
    keep = pltpu.make_async_copy(shard, whole.at[pl.ds(pl.multiple_of(links.owner(0) * rows, 16), rows)], own.at[0])
    keep_small = pltpu.make_async_copy(small, smalls.at[pl.ds(pl.multiple_of(links.owner(0) * 16, 16), 16)], own.at[1])
    keep.start()
    keep_small.start()
    links.greet()
    large = Gather(links, shard, whole, sems, rows)
    little = SmallGather(links, small, smalls, sems_small)
    little.start()
    large.start()
    swaps = []
    for at, (source, target) in enumerate(((tokens, tokens_there), (cotangent, cotangent_there))):
        swaps.append(
            pltpu.make_async_remote_copy(
                src_ref=source, dst_ref=target, send_sem=sems_core.at[at, 0], recv_sem=sems_core.at[at, 1],
                device_id=links.sibling, device_id_type=MESH,
            )
        )
        swaps[-1].start()
    for step in range(1, large.far + 1):
        little.advance(step)
        large.advance(step)
    for swap in swaps:
        swap.wait()
    little.finish()
    large.finish()
    keep.wait()
    keep_small.wait()


class SmallGather(Gather):
    def __init__(self, links, shard, whole, sems):
        self.links, self.shard, self.whole, self.sems, self.rows = links, shard, whole, sems, 16
        self.far, self.shared, self.size, self.cut = links.count // 2, False, 16, 16

    def start(self):
        self.ring_copy(1, True).start()
        self.ring_copy(1, False).start()

    def advance(self, step):
        self.recv_copy(step, True).wait_recv()
        if step < self.far:
            self.ring_copy(step + 1, True).start()
            self.recv_copy(step, False).wait_recv()
            if step + 1 < self.far:
                self.ring_copy(step + 1, False).start()

    def finish(self):
        for step in range(1, self.far + 1):
            self.ring_copy(step, True).wait_send()
            if step < self.far:
                self.ring_copy(step, False).wait_send()


def gather_first(shard, small, tokens, cotangent, count, planes):
    rows, cols = shard.shape
    anywhere = pl.BlockSpec(memory_space=pl.ANY)
    return pl.pallas_call(
        functools.partial(gather_kernel, count, planes, rows),
        in_specs=[anywhere] * 4,
        out_specs=[anywhere] * 4,
        out_shape=[
            jax.ShapeDtypeStruct((count * rows, cols), shard.dtype),
            jax.ShapeDtypeStruct((count * 16, small.shape[1]), small.dtype),
            jax.ShapeDtypeStruct(tokens.shape, tokens.dtype),
            jax.ShapeDtypeStruct(cotangent.shape, cotangent.dtype),
        ],
        scratch_shapes=[
            pltpu.SemaphoreType.DMA((6, count)),
            pltpu.SemaphoreType.DMA((4, count)),
            pltpu.SemaphoreType.DMA((2, 2)),
            pltpu.SemaphoreType.DMA((2,)),
        ],
        compiler_params=pltpu.CompilerParams(collective_id=0, has_side_effects=True),
        name="gather_first",
    )(shard, small, tokens, cotangent)


class Scatter:
    def __init__(self, links, grads, inbox, totals, mine, came, made, total, send_sems, recv_sems, near_sems, total_sems, rows):
        self.links, self.grads, self.inbox, self.totals = links, grads, inbox, totals
        self.mine, self.came, self.made, self.total = mine, came, made, total
        self.send_sems, self.recv_sems, self.near_sems, self.total_sems = send_sems, recv_sems, near_sems, total_sems
        self.rows = rows
        self.far = links.count // 2
        self.cut = -(-(rows // 2) // 16) * 16
        self.spaces = made.shape[0]

    def part(self, step, way):
        if step > 1:
            return 0, self.rows
        return (0, self.cut) if way == 0 else (self.cut, self.rows - self.cut)

    def term(self, chunk, shift, offset, size):
        start = self.links.owner(shift) * self.rows + offset
        return self.grads.at[chunk, pl.ds(pl.multiple_of(start, 16), size)]

    def hop(self, chunk, step, way):
        offset, size = self.part(step, way)
        if step == 1:
            source = self.term(chunk, self.far, offset, size)
        else:
            source = self.made.at[lax.rem(chunk, self.spaces), way, pl.ds(offset, size)]
        return pltpu.make_async_remote_copy(
            src_ref=source,
            dst_ref=self.inbox.at[chunk, way, step - 1, pl.ds(offset, size)],
            send_sem=self.send_sems.at[chunk, way, step - 1],
            recv_sem=self.recv_sems.at[chunk, way, step - 1],
            device_id=self.links.behind if way else self.links.ahead,
            device_id_type=MESH,
        )

    def near(self, chunk, step, way):
        offset, size = self.part(step, way)
        space = lax.rem(chunk, self.spaces)
        shift = (step - self.far) if way else (self.far - step)
        copies = [
            pltpu.make_async_copy(
                self.inbox.at[chunk, way, step - 1, pl.ds(offset, size)],
                self.came.at[space, way, pl.ds(offset, size)],
                self.near_sems.at[space, way, 0],
            )
        ]
        if step < self.far or way == 0:
            copies.append(
                pltpu.make_async_copy(
                    self.term(chunk, shift, 0, self.rows), self.mine.at[space, way], self.near_sems.at[space, way, 1]
                )
            )
        return copies

    def start(self, chunk):
        for way in range(2):
            self.hop(chunk, 1, way).start()

    def fetch(self, chunk, step):
        for way in range(2):
            self.hop(chunk, step, way).wait_recv()
            for copy in self.near(chunk, step, way):
                copy.start()

    def pass_on(self, chunk, step):
        space = lax.rem(chunk, self.spaces)
        for way in range(2):
            for copy in self.near(chunk, step, way):
                copy.wait()
            self.hop(chunk, step, way).wait_send()
            offset, size = self.part(step, way)
            rows = pl.ds(offset, size)
            if size < self.rows:
                other = pl.ds(0 if way else size, self.rows - size)
                self.made[space, way, other] = self.mine[space, way, other]
            self.made[space, way, rows] = add_low(self.mine[space, way, rows], self.came[space, way, rows])
            self.hop(chunk, step + 1, way).start()

    def total_copy(self, chunk):
        return pltpu.make_async_copy(self.total, self.totals.at[chunk], self.total_sems.at[0])

    def close(self, chunk):
        space = lax.rem(chunk, self.spaces)
        for way in range(2):
            for copy in self.near(chunk, self.far, way):
                copy.wait()
            self.hop(chunk, self.far, way).wait_send()

        @pl.when(chunk > 0)
        def _():
            self.total_copy(chunk - 1).wait()

        total = self.mine[space, 0].astype(jnp.float32) + self.came[space, 0].astype(jnp.float32)
        self.total[...] = total + self.came[space, 1].astype(jnp.float32)
        self.total_copy(chunk).start()


def feed_kernel(plan, *refs):
    count, planes, rows, chunks, early, tile, block, groups = plan
    late = chunks - early
    (normed, down, *rest) = refs
    ready, shards = rest[:early], rest[early:chunks]
    rest = rest[chunks:]
    back_kept, back_got, out_kept, out_got, totals, pieces, grads, inbox = rest[:8]
    wholes = rest[8 : 8 + late]
    (
        a_all, b_all, weights, piece, stage, mine, came, made, total, out_stage,
        in_sems, piece_sems, stage_sems, fetch_sems, keep_sems, give_sems, take_sems,
        send_sems, recv_sems, near_sems, total_sems, own_sems, *gather_sems,
    ) = rest[8 + late :]
    tokens, depth = a_all.shape
    width = weights.shape[2] // 3
    tiles, blocks = tokens // tile, depth // block
    per = tiles + blocks
    front = chunks * per
    links = Links(count, planes)
    far = count // 2

    loads = [pltpu.make_async_copy(normed, a_all, in_sems.at[chunks]), pltpu.make_async_copy(down, b_all, in_sems.at[chunks + 1])]
    loads += [pltpu.make_async_copy(ready[n], weights.at[n], in_sems.at[n]) for n in range(early)]
    keeps = []
    for n in range(late):
        place = wholes[n].at[pl.ds(pl.multiple_of(links.owner(0) * rows, 16), rows)]
        keeps.append(pltpu.make_async_copy(shards[n], place, own_sems.at[n]))
    for copy in loads + keeps:
        copy.start()
    links.greet()
    gathers = [Gather(links, shards[n], wholes[n], gather_sems[n], rows) for n in range(late)]
    scatter = Scatter(
        links, grads, inbox, totals, mine, came, made, total, send_sems, recv_sems, near_sems, total_sems, rows
    )
    loads[0].wait()
    loads[1].wait()

    gap_gather = max(1, 16 // far)
    gap = max(2, 20 // far)

    def load_weights(n):
        source = ready[n] if n < early else wholes[n - early]
        return pltpu.make_async_copy(source, weights.at[n], in_sems.at[n])

    def piece_copy(n, t):
        place = pl.ds(pl.multiple_of(t * tile, 16), tile)
        return pltpu.make_async_copy(piece.at[place], pieces.at[n, place], piece_sems.at[t])

    def stage_copy(n, b):
        slot = lax.rem(b, 2)
        place = pl.ds(pl.multiple_of(b * block, 16), block)
        return pltpu.make_async_copy(stage.at[slot], grads.at[n, place], stage_sems.at[slot])

    def back_rows(g, half):
        start = (2 * g + half) * tile
        return pl.ds(pl.multiple_of(start, 16), tile)

    def fetch_copy(n, t):
        half = jnp.where(lax.rem(t, 2) == 0, 1 - links.core, links.core)
        slot = lax.rem(t, 2)
        target = pl.ds(pl.multiple_of((slot * chunks + n) * tile, 16), tile)
        return pltpu.make_async_copy(pieces.at[n, back_rows(t // 2, half)], piece.at[target], fetch_sems.at[slot, n])

    def give_copy(kind, g):
        target = (back_got, out_got)[kind]
        return pltpu.make_async_remote_copy(
            src_ref=out_stage.at[kind, 0], dst_ref=target.at[g], send_sem=give_sems.at[kind], recv_sem=take_sems.at[kind, g],
            device_id=links.sibling, device_id_type=MESH,
        )

    def keep_copy(kind, g):
        target = (back_kept, out_kept)[kind]
        return pltpu.make_async_copy(out_stage.at[kind, 1], target.at[g], keep_sems.at[kind])

    items_back = 4 * groups
    last_event = front + 1 + gap * far
    total_items = max(front + items_back, last_event + 1)

    def item(i, carry):
        n, j = i // per, lax.rem(i, per)

        for k in range(late):
            base = k * per
            for step in range(far + 2):

                @pl.when(i == base + step * gap_gather)
                def _(k=k, step=step):
                    if step == 0:
                        gathers[k].start()
                    elif step <= far:
                        gathers[k].advance(step)
                    else:
                        gathers[k].finish()
                        keeps[k].wait()
                        load_weights(early + k).start()

        def event(offset, act):
            past = i - per - offset

            @pl.when((past >= 0) & (past < front) & (lax.rem(past + per * 64, per) == 0))
            def _():
                act(past // per)

        def begin(chunk):
            for b in (blocks - 2, blocks - 1):
                stage_copy(chunk, b).wait()
            scatter.start(chunk)

        event(0, begin)
        for step in range(1, far + 1):
            event(step * gap - 1, lambda chunk, step=step: scatter.fetch(chunk, step))
            if step < far:
                event(step * gap, lambda chunk, step=step: scatter.pass_on(chunk, step))
            else:
                event(step * gap, scatter.close)

        @pl.when((i < front) & (j == 0))
        def _():
            for m in range(chunks):

                @pl.when(n == m)
                def _(m=m):
                    load_weights(m).wait()

        @pl.when((i < front) & (j < tiles))
        def _():
            @pl.when(n > 0)
            def _():
                piece_copy(n - 1, j).wait()

            place = pl.ds(pl.multiple_of(j * tile, 16), tile)
            a, d = a_all[place], b_all[place]
            gate = dot32(a, weights[n, :, :width], NN)
            up = dot32(a, weights[n, :, width : 2 * width], NN)
            grad = dot32(d, weights[n, :, 2 * width :], NN)
            d_gate, d_up, hidden = gated_values(gate, up, grad)
            piece[place, :width] = d_gate
            piece[place, width : 2 * width] = d_up
            piece[place, 2 * width :] = hidden
            piece_copy(n, j).start()

        @pl.when((i < front) & (j >= tiles))
        def _():
            b = j - tiles

            @pl.when(b >= 2)
            def _():
                stage_copy(n, b - 2).wait()

            place = pl.ds(pl.multiple_of(b * block, LANES), block)
            slot = lax.rem(b, 2)
            first = dot32(a_all[:, place], piece[:, : 2 * width], TN)
            stage[slot, :, : 2 * width] = first.astype(stage.dtype)
            second = dot32(b_all[:, place], piece[:, 2 * width :], TN)
            stage[slot, :, 2 * width :] = second.astype(stage.dtype)
            stage_copy(n, b).start()

        @pl.when(i == front)
        def _():
            for t in range(tiles):
                piece_copy(chunks - 1, t).wait()
            for m in range(chunks):
                fetch_copy(m, 0).start()

        at = i - front
        t, kind_at = at // 2, lax.rem(at + 2 * per, 2)
        for kind in range(2):

            @pl.when((at >= 0) & (at < items_back) & (kind_at == kind))
            def _(kind=kind):
                slot, g = lax.rem(t, 2), t // 2
                if kind == 0:
                    for m in range(chunks):
                        fetch_copy(m, t).wait()

                    @pl.when(t + 1 < 2 * groups)
                    def _():
                        for m in range(chunks):
                            fetch_copy(m, t + 1).start()

                columns = slice(0, 2 * width) if kind == 0 else slice(2 * width, 3 * width)
                made_sum = None
                for m in range(chunks):
                    place = pl.ds(pl.multiple_of((slot * chunks + m) * tile, 16), tile)
                    term = dot32(piece[place, columns], weights[m, :, columns], NT)
                    made_sum = term if made_sum is None else made_sum + term

                @pl.when((t >= 2) & (slot == 0))
                def _():
                    give_copy(kind, g - 1).wait_send()

                @pl.when((t >= 2) & (slot == 1))
                def _():
                    keep_copy(kind, g - 1).wait()

                out_stage[kind, slot] = made_sum.astype(out_stage.dtype)

                @pl.when(slot == 0)
                def _():
                    give_copy(kind, g).start()

                @pl.when(slot == 1)
                def _():
                    keep_copy(kind, g).start()

        return carry

    lax.fori_loop(0, total_items, item, 0)
    scatter.total_copy(chunks - 1).wait()
    for kind in range(2):
        give_copy(kind, groups - 1).wait_send()
        keep_copy(kind, groups - 1).wait()
        for g in range(groups):
            give_copy(kind, g).wait_recv()


def feed(normed, down, ready, shards, count, planes, tile):
    tokens, depth = normed.shape
    rows, cols = shards[0].shape
    early, chunks = len(ready), len(ready) + len(shards)
    far = count // 2
    block = 384
    groups = tokens // (2 * tile)
    spaces = 2 if far <= 4 else chunks
    plan = (count, planes, rows, chunks, early, tile, block, groups)
    anywhere = pl.BlockSpec(memory_space=pl.ANY)
    low, wide = jnp.bfloat16, jnp.float32
    part = jax.ShapeDtypeStruct((groups, tile, depth), low)
    shapes = [part] * 4 + [
        jax.ShapeDtypeStruct((chunks, rows, cols), wide),
        jax.ShapeDtypeStruct((chunks, tokens, cols), low),
        jax.ShapeDtypeStruct((chunks, depth, cols), low),
        jax.ShapeDtypeStruct((chunks, 2, far, rows, cols), low),
    ]
    shapes += [jax.ShapeDtypeStruct((depth, cols), low)] * len(shards)
    dma = pltpu.SemaphoreType.DMA
    made = pl.pallas_call(
        functools.partial(feed_kernel, plan),
        in_specs=[anywhere] * (2 + chunks),
        out_specs=[anywhere] * len(shapes),
        out_shape=shapes,
        scratch_shapes=[
            pltpu.VMEM((tokens, depth), low),
            pltpu.VMEM((tokens, depth), low),
            pltpu.VMEM((chunks, depth, cols), low),
            pltpu.VMEM((tokens, cols), low),
            pltpu.VMEM((2, block, cols), low),
            pltpu.VMEM((spaces, 2, rows, cols), low),
            pltpu.VMEM((spaces, 2, rows, cols), low),
            pltpu.VMEM((spaces, 2, rows, cols), low),
            pltpu.VMEM((rows, cols), wide),
            pltpu.VMEM((2, 2, tile, depth), low),
            dma((chunks + 2,)),
            dma((tokens // tile,)),
            dma((2,)),
            dma((2, chunks)),
            dma((2,)),
            dma((2,)),
            dma((2, groups)),
            dma((chunks, 2, far)),
            dma((chunks, 2, far)),
            dma((spaces, 2, 2)),
            dma((1,)),
            dma((len(shards),)),
        ]
        + [dma((6, count))] * len(shards),
        compiler_params=pltpu.CompilerParams(
            collective_id=1, has_side_effects=True, vmem_limit_bytes=62 * 1024 * 1024
        ),
        cost_estimate=pl.CostEstimate(
            flops=18 * tokens * depth * cols // 3 * chunks, bytes_accessed=10 * tokens * depth, transcendentals=0
        ),
        name="feed",
    )(normed, down, *ready, *shards)
    return made[:5]


def mix_back_kernel(plan, len_ref, lse_ref, diag_ref, *refs):
    count, planes, rows, micro, rows_of, head_dim, block, pairs = plan
    qkvs, grads_mixed = refs[:micro], refs[micro : 2 * micro]
    attn_in, mixed, normed = refs[2 * micro : 2 * micro + 3]
    dqkv, dd_ref, totals, attn_there = refs[2 * micro + 3 : 2 * micro + 7]
    (
        qkv_v, do_v, res, sums_v, attn_v, mixed_v, normed_v, grads, inbox,
        strip, keys, acc_bias, acc_k, acc_v, mine, came, made, total,
        load_sems, do_sems, res_sems, attn_sems, dqkv_sems, send_sems, recv_sems, near_sems, total_sems,
    ) = refs[2 * micro + 7 :]
    seq_len = do_v.shape[1]
    span = diag_ref.shape[-1]
    plane_len = seq_len // 2
    local = attn_in.shape[2]
    steps = seq_len // block
    per = LANES // head_dim
    wide = 3 * LANES
    units = pairs * micro
    links = Links(count, planes)
    far = count // 2
    plane, core = links.plane, links.core
    lanes_k = lax.broadcasted_iota(jnp.int32, (seq_len, LANES), 1)
    lanes_q = lax.broadcasted_iota(jnp.int32, (block, LANES), 1)

    def at_rows(start, size):
        return pl.ds(pl.multiple_of(start, 16), size)

    def do_far(m):
        return pltpu.make_async_remote_copy(
            src_ref=grads_mixed[m].at[1 - plane], dst_ref=do_v.at[m, at_rows(plane * plane_len, plane_len)],
            send_sem=do_sems.at[m, 0], recv_sem=do_sems.at[m, 1], device_id=links.across, device_id_type=MESH,
        )

    def do_near(m):
        return pltpu.make_async_copy(
            grads_mixed[m].at[plane], do_v.at[m, at_rows(plane * plane_len, plane_len)], do_sems.at[m, 2]
        )

    def attn_far():
        return pltpu.make_async_remote_copy(
            src_ref=attn_in, dst_ref=attn_there, send_sem=attn_sems.at[0], recv_sem=attn_sems.at[1],
            device_id=links.sibling, device_id_type=MESH,
        )

    def attn_loads():
        copies = []
        for m in range(micro):
            for r in range(rows_of):
                for side in range(2):
                    source = (attn_in, attn_there)[side]
                    half = core if side == 0 else 1 - core
                    start = (m * rows_of + r) * 2 * local + half * local
                    at = (m * rows_of + r) * 2 + side
                    copies.append(
                        pltpu.make_async_copy(source.at[m, r], attn_v.at[at_rows(start, local)], attn_sems.at[4 + at])
                    )
        return copies

    mixed_load = pltpu.make_async_copy(mixed, mixed_v, attn_sems.at[2])
    normed_load = pltpu.make_async_copy(normed, normed_v, attn_sems.at[3])

    def unit_loads(m, p, slot):
        return [
            pltpu.make_async_copy(
                qkvs[m].at[:, pl.ds(pl.multiple_of((3 * p + part) * LANES, LANES), LANES)],
                qkv_v.at[slot, part],
                load_sems.at[slot, part],
            )
            for part in range(3)
        ]

    def start_unit(u):
        p, slot = u // micro, lax.rem(u, 2)
        for m in range(micro):

            @pl.when(lax.rem(u, micro) == m)
            def _(m=m):
                for copy in unit_loads(m, p, slot):
                    copy.start()

    def res_far(u):
        p, m = u // micro, lax.rem(u, micro)
        return pltpu.make_async_remote_copy(
            src_ref=res.at[lax.rem(u, 2), at_rows((1 - plane) * plane_len, plane_len)],
            dst_ref=sums_v.at[p, m * rows_of + plane],
            send_sem=res_sems.at[0, lax.rem(u, 2)], recv_sem=res_sems.at[1, u],
            device_id=links.across, device_id_type=MESH,
        )

    def dqkv_copy(p, at):
        return pltpu.make_async_copy(
            sums_v.at[p, at], dqkv.at[at, :, pl.ds(p * wide, wide)], dqkv_sems.at[p, at]
        )

    start_unit(jnp.int32(0))
    mixed_load.start()
    normed_load.start()
    for m in range(micro):
        do_near(m).start()
    links.greet()
    for m in range(micro):
        do_far(m).start()
    attn_far().start()
    scatter = Scatter(
        links, grads, inbox, totals, mine, came, made, total, send_sems, recv_sems, near_sems, total_sems, rows
    )

    def weight_grads(group, left, right):
        for at in range(left.shape[1] // 384):
            place = slice(at * 384, (at + 1) * 384)
            made_now = dot32(left[:, place], right, TN)
            grads[group, place] = made_now.astype(grads.dtype)
        scatter.start(jnp.int32(group))

    def grads_out():
        for copy in attn_loads():
            copy.wait()
        mixed_load.wait()
        weight_grads(0, attn_v, mixed_v[...])

    def grads_pair(p):
        if p == 0:
            normed_load.wait()
        for m in range(micro):
            res_far(jnp.int32(p * micro + m)).wait_recv()
        for at in range(micro * rows_of):
            dqkv_copy(p, at).start()
        right = sums_v[p].reshape(micro * rows_of * plane_len, wide)
        weight_grads(1 + p, normed_v, right)

    per_pair = micro * steps
    work = pairs * per_pair
    begins = [4] + [per_pair * (p + 1) + 3 for p in range(pairs - 1)] + [work + 2]
    gap = max(1, 8 // far)
    last = begins[-1] + 2 * far * gap

    def item(i, carry):
        u, b = i // steps, lax.rem(i, steps)
        p, m = u // micro, lax.rem(u, micro)
        slot = lax.rem(u, 2)

        @pl.when(i == 3)
        def _():
            attn_far().wait_recv()
            for copy in attn_loads():
                copy.start()

        for group, begin in enumerate(begins):
            g = jnp.int32(group)

            @pl.when(i == begin)
            def _(group=group):
                grads_out() if group == 0 else grads_pair(group - 1)

            for step in range(1, far + 1):

                @pl.when(i == begin + (2 * step - 1) * gap)
                def _(g=g, step=step):
                    scatter.fetch(g, step)

                @pl.when(i == begin + 2 * step * gap)
                def _(g=g, step=step):
                    if step < far:
                        scatter.pass_on(g, step)
                    else:
                        scatter.close(g)

        @pl.when((i < work) & (b == 0))
        def _():
            for copy in unit_loads(0, p, slot):
                copy.wait()

            @pl.when(u + 1 < units)
            def _():
                start_unit(u + 1)

            for k in range(micro):

                @pl.when(u == k)
                def _(k=k):
                    do_near(k).wait()
                    do_far(k).wait_recv()

            @pl.when(u >= 2)
            def _():
                res_far(u - 2).wait_send()

            @pl.when(m == 0)
            def _():
                for head in range(per):
                    strip[head] = toeplitz_strip(diag_ref[p * per + head], span).T
                acc_bias[...] = jnp.zeros_like(acc_bias)

            length = len_ref[m]
            for head in range(per):
                here = lanes_k // head_dim == head
                spare = ((head + 1) % per) * head_dim
                keys[head] = with_mask_lane(qkv_v[slot, 1], lanes_k, here, spare, length)
            acc_k[...] = jnp.zeros_like(acc_k)
            acc_v[...] = jnp.zeros_like(acc_v)

        @pl.when(i < work)
        def _():
            place = at_rows(b * block, block)
            q_now = qkv_v[slot, 0, place]
            do_now = do_v[m, place, pl.ds(pl.multiple_of(p * LANES, LANES), LANES)]
            grad_query = None
            for head in range(per):
                here = lanes_q // head_dim == head
                spare = ((head + 1) % per) * head_dim
                zero = jnp.zeros_like(q_now)
                one = (lanes_q == spare).astype(q_now.dtype)
                query = jnp.where(here, q_now, zero)
                grad = jnp.where(here, do_now, zero)
                raw = dot32(keys[head], query + one, NT)
                grad_probs = dot32(qkv_v[slot, 2], grad, NT)
                parts, offsets = [], []
                for sub in range(block // LANES):
                    offset = pl.multiple_of(seq_len - LANES - (b * block + sub * LANES), LANES)
                    offsets.append(offset)
                    parts.append(raw[:, sub * LANES : (sub + 1) * LANES] + strip[head, pl.ds(offset, seq_len), :])
                scores = jnp.concatenate(parts, axis=1)
                lse = lse_ref[m * pairs * per + p * per + head, :, pl.ds(pl.multiple_of(b * block, LANES), block)]
                probs = jnp.exp(scores - lse)
                product = probs * grad_probs
                inner = jnp.sum(product, axis=0, keepdims=True)
                grad_scores = product - probs * inner
                for sub, offset in enumerate(offsets):
                    acc_bias[head, pl.ds(offset, seq_len), :] += grad_scores[:, sub * LANES : (sub + 1) * LANES]
                rounded = grad_scores.astype(jnp.bfloat16)
                acc_v[...] += dot32(probs.astype(jnp.bfloat16), grad, NN)
                acc_k[...] += dot32(rounded, query, NN)
                made_now = dot32(rounded, qkv_v[slot, 1], TN)
                grad_query = made_now if grad_query is None else jnp.where(here, made_now, grad_query)
            res[slot, place, :LANES] = grad_query.astype(res.dtype)

        @pl.when((i < work) & (b == steps - 1))
        def _():
            res[slot, :, LANES : 2 * LANES] = acc_k[...].astype(res.dtype)
            res[slot, :, 2 * LANES :] = acc_v[...].astype(res.dtype)
            res_far(u).start()
            sums_v[p, m * rows_of + plane] = res[slot, at_rows(plane * plane_len, plane_len)]

            @pl.when(m == micro - 1)
            def _():
                row = lax.broadcasted_iota(jnp.int32, (LANES, LANES), 0)
                col = lax.broadcasted_iota(jnp.int32, (LANES, LANES), 1)
                flip = (row + col == LANES - 1).astype(jnp.float32)
                for head in range(per):
                    turned = lax.dot_general(
                        flip, acc_bias[head], NT, precision=highest, preferred_element_type=jnp.float32
                    )
                    aligned = pltpu.roll(turned, 0, 1, stride=1, stride_axis=0)
                    dd_ref[p * per + head] = jnp.sum(aligned, axis=0, keepdims=True)

        return carry

    lax.fori_loop(0, last + 1, item, 0)
    scatter.total_copy(jnp.int32(pairs)).wait()
    for m in range(micro):
        do_far(m).wait_send()
    attn_far().wait_send()
    for u in range(max(0, units - 2), units):
        res_far(jnp.int32(u)).wait_send()
    for p in range(pairs):
        for at in range(micro * rows_of):
            dqkv_copy(p, at).wait()


def mix_back(qkvs, grads_mixed, attn_in, mixed, normed, lse, diag, lengths, head_dim, count, planes, block=256):
    micro, rows_of, local, depth = attn_in.shape
    seq_len, cols = qkvs[0].shape[0], qkvs[0].shape[1] // 3
    pairs, per, span = cols // LANES, LANES // head_dim, diag.shape[-1]
    tokens = normed.shape[0]
    rows, wide, far = depth // count, 3 * LANES, count // 2
    groups = 1 + pairs
    plan = (count, planes, rows, micro, rows_of, head_dim, block, pairs)
    anywhere = pl.BlockSpec(memory_space=pl.ANY)
    low, f32 = jnp.bfloat16, jnp.float32
    dma = pltpu.SemaphoreType.DMA
    return pl.pallas_call(
        functools.partial(mix_back_kernel, plan),
        in_specs=[pl.BlockSpec(memory_space=pltpu.SMEM)]
        + [pl.BlockSpec(memory_space=pltpu.VMEM)] * 2
        + [anywhere] * (2 * micro + 3),
        out_specs=[anywhere, pl.BlockSpec(memory_space=pltpu.VMEM), anywhere, anywhere],
        out_shape=[
            jax.ShapeDtypeStruct((micro * rows_of, 2 * local, 3 * cols), low),
            jax.ShapeDtypeStruct(diag.shape, f32),
            jax.ShapeDtypeStruct((groups, rows, wide), f32),
            jax.ShapeDtypeStruct(attn_in.shape, low),
        ],
        scratch_shapes=[
            pltpu.VMEM((2, 3, seq_len, LANES), low),
            pltpu.VMEM((micro, seq_len, cols), low),
            pltpu.VMEM((2, seq_len, wide), low),
            pltpu.VMEM((pairs, micro * rows_of, seq_len // 2, wide), low),
            pltpu.VMEM((tokens, depth), low),
            pltpu.VMEM((tokens, cols), low),
            pltpu.VMEM((tokens, depth), low),
            pltpu.VMEM((groups, depth, wide), low),
            pltpu.VMEM((groups, 2, far, rows, wide), low),
            pltpu.VMEM((per, span, LANES), f32),
            pltpu.VMEM((per, seq_len, LANES), low),
            pltpu.VMEM((per, span, LANES), f32),
            pltpu.VMEM((seq_len, LANES), f32),
            pltpu.VMEM((seq_len, LANES), f32),
            pltpu.VMEM((2, 2, rows, wide), low),
            pltpu.VMEM((2, 2, rows, wide), low),
            pltpu.VMEM((2, 2, rows, wide), low),
            pltpu.VMEM((rows, wide), f32),
            dma((2, 3)),
            dma((micro, 3)),
            dma((2, pairs * micro)),
            dma((4 + 2 * micro * rows_of,)),
            dma((pairs, micro * rows_of)),
            dma((groups, 2, far)),
            dma((groups, 2, far)),
            dma((2, 2, 2)),
            dma((1,)),
        ],
        compiler_params=pltpu.CompilerParams(
            collective_id=2, has_side_effects=True, vmem_limit_bytes=62 * 1024 * 1024
        ),
        name="mix_back",
    )(lengths, lse, diag, *qkvs, *grads_mixed, attn_in, mixed, normed)


class Ring:
    def __init__(self, count):
        order = ring_order(count)
        place = [0] * count
        for at, index in enumerate(order):
            place[index] = at
        self.count = count
        self.order = jnp.array(order, jnp.int32)
        self.here = jnp.array(place, jnp.int32)[lax.axis_index("dp")]
        self.ahead = [(order[i], order[(i + 1) % count]) for i in range(count)]
        self.behind = [(order[i], order[(i - 1) % count]) for i in range(count)]

    def owner(self, shift):
        return self.order[(self.here + shift) % self.count]

    def send(self, block, forward):
        return lax.ppermute(block, "dp", self.ahead if forward else self.behind)

    def gather(self, shard):
        rows, cols = shard.shape
        cut = cols // 2
        far = self.count // 2
        whole = jnp.zeros((self.count * rows, cols), shard.dtype)

        def put(whole, block, shift, column=0):
            return lax.dynamic_update_slice(whole, block, (self.owner(shift) * rows, column))

        whole = put(whole, shard, 0)
        ahead = behind = shard
        for step in range(1, far):
            ahead, behind = self.send(ahead, True), self.send(behind, False)
            whole = put(put(whole, ahead, -step), behind, step)
        last = (ahead, behind)
        ahead, behind = self.send(ahead[:, :cut], True), self.send(behind[:, cut:], False)
        whole = put(put(whole, ahead, -far), behind, far, cut)
        return whole, last

    def scatter(self, local, cols):
        cut = cols // 2
        far = self.count // 2
        most = local(self.owner(far))
        ahead, behind = self.send(most[:, :cut], True), self.send(most[:, cut:], False)
        for step in range(far - 1, 0, -1):
            mine = local(self.owner(step))
            other = local(self.owner(-step))
            if step == far - 1:
                ahead = jnp.concatenate([add_low(mine[:, :cut], ahead), mine[:, cut:]], axis=1)
                behind = jnp.concatenate([other[:, :cut], add_low(other[:, cut:], behind)], axis=1)
            else:
                ahead, behind = add_low(mine, ahead), add_low(other, behind)
            ahead, behind = self.send(ahead, True), self.send(behind, False)
        return local(self.owner(0)).astype(jnp.float32) + ahead.astype(jnp.float32) + behind.astype(jnp.float32)


def add_low(a, b):
    return (a.astype(jnp.float32) + b.astype(jnp.float32)).astype(jnp.bfloat16)


def body(
    tokens, cotangent, lengths, buckets, gain_one, gain_two, table,
    w_query, w_key, w_value, w_out, w_gate, w_up, w_down,
):
    micro, rows, local, width = tokens.shape
    seq_devices = lax.axis_size("seq")
    dp_devices = lax.axis_size("dp")
    seq_rank = lax.axis_index("seq")
    core = seq_rank % 2
    plane = seq_rank // 2
    planes = seq_devices // 2
    heads = table.shape[1]
    shard_rows, inner = w_query.shape
    head_dim = inner // heads
    half_inner = inner // 2
    hidden_units = w_gate.shape[1]
    pair_local = 2 * local
    seq_len = local * seq_devices
    first = core == 0
    core_pairs = [(i, i ^ 1) for i in range(seq_devices)]
    plane_groups = [[2 * p + c for p in range(planes)] for c in range(2)]
    ring = Ring(dp_devices)

    def swap_core(value):
        return lax.ppermute(value, "seq", core_pairs)

    def both_cores(own, other, axis):
        return jnp.concatenate([jnp.where(first, own, other), jnp.where(first, other, own)], axis=axis)

    def own_half(value, axis):
        return lax.dynamic_slice_in_dim(value, core * local, local, axis)

    def other_half(value, axis):
        return lax.dynamic_slice_in_dim(value, (1 - core) * local, local, axis)

    def core_columns(weight, split):
        low, high = weight[:, :split], weight[:, split:]
        high = jnp.pad(high, ((0, 0), (0, split - high.shape[1])))
        return jnp.where(first, low, high)

    chunk = 512
    chunks = -(-(hidden_units // 2) // chunk)
    split = chunks * chunk
    if split > hidden_units:
        split = hidden_units
    fused = planes == 2 and rows == 2 and half_inner % LANES == 0
    attn_parts = [core_columns(w, half_inner) for w in (w_query, w_key, w_value)]
    if fused:
        attn_parts = [w[:, p : p + LANES] for p in range(0, half_inner, LANES) for w in attn_parts]
    attn_shard = jnp.concatenate(attn_parts + [core_columns(w_out.T, half_inner)], axis=1)
    up_parts = [core_columns(w, split) for w in (w_gate, w_up, w_down.T)]
    chunk_shards = [
        jnp.concatenate([w[:, n * chunk : (n + 1) * chunk] for w in up_parts], axis=1) for n in range(chunks)
    ]

    small = jnp.concatenate([gain_one, gain_two, table.reshape(-1)])
    small = jnp.pad(small, (0, -small.shape[0] % LANES))
    small = jnp.pad(small[None], ((0, 15), (0, 0)))
    attn_weights, small, tokens_other, cotangent_other = gather_first(
        attn_shard, small, tokens, cotangent, dp_devices, planes
    )
    small = small.reshape(dp_devices, 16, -1)[:, 0].astype(jnp.float32)
    gain_first = small[:, :shard_rows].reshape(-1)
    gain_second = small[:, shard_rows : 2 * shard_rows].reshape(-1)
    full_table = small[:, 2 * shard_rows : 2 * shard_rows + table.size].reshape(-1, heads)
    last = attn_weights
    qkv_weights = attn_weights[:, : 3 * half_inner]
    out_own = attn_weights[:, 3 * half_inner :]
    out_other = swap_core(out_own)
    out_pair = jnp.concatenate([out_own, out_other], axis=1)

    early = min(2, chunks - 1)
    ready = []
    for shard in chunk_shards[:early]:
        shard, last = lax.optimization_barrier((shard, last))
        ready.append(lax.all_gather(shard, "dp", axis=0, tiled=True))

    tokens_pair = both_cores(tokens, tokens_other, 2)
    down_in = both_cores(cotangent, cotangent_other, 2)

    core_heads = heads // 2
    head_splits = planes // rows
    item_heads = core_heads // head_splits
    item_cols = item_heads * head_dim
    padded_cols = -(-item_cols // LANES) * LANES
    padded_heads = padded_cols // head_dim
    item_row = plane // head_splits
    item_group = plane % head_splits
    head_start = core * core_heads + item_group * item_heads
    item_table = lax.dynamic_slice_in_dim(full_table, head_start, item_heads, 1)
    item_table = jnp.pad(item_table, ((0, 0), (0, padded_heads - item_heads)))
    levels = full_table.shape[0]
    bucket_hot = (buckets[:, None] == jnp.arange(levels)[None, :]).astype(jnp.float32)
    bucket_hot = jnp.pad(bucket_hot, ((0, 1), (0, 0)))
    diag = jnp.dot(item_table.T, bucket_hot.T, precision=highest)[:, None, :]

    def to_items(value, parts):
        if planes == 2 and rows == 2:
            mine = lax.dynamic_index_in_dim(value, plane, 0, keepdims=False)
            sent = lax.dynamic_index_in_dim(value, 1 - plane, 0, keepdims=False)
            got = lax.ppermute(sent, "seq", [(i, i ^ 2) for i in range(4)])
            low = plane == 0
            return jnp.concatenate([jnp.where(low, mine, got), jnp.where(low, got, mine)], axis=0)
        value = value.reshape(rows, pair_local, parts, head_splits, item_cols)
        value = value.transpose(0, 3, 1, 2, 4).reshape(planes, pair_local, parts * item_cols)
        value = lax.all_to_all(value, "seq", 0, 0, tiled=True, axis_index_groups=plane_groups)
        value = value.reshape(seq_len, parts, item_cols)
        value = jnp.pad(value, ((0, 0), (0, 0), (0, padded_cols - item_cols)))
        return value.reshape(seq_len, parts * padded_cols)

    def from_items(values):
        parts = len(values)
        if planes == 2 and rows == 2:
            value = jnp.concatenate(values, axis=1)
            mine = lax.dynamic_slice_in_dim(value, plane * pair_local, pair_local, 0)
            sent = lax.dynamic_slice_in_dim(value, (1 - plane) * pair_local, pair_local, 0)
            got = lax.ppermute(sent, "seq", [(i, i ^ 2) for i in range(4)])
            low = plane == 0
            return jnp.stack([jnp.where(low, mine, got), jnp.where(low, got, mine)])
        value = jnp.concatenate([v[:, :item_cols] for v in values], axis=1)
        value = value.reshape(planes, pair_local, parts * item_cols)
        value = lax.all_to_all(value, "seq", 0, 0, tiled=True, axis_index_groups=plane_groups)
        value = value.reshape(rows, head_splits, pair_local, parts, item_cols).transpose(0, 2, 3, 1, 4)
        return value.reshape(rows, pair_local, parts * half_inner)

    normed, roots, qkvs, lses, mixes, resids, normed_twos, item_lens = [], [], [], [], [], [], [], []
    for step in range(micro):
        rows_in = tokens_pair[step].astype(jnp.float32)
        root = lax.rsqrt(jnp.mean(rows_in * rows_in, axis=-1, keepdims=True) + eps)
        roots.append(root)
        normed.append((rows_in * root * gain_first).astype(jnp.bfloat16))
    for step in range(micro):
        made = jnp.einsum("rld,de->rle", normed[step], qkv_weights, preferred_element_type=jnp.float32)
        qkvs.append(to_items(made.astype(jnp.bfloat16), 3))
    for step in range(micro):
        item_len = lax.dynamic_slice_in_dim(lengths[step], item_row, 1, 0)
        item_lens.append(item_len)
        mixed, lse = attend(qkvs[step], diag, item_len, head_dim, fused)
        lses.append(lse)
        mixed_own = from_items([mixed])
        mixes.append(mixed_own)
        mixed_pair = jnp.concatenate([mixed_own, swap_core(mixed_own)], axis=2)
        resid = tokens_pair[step].astype(jnp.float32) + jnp.einsum(
            "rle,de->rld", mixed_pair, out_pair, preferred_element_type=jnp.float32
        )
        root = lax.rsqrt(jnp.mean(resid * resid, axis=-1, keepdims=True) + eps)
        normed_twos.append((resid * root * gain_second).astype(jnp.bfloat16))
        resids.append(own_half(resid, 1))

    def apart(qkvs, grads_items, lses, item_lens, attn_all, mixed_all, normed_all):
        grads_qkv, diag_sum = [], 0.0
        for step in range(micro):
            grad_q, grad_k, grad_v, grad_diag = attend_back(
                qkvs[step], grads_items[step], lses[step], diag, item_lens[step], head_dim
            )
            diag_sum = diag_sum + grad_diag[:item_heads, 0]
            grads_qkv.append(from_items([grad_q, grad_k, grad_v]))
        grads_all = jnp.concatenate([flat(v) for v in grads_qkv])
        attn_all = flat(both_cores(attn_all, swap_core(attn_all), 2))
        grad_attn = jnp.einsum("td,te->de", normed_all, grads_all, preferred_element_type=jnp.float32)
        grad_o = jnp.einsum("td,te->de", attn_all, mixed_all, preferred_element_type=jnp.float32)
        both = jnp.concatenate([grad_o, grad_attn], axis=1).astype(jnp.bfloat16)
        total = ring.scatter(
            lambda index: lax.dynamic_slice_in_dim(both, index * shard_rows, shard_rows, 0), 4 * half_inner
        )
        return grads_qkv, diag_sum, total

    flat = lambda value: value.reshape(-1, value.shape[-1])
    normed_two_all = jnp.concatenate([flat(v) for v in normed_twos])
    down_all = flat(down_in)
    back_kept, back_got, out_kept, out_got, chunk_totals = feed(
        normed_two_all, down_all, ready, chunk_shards[early:], dp_devices, planes, local
    )
    back_kept, back_got, out_kept, out_got = [
        v.reshape(micro, rows, local, width).astype(jnp.float32) for v in (back_kept, back_got, out_kept, out_got)
    ]

    grad_resids, grads_mixed, attn_ins = [], [], []
    gain_two_sum = jnp.zeros((width,), jnp.float32)
    for step in range(micro):
        grad_normed = back_kept[step] + back_got[step]
        resid = resids[step]
        root = lax.rsqrt(jnp.mean(resid * resid, axis=-1, keepdims=True) + eps)
        gain_two_sum = gain_two_sum + jnp.sum(grad_normed * resid * root, axis=(0, 1))
        scaled = grad_normed * gain_second
        shared = jnp.mean(scaled * resid, axis=-1, keepdims=True) * root * root * root
        grad_resid = cotangent[step].astype(jnp.float32) + scaled * root - resid * shared
        grad_resids.append(grad_resid)
        attn_in = grad_resid.astype(jnp.bfloat16)
        attn_ins.append(attn_in)
        made_own = jnp.einsum("rld,de->rle", attn_in, out_own, preferred_element_type=jnp.float32).astype(jnp.bfloat16)
        made_other = jnp.einsum("rld,de->rle", attn_in, out_other, preferred_element_type=jnp.float32).astype(
            jnp.bfloat16
        )
        grads_mixed.append(both_cores(made_own, swap_core(made_other), 1))

    outputs = []
    for step in range(micro):
        outputs.append((resids[step] + out_kept[step] + out_got[step]).astype(jnp.bfloat16))

    normed_all = jnp.concatenate([flat(v) for v in normed])
    mixed_all = jnp.concatenate([flat(v) for v in mixes])
    attn_all = jnp.stack(attn_ins)
    if fused:
        grads_all, diag_sum, attn_totals, _ = mix_back(
            qkvs, grads_mixed, attn_all, mixed_all, normed_all, jnp.concatenate(lses), diag,
            jnp.concatenate(item_lens), head_dim, dp_devices, planes,
        )
        grads_qkv = grads_all.reshape(micro, rows, pair_local, 3 * half_inner)
        diag_sum = diag_sum[:, 0]
    else:
        grads_qkv, diag_sum, attn_totals = apart(
            qkvs, [to_items(g, 1) for g in grads_mixed], lses, item_lens, attn_all, mixed_all, normed_all
        )
    item_grad = jnp.dot(diag_sum, bucket_hot, precision=highest)
    grad_table = lax.dynamic_update_slice(jnp.zeros((heads, levels), jnp.float32), item_grad, (head_start, 0))

    input_grads = []
    gain_one_sum = jnp.zeros((width,), jnp.float32)
    for step in range(micro):
        made = jnp.einsum("rle,de->rld", other_half(grads_qkv[step], 1), qkv_weights, preferred_element_type=jnp.float32)
        got = swap_core(made.astype(jnp.bfloat16))
        kept = jnp.einsum("rle,de->rld", own_half(grads_qkv[step], 1), qkv_weights, preferred_element_type=jnp.float32)
        grad_normed = kept + got.astype(jnp.float32)
        rows_in = tokens[step].astype(jnp.float32)
        root = own_half(roots[step], 1)
        gain_one_sum = gain_one_sum + jnp.sum(grad_normed * rows_in * root, axis=(0, 1))
        scaled = grad_normed * gain_first
        shared = jnp.mean(scaled * rows_in, axis=-1, keepdims=True) * root * root * root
        input_grads.append(grad_resids[step] + scaled * root - rows_in * shared)

    def finish(total):
        if planes == 2:
            low = total.astype(jnp.bfloat16)
            got = lax.ppermute(low, "seq", [(i, i ^ 2) for i in range(4)])
            total = low.astype(jnp.float32) + got.astype(jnp.float32)
        else:
            total = lax.psum(total, "seq", axis_index_groups=plane_groups)
        return total, swap_core(total)

    def whole_columns(own, other, size):
        low, high = jnp.where(first, own, other), jnp.where(first, other, own)
        return jnp.concatenate([low, high[:, : size - low.shape[1]]], axis=1)

    own, other = finish(attn_totals)
    if fused:
        grad_out = whole_columns(own[0], other[0], inner)
        grad_query, grad_key, grad_value = [
            whole_columns(
                jnp.concatenate(list(own[1:, :, part * LANES : (part + 1) * LANES]), axis=1),
                jnp.concatenate(list(other[1:, :, part * LANES : (part + 1) * LANES]), axis=1),
                inner,
            )
            for part in range(3)
        ]
    else:
        parts = [slice(i * half_inner, (i + 1) * half_inner) for i in range(4)]
        grad_out, grad_query, grad_key, grad_value = [whole_columns(own[:, p], other[:, p], inner) for p in parts]
    done = [finish(chunk_totals[n]) for n in range(chunks)]
    parts = [slice(i * chunk, (i + 1) * chunk) for i in range(3)]
    grad_gate, grad_up, grad_down = [
        whole_columns(
            jnp.concatenate([own[:, p] for own, _ in done], axis=1),
            jnp.concatenate([other[:, p] for _, other in done], axis=1),
            hidden_units,
        )
        for p in parts
    ]

    dp_rank = lax.axis_index("dp")
    small = lax.psum(
        jnp.concatenate([gain_one_sum, gain_two_sum, grad_table.T.reshape(-1)]), ("dp", "seq")
    )
    grad_gain_one = lax.dynamic_slice_in_dim(small, dp_rank * shard_rows, shard_rows, 0)
    grad_gain_two = lax.dynamic_slice_in_dim(small, width + dp_rank * shard_rows, shard_rows, 0)
    table_part = levels // dp_devices
    grad_table = lax.dynamic_slice_in_dim(small[2 * width :].reshape(levels, heads), dp_rank * table_part, table_part, 0)

    return (
        jnp.stack(outputs), jnp.stack(input_grads), grad_gain_one, grad_gain_two, grad_table,
        grad_query, grad_key, grad_value, grad_out.T, grad_gate, grad_up, grad_down.T,
    )


def solution(mesh):
    weight, turned = P("dp", None), P(None, "dp")
    return jax.shard_map(
        body,
        mesh=mesh,
        in_specs=(
            P(None, "dp", "seq", None), P(None, "dp", "seq", None), P(None, "dp"), P(), P("dp"), P("dp"),
            weight, weight, weight, weight, turned, weight, weight, turned,
        ),
        out_specs=(
            P(None, "dp", "seq", None), P(None, "dp", "seq", None), P("dp"), P("dp"),
            weight, weight, weight, weight, turned, weight, weight, turned,
        ),
        check_vma=False,
    )
```

```python
import functools

import jax
import jax.numpy as jnp
from jax import lax
from jax.experimental import pallas as pl
from jax.experimental.pallas import tpu as pltpu
from jax.sharding import PartitionSpec as P

eps = 1e-06
masked_value = -1e30
highest = lax.Precision.HIGHEST
gelu_scale = 0.7978845608028654
gelu_cubic = 0.044715
LANES = 128
VMEM_LIMIT = 56 * 1024 * 1024
NT = (((1,), (1,)), ((), ()))
NN = (((1,), (0,)), ((), ()))
TN = (((0,), (0,)), ((), ()))


def dot32(a, b, dims):
    return lax.dot_general(a, b, dims, preferred_element_type=jnp.float32)


def toeplitz_strip(diag_row, span):
    wide = jnp.broadcast_to(diag_row, (LANES, span))
    return pltpu.roll(wide, span - (LANES - 1), 1, stride=1, stride_axis=0)


def with_mask_lane(key_pair, lanes, here, spare, length):
    rows = lax.broadcasted_iota(jnp.int32, key_pair.shape, 0)
    mask = jnp.where(rows < length, 0.0, masked_value).astype(key_pair.dtype)
    zero = jnp.zeros_like(key_pair)
    return jnp.where(here, key_pair, jnp.where(lanes == spare, mask, zero))


def attend_kernel(head_dim, block, len_ref, diag_ref, q_ref, k_ref, v_ref, mixed_ref, lse_ref, strip, keys):
    step = pl.program_id(1)
    seq_len = k_ref.shape[0]
    span = diag_ref.shape[-1]
    length = len_ref[0]
    per = LANES // head_dim
    lanes_k = lax.broadcasted_iota(jnp.int32, (seq_len, LANES), 1)
    lanes_q = lax.broadcasted_iota(jnp.int32, (block, LANES), 1)

    @pl.when(step == 0)
    def _():
        for head in range(per):
            strip[head] = toeplitz_strip(diag_ref[head], span)
            here = lanes_k // head_dim == head
            spare = ((head + 1) % per) * head_dim
            keys[head] = with_mask_lane(k_ref[...], lanes_k, here, spare, length)

    mixed = None
    for head in range(per):
        here = lanes_q // head_dim == head
        spare = ((head + 1) % per) * head_dim
        one = (lanes_q == spare).astype(q_ref.dtype)
        query = jnp.where(here, q_ref[...], one)
        raw = dot32(query, keys[head], NT)
        parts = []
        for sub in range(block // LANES):
            offset = seq_len - LANES - (step * block + sub * LANES)
            offset = pl.multiple_of(offset, LANES)
            parts.append(raw[sub * LANES : (sub + 1) * LANES] + strip[head, :, pl.ds(offset, seq_len)])
        scores = jnp.concatenate(parts, axis=0)
        top = jnp.max(scores, axis=1, keepdims=True)
        expo = jnp.exp(scores - top)
        total = jnp.sum(expo, axis=1, keepdims=True)
        made = dot32(expo.astype(jnp.bfloat16), v_ref[...], NN) / total
        mixed = made if mixed is None else jnp.where(here, made, mixed)
        lse = jnp.broadcast_to(top + jnp.log(total), (block, LANES))
        lse_ref[head] = lse.T[:1]
    mixed_ref[...] = mixed.astype(mixed_ref.dtype)


def attend(qkv, diag, length, head_dim, by_pair=False, block=256):
    seq_len, cols = qkv.shape[0], qkv.shape[1] // 3
    pairs = cols // LANES
    per = LANES // head_dim
    span = diag.shape[-1]
    at = (lambda part, p: 3 * p + part) if by_pair else (lambda part, p: part * pairs + p)
    flops = 2 * 2 * seq_len * seq_len * LANES * 2 * cols // head_dim
    return pl.pallas_call(
        functools.partial(attend_kernel, head_dim, block),
        grid=(pairs, seq_len // block),
        in_specs=[
            pl.BlockSpec(memory_space=pltpu.SMEM),
            pl.BlockSpec((per, 1, span), lambda p, b: (p, 0, 0)),
            pl.BlockSpec((block, LANES), lambda p, b: (b, at(0, p))),
            pl.BlockSpec((seq_len, LANES), lambda p, b: (0, at(1, p))),
            pl.BlockSpec((seq_len, LANES), lambda p, b: (0, at(2, p))),
        ],
        out_specs=[
            pl.BlockSpec((block, LANES), lambda p, b: (b, p)),
            pl.BlockSpec((per, 1, block), lambda p, b: (p, 0, b)),
        ],
        out_shape=[
            jax.ShapeDtypeStruct((seq_len, cols), jnp.bfloat16),
            jax.ShapeDtypeStruct((cols // head_dim, 1, seq_len), jnp.float32),
        ],
        scratch_shapes=[
            pltpu.VMEM((per, LANES, span), jnp.float32),
            pltpu.VMEM((per, seq_len, LANES), jnp.bfloat16),
        ],
        compiler_params=pltpu.CompilerParams(vmem_limit_bytes=VMEM_LIMIT),
        cost_estimate=pl.CostEstimate(flops=flops, bytes_accessed=8 * seq_len * cols, transcendentals=0),
        name="attend",
    )(length, diag, qkv, qkv, qkv)


def attend_back_kernel(
    head_dim, block, len_ref, diag_ref, q_ref, k_ref, v_ref, do_ref, lse_ref,
    dq_ref, dk_ref, dv_ref, dd_ref, strip, keys, acc_bias, acc_k, acc_v,
):
    step = pl.program_id(1)
    steps = pl.num_programs(1)
    seq_len = k_ref.shape[0]
    span = diag_ref.shape[-1]
    length = len_ref[0]
    per = LANES // head_dim
    lanes_k = lax.broadcasted_iota(jnp.int32, (seq_len, LANES), 1)
    lanes_q = lax.broadcasted_iota(jnp.int32, (block, LANES), 1)
    subs = block // LANES

    @pl.when(step == 0)
    def _():
        for head in range(per):
            strip[head] = toeplitz_strip(diag_ref[head], span).T
            here = lanes_k // head_dim == head
            spare = ((head + 1) % per) * head_dim
            keys[head] = with_mask_lane(k_ref[...], lanes_k, here, spare, length)
        acc_bias[...] = jnp.zeros_like(acc_bias)
        acc_k[...] = jnp.zeros_like(acc_k)
        acc_v[...] = jnp.zeros_like(acc_v)

    grad_query = None
    for head in range(per):
        here = lanes_q // head_dim == head
        spare = ((head + 1) % per) * head_dim
        zero = jnp.zeros_like(q_ref[...])
        one = (lanes_q == spare).astype(q_ref.dtype)
        query = jnp.where(here, q_ref[...], zero)
        grad = jnp.where(here, do_ref[...], zero)
        raw = dot32(keys[head], query + one, NT)
        grad_probs = dot32(v_ref[...], grad, NT)
        parts = []
        offsets = []
        for sub in range(subs):
            offset = seq_len - LANES - (step * block + sub * LANES)
            offset = pl.multiple_of(offset, LANES)
            offsets.append(offset)
            parts.append(raw[:, sub * LANES : (sub + 1) * LANES] + strip[head, pl.ds(offset, seq_len), :])
        scores = jnp.concatenate(parts, axis=1)
        probs = jnp.exp(scores - lse_ref[head])
        product = probs * grad_probs
        inner = jnp.sum(product, axis=0, keepdims=True)
        grad_scores = product - probs * inner
        for sub in range(subs):
            rows = pl.ds(offsets[sub], seq_len)
            acc_bias[head, rows, :] += grad_scores[:, sub * LANES : (sub + 1) * LANES]
        rounded = grad_scores.astype(jnp.bfloat16)
        acc_v[...] += dot32(probs.astype(jnp.bfloat16), grad, NN)
        acc_k[...] += dot32(rounded, query, NN)
        made = dot32(rounded, k_ref[...], TN)
        grad_query = made if grad_query is None else jnp.where(here, made, grad_query)
    dq_ref[...] = grad_query.astype(dq_ref.dtype)

    @pl.when(step == steps - 1)
    def _():
        dk_ref[...] = acc_k[...].astype(dk_ref.dtype)
        dv_ref[...] = acc_v[...].astype(dv_ref.dtype)
        row = lax.broadcasted_iota(jnp.int32, (LANES, LANES), 0)
        col = lax.broadcasted_iota(jnp.int32, (LANES, LANES), 1)
        flip = (row + col == LANES - 1).astype(jnp.float32)
        for head in range(per):
            turned = lax.dot_general(
                flip, acc_bias[head], NT, precision=lax.Precision.HIGHEST, preferred_element_type=jnp.float32
            )
            aligned = pltpu.roll(turned, 0, 1, stride=1, stride_axis=0)
            dd_ref[head] = jnp.sum(aligned, axis=0, keepdims=True)


def attend_back(qkv, grad_mixed, lse, diag, length, head_dim, block=256):
    seq_len, cols = qkv.shape[0], qkv.shape[1] // 3
    pairs = cols // LANES
    per = LANES // head_dim
    span = diag.shape[-1]
    flops = 5 * 2 * seq_len * seq_len * LANES * 2 * cols // head_dim
    whole = lambda p, b: (0, p)
    part = lambda p, b: (b, p)
    flat = jax.ShapeDtypeStruct((seq_len, cols), jnp.bfloat16)
    return pl.pallas_call(
        functools.partial(attend_back_kernel, head_dim, block),
        grid=(pairs, seq_len // block),
        in_specs=[
            pl.BlockSpec(memory_space=pltpu.SMEM),
            pl.BlockSpec((per, 1, span), lambda p, b: (p, 0, 0)),
            pl.BlockSpec((block, LANES), part),
            pl.BlockSpec((seq_len, LANES), lambda p, b: (0, pairs + p)),
            pl.BlockSpec((seq_len, LANES), lambda p, b: (0, 2 * pairs + p)),
            pl.BlockSpec((block, LANES), part),
            pl.BlockSpec((per, 1, block), lambda p, b: (p, 0, b)),
        ],
        out_specs=[
            pl.BlockSpec((block, LANES), part),
            pl.BlockSpec((seq_len, LANES), whole),
            pl.BlockSpec((seq_len, LANES), whole),
            pl.BlockSpec((per, 1, span), lambda p, b: (p, 0, 0)),
        ],
        out_shape=[flat, flat, flat, jax.ShapeDtypeStruct(diag.shape, jnp.float32)],
        scratch_shapes=[
            pltpu.VMEM((per, span, LANES), jnp.float32),
            pltpu.VMEM((per, seq_len, LANES), jnp.bfloat16),
            pltpu.VMEM((per, span, LANES), jnp.float32),
            pltpu.VMEM((seq_len, LANES), jnp.float32),
            pltpu.VMEM((seq_len, LANES), jnp.float32),
        ],
        compiler_params=pltpu.CompilerParams(vmem_limit_bytes=VMEM_LIMIT),
        cost_estimate=pl.CostEstimate(flops=flops, bytes_accessed=16 * seq_len * cols, transcendentals=0),
        name="attend_back",
    )(length, diag, qkv, qkv, qkv, grad_mixed, lse)


def gated_values(gate, up, grad):
    square = gate * gate
    turn = jnp.tanh(gelu_scale * gate * (1.0 + gelu_cubic * square))
    half = 0.5 * (1.0 + turn)
    act = gate * half
    slope = half + 0.5 * gate * (1.0 - turn * turn) * gelu_scale * (1.0 + 3.0 * gelu_cubic * square)
    low = jnp.bfloat16
    return (grad * up * slope).astype(low), (grad * act).astype(low), (act * up).astype(low)


def ring_order(count):
    if count % 4 or count < 8:
        return list(range(count))
    long, short = 4, count // 4
    walk = []
    for line in range(long):
        columns = range(1, short) if line % 2 == 0 else range(short - 1, 0, -1)
        walk += [line * short + column for column in columns]
    return walk + [line * short for line in range(long - 1, -1, -1)]


MESH = pl.DeviceIdType.MESH


def pick(options, at):
    value = jnp.int32(options[0])
    for index in range(1, len(options)):
        value = jnp.where(at == index, jnp.int32(options[index]), value)
    return value


class Links:
    def __init__(self, count, planes):
        order = ring_order(count)
        place = [0] * count
        for at, index in enumerate(order):
            place[index] = at
        self.count, self.order, self.planes = count, order, planes
        self.place = pick(place, lax.axis_index("dp"))
        seq = lax.axis_index("seq")
        self.core = seq % 2
        self.plane = seq // 2
        self.sibling = {"seq": self.plane * 2 + 1 - self.core}
        self.across = {"seq": (1 - self.plane) * 2 + self.core}
        self.diagonal = {"seq": (1 - self.plane) * 2 + 1 - self.core}
        self.ahead = {"dp": self.owner(1)}
        self.behind = {"dp": self.owner(-1)}

    def owner(self, shift):
        return pick(self.order, lax.rem(self.place + shift + self.count, self.count))

    def greet(self, diagonal=False):
        barrier = pltpu.get_barrier_semaphore()
        friends = [self.ahead, self.behind, self.sibling] + ([self.across] if self.planes == 2 else [])
        if diagonal:
            friends.append(self.diagonal)
        for friend in friends:
            pl.semaphore_signal(barrier, inc=1, device_id=friend, device_id_type=MESH)
        pl.semaphore_wait(barrier, len(friends))


class Gather:
    def __init__(self, links, shard, whole, sems, rows):
        self.links, self.shard, self.whole, self.sems, self.rows = links, shard, whole, sems, rows
        self.far = links.count // 2
        self.shared = links.planes == 2
        self.third = rows // 3
        self.size = 2 * self.third if self.shared else rows
        self.cut = -(-(self.size // 2) // 16) * 16

    def base(self, shift):
        start = self.links.owner(shift) * self.rows
        if self.shared:
            start = start + self.links.plane * self.third
        return pl.multiple_of(start, 16)

    def ring_copy(self, step, forward):
        shift = (1 - step) if forward else (step - 1)
        offset, size = 0, self.size
        if step == self.far:
            offset, size = (0, self.cut) if forward else (self.cut, self.size - self.cut)
        place = self.whole.at[pl.ds(pl.multiple_of(self.base(shift) + offset, 16), size)]
        source = place
        if step == 1:
            first = self.links.plane * self.third if self.shared else 0
            source = self.shard.at[pl.ds(pl.multiple_of(first + offset, 16), size)]
        return pltpu.make_async_remote_copy(
            src_ref=source,
            dst_ref=place,
            send_sem=self.sems.at[0 if forward else 1, step],
            recv_sem=self.sems.at[2 if forward else 3, step],
            device_id=self.links.ahead if forward else self.links.behind,
            device_id_type=MESH,
        )

    def recv_copy(self, step, forward):
        shift = -step if forward else step
        offset, size = 0, self.size
        if step == self.far:
            offset, size = (0, self.cut) if forward else (self.cut, self.size - self.cut)
        place = self.whole.at[pl.ds(pl.multiple_of(self.base(shift) + offset, 16), size)]
        return pltpu.make_async_remote_copy(
            src_ref=place,
            dst_ref=place,
            send_sem=self.sems.at[0 if forward else 1, step],
            recv_sem=self.sems.at[2 if forward else 3, step],
            device_id=self.links.ahead if forward else self.links.behind,
            device_id_type=MESH,
        )

    def across_copy(self, slot, shift, receive):
        plane = 1 - self.links.plane if receive else self.links.plane
        start = self.links.owner(shift) * self.rows + plane * 2 * self.third
        place = self.whole.at[pl.ds(pl.multiple_of(start, 16), self.third)]
        return pltpu.make_async_remote_copy(
            src_ref=place,
            dst_ref=place,
            send_sem=self.sems.at[4, slot],
            recv_sem=self.sems.at[5, slot],
            device_id=self.links.across,
            device_id_type=MESH,
        )

    def start(self):
        self.ring_copy(1, True).start()
        self.ring_copy(1, False).start()

    def advance(self, step):
        last = step == self.far
        for forward in (True, False):
            self.recv_copy(step, forward).wait_recv()
            if not last:
                self.ring_copy(step + 1, forward).start()
            if self.shared and not last:
                slot = 2 * step - 2 + (0 if forward else 1)
                self.across_copy(slot, -step if forward else step, False).start()
        if self.shared and last:
            self.across_copy(2 * step - 2, step, False).start()

    def slots(self):
        shifts = []
        for step in range(1, self.far):
            shifts += [(2 * step - 2, -step), (2 * step - 1, step)]
        return shifts + [(2 * self.far - 2, self.far)]

    def finish(self):
        for step in range(1, self.far + 1):
            self.ring_copy(step, True).wait_send()
            self.ring_copy(step, False).wait_send()
        if self.shared:
            for slot, shift in self.slots():
                self.across_copy(slot, shift, False).wait_send()
                self.across_copy(slot, shift, True).wait_recv()


def gather_kernel(count, planes, rows, shard, small, tokens, cotangent, whole, smalls, tokens_there, cotangent_there, sems, sems_small, sems_core, own):
    links = Links(count, planes)
    keep = pltpu.make_async_copy(shard, whole.at[pl.ds(pl.multiple_of(links.owner(0) * rows, 16), rows)], own.at[0])
    keep_small = pltpu.make_async_copy(small, smalls.at[pl.ds(pl.multiple_of(links.owner(0) * 16, 16), 16)], own.at[1])
    keep.start()
    keep_small.start()
    links.greet()
    large = Gather(links, shard, whole, sems, rows)
    little = SmallGather(links, small, smalls, sems_small)
    little.start()
    large.start()
    swaps = []
    for at, (source, target) in enumerate(((tokens, tokens_there), (cotangent, cotangent_there))):
        swaps.append(
            pltpu.make_async_remote_copy(
                src_ref=source, dst_ref=target, send_sem=sems_core.at[at, 0], recv_sem=sems_core.at[at, 1],
                device_id=links.sibling, device_id_type=MESH,
            )
        )
        swaps[-1].start()
    for step in range(1, large.far + 1):
        little.advance(step)
        large.advance(step)
    for swap in swaps:
        swap.wait()
    little.finish()
    large.finish()
    keep.wait()
    keep_small.wait()


class SmallGather(Gather):
    def __init__(self, links, shard, whole, sems):
        self.links, self.shard, self.whole, self.sems, self.rows = links, shard, whole, sems, 16
        self.far, self.shared, self.size, self.cut = links.count // 2, False, 16, 16

    def start(self):
        self.ring_copy(1, True).start()
        self.ring_copy(1, False).start()

    def advance(self, step):
        self.recv_copy(step, True).wait_recv()
        if step < self.far:
            self.ring_copy(step + 1, True).start()
            self.recv_copy(step, False).wait_recv()
            if step + 1 < self.far:
                self.ring_copy(step + 1, False).start()

    def finish(self):
        for step in range(1, self.far + 1):
            self.ring_copy(step, True).wait_send()
            if step < self.far:
                self.ring_copy(step, False).wait_send()


def gather_first(shard, small, tokens, cotangent, count, planes):
    rows, cols = shard.shape
    anywhere = pl.BlockSpec(memory_space=pl.ANY)
    return pl.pallas_call(
        functools.partial(gather_kernel, count, planes, rows),
        in_specs=[anywhere] * 4,
        out_specs=[anywhere] * 4,
        out_shape=[
            jax.ShapeDtypeStruct((count * rows, cols), shard.dtype),
            jax.ShapeDtypeStruct((count * 16, small.shape[1]), small.dtype),
            jax.ShapeDtypeStruct(tokens.shape, tokens.dtype),
            jax.ShapeDtypeStruct(cotangent.shape, cotangent.dtype),
        ],
        scratch_shapes=[
            pltpu.SemaphoreType.DMA((6, count)),
            pltpu.SemaphoreType.DMA((4, count)),
            pltpu.SemaphoreType.DMA((2, 2)),
            pltpu.SemaphoreType.DMA((2,)),
        ],
        compiler_params=pltpu.CompilerParams(collective_id=0, has_side_effects=True),
        name="gather_first",
    )(shard, small, tokens, cotangent)


class Scatter:
    def __init__(self, links, grads, inbox, totals, mine, came, made, total, send_sems, recv_sems, near_sems, total_sems, rows):
        self.links, self.grads, self.inbox, self.totals = links, grads, inbox, totals
        self.mine, self.came, self.made, self.total = mine, came, made, total
        self.send_sems, self.recv_sems, self.near_sems, self.total_sems = send_sems, recv_sems, near_sems, total_sems
        self.rows = rows
        self.far = links.count // 2
        self.cut = -(-(rows // 2) // 16) * 16
        self.spaces = made.shape[0]

    def part(self, step, way):
        if step > 1:
            return 0, self.rows
        return (0, self.cut) if way == 0 else (self.cut, self.rows - self.cut)

    def term(self, chunk, shift, offset, size):
        start = self.links.owner(shift) * self.rows + offset
        return self.grads.at[chunk, pl.ds(pl.multiple_of(start, 16), size)]

    def hop(self, chunk, step, way):
        offset, size = self.part(step, way)
        if step == 1:
            source = self.term(chunk, self.far, offset, size)
        else:
            source = self.made.at[lax.rem(chunk, self.spaces), way, pl.ds(offset, size)]
        return pltpu.make_async_remote_copy(
            src_ref=source,
            dst_ref=self.inbox.at[chunk, way, step - 1, pl.ds(offset, size)],
            send_sem=self.send_sems.at[chunk, way, step - 1],
            recv_sem=self.recv_sems.at[chunk, way, step - 1],
            device_id=self.links.behind if way else self.links.ahead,
            device_id_type=MESH,
        )

    def near(self, chunk, step, way):
        offset, size = self.part(step, way)
        space = lax.rem(chunk, self.spaces)
        shift = (step - self.far) if way else (self.far - step)
        copies = [
            pltpu.make_async_copy(
                self.inbox.at[chunk, way, step - 1, pl.ds(offset, size)],
                self.came.at[space, way, pl.ds(offset, size)],
                self.near_sems.at[space, way, 0],
            )
        ]
        if step < self.far or way == 0:
            copies.append(
                pltpu.make_async_copy(
                    self.term(chunk, shift, 0, self.rows), self.mine.at[space, way], self.near_sems.at[space, way, 1]
                )
            )
        return copies

    def start(self, chunk):
        for way in range(2):
            self.hop(chunk, 1, way).start()

    def fetch(self, chunk, step):
        for way in range(2):
            self.hop(chunk, step, way).wait_recv()
            for copy in self.near(chunk, step, way):
                copy.start()

    def pass_on(self, chunk, step):
        space = lax.rem(chunk, self.spaces)
        for way in range(2):
            for copy in self.near(chunk, step, way):
                copy.wait()
            self.hop(chunk, step, way).wait_send()
            offset, size = self.part(step, way)
            rows = pl.ds(offset, size)
            if size < self.rows:
                other = pl.ds(0 if way else size, self.rows - size)
                self.made[space, way, other] = self.mine[space, way, other]
            self.made[space, way, rows] = add_low(self.mine[space, way, rows], self.came[space, way, rows])
            self.hop(chunk, step + 1, way).start()

    def total_copy(self, chunk):
        return pltpu.make_async_copy(self.total, self.totals.at[chunk], self.total_sems.at[0])

    def close(self, chunk):
        space = lax.rem(chunk, self.spaces)
        for way in range(2):
            for copy in self.near(chunk, self.far, way):
                copy.wait()
            self.hop(chunk, self.far, way).wait_send()

        @pl.when(chunk > 0)
        def _():
            self.total_copy(chunk - 1).wait()

        total = self.mine[space, 0].astype(jnp.float32) + self.came[space, 0].astype(jnp.float32)
        self.total[...] = total + self.came[space, 1].astype(jnp.float32)
        self.total_copy(chunk).start()


def feed_kernel(plan, *refs):
    count, planes, rows, chunks, early, tile, block, groups = plan
    late = chunks - early
    (normed, down, *rest) = refs
    ready, shards = rest[:early], rest[early:chunks]
    rest = rest[chunks:]
    back_kept, back_got, out_kept, out_got, totals, pieces, grads, inbox = rest[:8]
    wholes = rest[8 : 8 + late]
    (
        a_all, b_all, weights, piece, stage, mine, came, made, total, out_stage,
        in_sems, piece_sems, stage_sems, fetch_sems, keep_sems, give_sems, take_sems,
        send_sems, recv_sems, near_sems, total_sems, own_sems, *gather_sems,
    ) = rest[8 + late :]
    tokens, depth = a_all.shape
    width = weights.shape[2] // 3
    tiles, blocks = tokens // tile, depth // block
    per = tiles + blocks
    front = chunks * per
    links = Links(count, planes)
    far = count // 2

    loads = [pltpu.make_async_copy(normed, a_all, in_sems.at[chunks]), pltpu.make_async_copy(down, b_all, in_sems.at[chunks + 1])]
    loads += [pltpu.make_async_copy(ready[n], weights.at[n], in_sems.at[n]) for n in range(early)]
    keeps = []
    for n in range(late):
        place = wholes[n].at[pl.ds(pl.multiple_of(links.owner(0) * rows, 16), rows)]
        keeps.append(pltpu.make_async_copy(shards[n], place, own_sems.at[n]))
    for copy in loads + keeps:
        copy.start()
    links.greet()
    gathers = [Gather(links, shards[n], wholes[n], gather_sems[n], rows) for n in range(late)]
    scatter = Scatter(
        links, grads, inbox, totals, mine, came, made, total, send_sems, recv_sems, near_sems, total_sems, rows
    )
    loads[0].wait()
    loads[1].wait()

    gap_gather = max(1, 16 // far)
    gap = max(2, 20 // far)

    def load_weights(n):
        source = ready[n] if n < early else wholes[n - early]
        return pltpu.make_async_copy(source, weights.at[n], in_sems.at[n])

    def piece_copy(n, t):
        place = pl.ds(pl.multiple_of(t * tile, 16), tile)
        return pltpu.make_async_copy(piece.at[place], pieces.at[n, place], piece_sems.at[t])

    def stage_copy(n, b):
        slot = lax.rem(b, 2)
        place = pl.ds(pl.multiple_of(b * block, 16), block)
        return pltpu.make_async_copy(stage.at[slot], grads.at[n, place], stage_sems.at[slot])

    def back_rows(g, half):
        start = (2 * g + half) * tile
        return pl.ds(pl.multiple_of(start, 16), tile)

    def fetch_copy(n, t):
        half = jnp.where(lax.rem(t, 2) == 0, 1 - links.core, links.core)
        slot = lax.rem(t, 2)
        target = pl.ds(pl.multiple_of((slot * chunks + n) * tile, 16), tile)
        return pltpu.make_async_copy(pieces.at[n, back_rows(t // 2, half)], piece.at[target], fetch_sems.at[slot, n])

    def give_copy(kind, g):
        target = (back_got, out_got)[kind]
        return pltpu.make_async_remote_copy(
            src_ref=out_stage.at[kind, 0], dst_ref=target.at[g], send_sem=give_sems.at[kind], recv_sem=take_sems.at[kind, g],
            device_id=links.sibling, device_id_type=MESH,
        )

    def keep_copy(kind, g):
        target = (back_kept, out_kept)[kind]
        return pltpu.make_async_copy(out_stage.at[kind, 1], target.at[g], keep_sems.at[kind])

    items_back = 4 * groups
    last_event = front + 1 + gap * far
    total_items = max(front + items_back, last_event + 1)

    def item(i, carry):
        n, j = i // per, lax.rem(i, per)

        for k in range(late):
            base = k * per
            for step in range(far + 2):

                @pl.when(i == base + step * gap_gather)
                def _(k=k, step=step):
                    if step == 0:
                        gathers[k].start()
                    elif step <= far:
                        gathers[k].advance(step)
                    else:
                        gathers[k].finish()
                        keeps[k].wait()
                        load_weights(early + k).start()

        def event(offset, act):
            past = i - per - offset

            @pl.when((past >= 0) & (past < front) & (lax.rem(past + per * 64, per) == 0))
            def _():
                act(past // per)

        def begin(chunk):
            for b in (blocks - 2, blocks - 1):
                stage_copy(chunk, b).wait()
            scatter.start(chunk)

        event(0, begin)
        for step in range(1, far + 1):
            event(step * gap - 1, lambda chunk, step=step: scatter.fetch(chunk, step))
            if step < far:
                event(step * gap, lambda chunk, step=step: scatter.pass_on(chunk, step))
            else:
                event(step * gap, scatter.close)

        @pl.when((i < front) & (j == 0))
        def _():
            for m in range(chunks):

                @pl.when(n == m)
                def _(m=m):
                    load_weights(m).wait()

        @pl.when((i < front) & (j < tiles))
        def _():
            @pl.when(n > 0)
            def _():
                piece_copy(n - 1, j).wait()

            place = pl.ds(pl.multiple_of(j * tile, 16), tile)
            a, d = a_all[place], b_all[place]
            gate = dot32(a, weights[n, :, :width], NN)
            up = dot32(a, weights[n, :, width : 2 * width], NN)
            grad = dot32(d, weights[n, :, 2 * width :], NN)
            d_gate, d_up, hidden = gated_values(gate, up, grad)
            piece[place, :width] = d_gate
            piece[place, width : 2 * width] = d_up
            piece[place, 2 * width :] = hidden
            piece_copy(n, j).start()

        @pl.when((i < front) & (j >= tiles))
        def _():
            b = j - tiles

            @pl.when(b >= 2)
            def _():
                stage_copy(n, b - 2).wait()

            place = pl.ds(pl.multiple_of(b * block, LANES), block)
            slot = lax.rem(b, 2)
            first = dot32(a_all[:, place], piece[:, : 2 * width], TN)
            stage[slot, :, : 2 * width] = first.astype(stage.dtype)
            second = dot32(b_all[:, place], piece[:, 2 * width :], TN)
            stage[slot, :, 2 * width :] = second.astype(stage.dtype)
            stage_copy(n, b).start()

        @pl.when(i == front)
        def _():
            for t in range(tiles):
                piece_copy(chunks - 1, t).wait()
            for m in range(chunks):
                fetch_copy(m, 0).start()

        at = i - front
        t, kind_at = at // 2, lax.rem(at + 2 * per, 2)
        for kind in range(2):

            @pl.when((at >= 0) & (at < items_back) & (kind_at == kind))
            def _(kind=kind):
                slot, g = lax.rem(t, 2), t // 2
                if kind == 0:
                    for m in range(chunks):
                        fetch_copy(m, t).wait()

                    @pl.when(t + 1 < 2 * groups)
                    def _():
                        for m in range(chunks):
                            fetch_copy(m, t + 1).start()

                columns = slice(0, 2 * width) if kind == 0 else slice(2 * width, 3 * width)
                made_sum = None
                for m in range(chunks):
                    place = pl.ds(pl.multiple_of((slot * chunks + m) * tile, 16), tile)
                    term = dot32(piece[place, columns], weights[m, :, columns], NT)
                    made_sum = term if made_sum is None else made_sum + term

                @pl.when((t >= 2) & (slot == 0))
                def _():
                    give_copy(kind, g - 1).wait_send()

                @pl.when((t >= 2) & (slot == 1))
                def _():
                    keep_copy(kind, g - 1).wait()

                out_stage[kind, slot] = made_sum.astype(out_stage.dtype)

                @pl.when(slot == 0)
                def _():
                    give_copy(kind, g).start()

                @pl.when(slot == 1)
                def _():
                    keep_copy(kind, g).start()

        return carry

    lax.fori_loop(0, total_items, item, 0)
    scatter.total_copy(chunks - 1).wait()
    for kind in range(2):
        give_copy(kind, groups - 1).wait_send()
        keep_copy(kind, groups - 1).wait()
        for g in range(groups):
            give_copy(kind, g).wait_recv()


def feed(normed, down, ready, shards, count, planes, tile):
    tokens, depth = normed.shape
    rows, cols = shards[0].shape
    early, chunks = len(ready), len(ready) + len(shards)
    far = count // 2
    block = 384
    groups = tokens // (2 * tile)
    spaces = 2 if far <= 4 else chunks
    plan = (count, planes, rows, chunks, early, tile, block, groups)
    anywhere = pl.BlockSpec(memory_space=pl.ANY)
    low, wide = jnp.bfloat16, jnp.float32
    part = jax.ShapeDtypeStruct((groups, tile, depth), low)
    shapes = [part] * 4 + [
        jax.ShapeDtypeStruct((chunks, rows, cols), wide),
        jax.ShapeDtypeStruct((chunks, tokens, cols), low),
        jax.ShapeDtypeStruct((chunks, depth, cols), low),
        jax.ShapeDtypeStruct((chunks, 2, far, rows, cols), low),
    ]
    shapes += [jax.ShapeDtypeStruct((depth, cols), low)] * len(shards)
    dma = pltpu.SemaphoreType.DMA
    made = pl.pallas_call(
        functools.partial(feed_kernel, plan),
        in_specs=[anywhere] * (2 + chunks),
        out_specs=[anywhere] * len(shapes),
        out_shape=shapes,
        scratch_shapes=[
            pltpu.VMEM((tokens, depth), low),
            pltpu.VMEM((tokens, depth), low),
            pltpu.VMEM((chunks, depth, cols), low),
            pltpu.VMEM((tokens, cols), low),
            pltpu.VMEM((2, block, cols), low),
            pltpu.VMEM((spaces, 2, rows, cols), low),
            pltpu.VMEM((spaces, 2, rows, cols), low),
            pltpu.VMEM((spaces, 2, rows, cols), low),
            pltpu.VMEM((rows, cols), wide),
            pltpu.VMEM((2, 2, tile, depth), low),
            dma((chunks + 2,)),
            dma((tokens // tile,)),
            dma((2,)),
            dma((2, chunks)),
            dma((2,)),
            dma((2,)),
            dma((2, groups)),
            dma((chunks, 2, far)),
            dma((chunks, 2, far)),
            dma((spaces, 2, 2)),
            dma((1,)),
            dma((len(shards),)),
        ]
        + [dma((6, count))] * len(shards),
        compiler_params=pltpu.CompilerParams(
            collective_id=1, has_side_effects=True, vmem_limit_bytes=62 * 1024 * 1024
        ),
        cost_estimate=pl.CostEstimate(
            flops=18 * tokens * depth * cols // 3 * chunks, bytes_accessed=10 * tokens * depth, transcendentals=0
        ),
        name="feed",
    )(normed, down, *ready, *shards)
    return made[:5]


def mix_back_kernel(plan, len_ref, lse_ref, diag_ref, *refs):
    count, planes, rows, micro, rows_of, head_dim, block, pairs = plan
    qkvs = refs[:micro]
    made_own, made_other, attn_in, mixed, normed = refs[micro : micro + 5]
    dqkv_own, dqkv_there, dd_ref, totals, attn_there = refs[micro + 5 : micro + 10]
    (
        qkv_v, do_v, res, sums_v, attn_v, mixed_v, normed_v, grads, inbox,
        strip, keys, acc_bias, acc_k, acc_v, mine, came, made, total,
        load_sems, do_sems, res_sems, attn_sems, dqkv_sems, send_sems, recv_sems, near_sems, total_sems,
    ) = refs[micro + 10 :]
    seq_len = do_v.shape[1]
    span = diag_ref.shape[-1]
    plane_len = seq_len // 2
    local = attn_in.shape[1]
    steps = seq_len // block
    per = LANES // head_dim
    wide = 3 * LANES
    units = pairs * micro
    links = Links(count, planes)
    far = count // 2
    plane, core = links.plane, links.core
    lanes_k = lax.broadcasted_iota(jnp.int32, (seq_len, LANES), 1)
    lanes_q = lax.broadcasted_iota(jnp.int32, (block, LANES), 1)

    def at_rows(start, size):
        return pl.ds(pl.multiple_of(start, 16), size)

    def do_copies(m):
        at = lambda p, c: do_v.at[m, at_rows((2 * p + c) * local, local)]
        far = []
        for way, (source, row, device) in enumerate(
            (
                (made_other, plane, links.sibling),
                (made_own, 1 - plane, links.across),
                (made_other, 1 - plane, links.diagonal),
            )
        ):
            far.append(
                pltpu.make_async_remote_copy(
                    src_ref=source.at[m * rows_of + row], dst_ref=at(plane, core), send_sem=do_sems.at[m, way],
                    recv_sem=do_sems.at[m, 3 + way], device_id=device, device_id_type=MESH,
                )
            )
        return far, pltpu.make_async_copy(made_own.at[m * rows_of + plane], at(plane, core), do_sems.at[m, 6])

    def attn_far():
        return pltpu.make_async_remote_copy(
            src_ref=attn_in, dst_ref=attn_there, send_sem=attn_sems.at[0], recv_sem=attn_sems.at[1],
            device_id=links.sibling, device_id_type=MESH,
        )

    def attn_loads():
        copies = []
        for m in range(micro):
            for r in range(rows_of):
                for side in range(2):
                    source = (attn_in, attn_there)[side]
                    half = core if side == 0 else 1 - core
                    start = (m * rows_of + r) * 2 * local + half * local
                    at = (m * rows_of + r) * 2 + side
                    copies.append(
                        pltpu.make_async_copy(source.at[m * rows_of + r], attn_v.at[at_rows(start, local)], attn_sems.at[4 + at])
                    )
        return copies

    mixed_load = pltpu.make_async_copy(mixed, mixed_v, attn_sems.at[2])
    normed_load = pltpu.make_async_copy(normed, normed_v, attn_sems.at[3])

    def unit_loads(m, p, slot):
        return [
            pltpu.make_async_copy(
                qkvs[m].at[:, pl.ds(pl.multiple_of((3 * p + part) * LANES, LANES), LANES)],
                qkv_v.at[slot, part],
                load_sems.at[slot, part],
            )
            for part in range(3)
        ]

    def start_unit(u):
        p, slot = u // micro, lax.rem(u, 2)
        for m in range(micro):

            @pl.when(lax.rem(u, micro) == m)
            def _(m=m):
                for copy in unit_loads(m, p, slot):
                    copy.start()

    def res_far(u):
        p, m = u // micro, lax.rem(u, micro)
        return pltpu.make_async_remote_copy(
            src_ref=res.at[lax.rem(u, 2), at_rows((1 - plane) * plane_len, plane_len)],
            dst_ref=sums_v.at[p, m * rows_of + plane],
            send_sem=res_sems.at[0, lax.rem(u, 2)], recv_sem=res_sems.at[1, u],
            device_id=links.across, device_id_type=MESH,
        )

    def dqkv_near(p, at):
        return pltpu.make_async_copy(
            sums_v.at[p, at, at_rows(core * local, local)], dqkv_own.at[at, :, pl.ds(p * wide, wide)], dqkv_sems.at[p, at, 0]
        )

    def dqkv_far(p, at):
        return pltpu.make_async_remote_copy(
            src_ref=sums_v.at[p, at, at_rows((1 - core) * local, local)],
            dst_ref=dqkv_there.at[at, :, pl.ds(p * wide, wide)],
            send_sem=dqkv_sems.at[p, at, 1], recv_sem=dqkv_sems.at[p, at, 2],
            device_id=links.sibling, device_id_type=MESH,
        )

    start_unit(jnp.int32(0))
    mixed_load.start()
    normed_load.start()
    for m in range(micro):
        do_copies(m)[1].start()
    links.greet(True)
    for m in range(micro):
        for copy in do_copies(m)[0]:
            copy.start()
    attn_far().start()
    scatter = Scatter(
        links, grads, inbox, totals, mine, came, made, total, send_sems, recv_sems, near_sems, total_sems, rows
    )

    def weight_grads(group, left, right):
        for at in range(left.shape[1] // 384):
            place = slice(at * 384, (at + 1) * 384)
            made_now = dot32(left[:, place], right, TN)
            grads[group, place] = made_now.astype(grads.dtype)
        scatter.start(jnp.int32(group))

    def grads_out():
        for copy in attn_loads():
            copy.wait()
        mixed_load.wait()
        weight_grads(0, attn_v, mixed_v[...])

    def grads_pair(p):
        if p == 0:
            normed_load.wait()
        for m in range(micro):
            res_far(jnp.int32(p * micro + m)).wait_recv()
        for at in range(micro * rows_of):
            dqkv_near(p, at).start()
            dqkv_far(p, at).start()
        right = sums_v[p].reshape(micro * rows_of * plane_len, wide)
        weight_grads(1 + p, normed_v, right)

    per_pair = micro * steps
    work = pairs * per_pair
    begins = [4] + [per_pair * (p + 1) + 3 for p in range(pairs - 1)] + [work + 2]
    gap = max(1, 8 // far)
    last = begins[-1] + 2 * far * gap

    def item(i, carry):
        u, b = i // steps, lax.rem(i, steps)
        p, m = u // micro, lax.rem(u, micro)
        slot = lax.rem(u, 2)

        @pl.when(i == 3)
        def _():
            attn_far().wait_recv()
            for copy in attn_loads():
                copy.start()

        for group, begin in enumerate(begins):
            g = jnp.int32(group)

            @pl.when(i == begin)
            def _(group=group):
                grads_out() if group == 0 else grads_pair(group - 1)

            for step in range(1, far + 1):

                @pl.when(i == begin + (2 * step - 1) * gap)
                def _(g=g, step=step):
                    scatter.fetch(g, step)

                @pl.when(i == begin + 2 * step * gap)
                def _(g=g, step=step):
                    if step < far:
                        scatter.pass_on(g, step)
                    else:
                        scatter.close(g)

        @pl.when((i < work) & (b == 0))
        def _():
            for copy in unit_loads(0, p, slot):
                copy.wait()

            @pl.when(u + 1 < units)
            def _():
                start_unit(u + 1)

            for k in range(micro):

                @pl.when(u == k)
                def _(k=k):
                    far_copies, near_copy = do_copies(k)
                    near_copy.wait()
                    for copy in far_copies:
                        copy.wait_recv()

            @pl.when(u >= 2)
            def _():
                res_far(u - 2).wait_send()

            @pl.when(m == 0)
            def _():
                for head in range(per):
                    strip[head] = toeplitz_strip(diag_ref[p * per + head], span).T
                acc_bias[...] = jnp.zeros_like(acc_bias)

            length = len_ref[m]
            for head in range(per):
                here = lanes_k // head_dim == head
                spare = ((head + 1) % per) * head_dim
                keys[head] = with_mask_lane(qkv_v[slot, 1], lanes_k, here, spare, length)
            acc_k[...] = jnp.zeros_like(acc_k)
            acc_v[...] = jnp.zeros_like(acc_v)

        @pl.when(i < work)
        def _():
            place = at_rows(b * block, block)
            q_now = qkv_v[slot, 0, place]
            do_now = do_v[m, place, pl.ds(pl.multiple_of(p * LANES, LANES), LANES)]
            grad_query = None
            for head in range(per):
                here = lanes_q // head_dim == head
                spare = ((head + 1) % per) * head_dim
                zero = jnp.zeros_like(q_now)
                one = (lanes_q == spare).astype(q_now.dtype)
                query = jnp.where(here, q_now, zero)
                grad = jnp.where(here, do_now, zero)
                raw = dot32(keys[head], query + one, NT)
                grad_probs = dot32(qkv_v[slot, 2], grad, NT)
                parts, offsets = [], []
                for sub in range(block // LANES):
                    offset = pl.multiple_of(seq_len - LANES - (b * block + sub * LANES), LANES)
                    offsets.append(offset)
                    parts.append(raw[:, sub * LANES : (sub + 1) * LANES] + strip[head, pl.ds(offset, seq_len), :])
                scores = jnp.concatenate(parts, axis=1)
                lse = lse_ref[m * pairs * per + p * per + head, :, pl.ds(pl.multiple_of(b * block, LANES), block)]
                probs = jnp.exp(scores - lse)
                product = probs * grad_probs
                inner = jnp.sum(product, axis=0, keepdims=True)
                grad_scores = product - probs * inner
                for sub, offset in enumerate(offsets):
                    acc_bias[head, pl.ds(offset, seq_len), :] += grad_scores[:, sub * LANES : (sub + 1) * LANES]
                rounded = grad_scores.astype(jnp.bfloat16)
                acc_v[...] += dot32(probs.astype(jnp.bfloat16), grad, NN)
                acc_k[...] += dot32(rounded, query, NN)
                made_now = dot32(rounded, qkv_v[slot, 1], TN)
                grad_query = made_now if grad_query is None else jnp.where(here, made_now, grad_query)
            res[slot, place, :LANES] = grad_query.astype(res.dtype)

        @pl.when((i < work) & (b == steps - 1))
        def _():
            res[slot, :, LANES : 2 * LANES] = acc_k[...].astype(res.dtype)
            res[slot, :, 2 * LANES :] = acc_v[...].astype(res.dtype)
            res_far(u).start()
            sums_v[p, m * rows_of + plane] = res[slot, at_rows(plane * plane_len, plane_len)]

            @pl.when(m == micro - 1)
            def _():
                row = lax.broadcasted_iota(jnp.int32, (LANES, LANES), 0)
                col = lax.broadcasted_iota(jnp.int32, (LANES, LANES), 1)
                flip = (row + col == LANES - 1).astype(jnp.float32)
                for head in range(per):
                    turned = lax.dot_general(
                        flip, acc_bias[head], NT, precision=highest, preferred_element_type=jnp.float32
                    )
                    aligned = pltpu.roll(turned, 0, 1, stride=1, stride_axis=0)
                    dd_ref[p * per + head] = jnp.sum(aligned, axis=0, keepdims=True)

        return carry

    lax.fori_loop(0, last + 1, item, 0)
    scatter.total_copy(jnp.int32(pairs)).wait()
    for m in range(micro):
        for copy in do_copies(m)[0]:
            copy.wait_send()
    attn_far().wait_send()
    for u in range(max(0, units - 2), units):
        res_far(jnp.int32(u)).wait_send()
    for p in range(pairs):
        for at in range(micro * rows_of):
            dqkv_near(p, at).wait()
            dqkv_far(p, at).wait()


def mix_back(qkvs, made_own, made_other, attn_in, mixed, normed, lse, diag, lengths, head_dim, count, planes, block=256):
    micro = len(qkvs)
    rows_of = attn_in.shape[0] // micro
    _, local, depth = attn_in.shape
    seq_len, cols = qkvs[0].shape[0], qkvs[0].shape[1] // 3
    pairs, per, span = cols // LANES, LANES // head_dim, diag.shape[-1]
    tokens = normed.shape[0]
    rows, wide, far = depth // count, 3 * LANES, count // 2
    groups = 1 + pairs
    plan = (count, planes, rows, micro, rows_of, head_dim, block, pairs)
    anywhere = pl.BlockSpec(memory_space=pl.ANY)
    low, f32 = jnp.bfloat16, jnp.float32
    dma = pltpu.SemaphoreType.DMA
    return pl.pallas_call(
        functools.partial(mix_back_kernel, plan),
        in_specs=[pl.BlockSpec(memory_space=pltpu.SMEM)]
        + [pl.BlockSpec(memory_space=pltpu.VMEM)] * 2
        + [anywhere] * (micro + 5),
        out_specs=[anywhere, anywhere, pl.BlockSpec(memory_space=pltpu.VMEM), anywhere, anywhere],
        out_shape=[
            jax.ShapeDtypeStruct((micro * rows_of, local, 3 * cols), low),
            jax.ShapeDtypeStruct((micro * rows_of, local, 3 * cols), low),
            jax.ShapeDtypeStruct(diag.shape, f32),
            jax.ShapeDtypeStruct((groups, rows, wide), f32),
            jax.ShapeDtypeStruct(attn_in.shape, low),
        ],
        scratch_shapes=[
            pltpu.VMEM((2, 3, seq_len, LANES), low),
            pltpu.VMEM((micro, seq_len, cols), low),
            pltpu.VMEM((2, seq_len, wide), low),
            pltpu.VMEM((pairs, micro * rows_of, seq_len // 2, wide), low),
            pltpu.VMEM((tokens, depth), low),
            pltpu.VMEM((tokens, cols), low),
            pltpu.VMEM((tokens, depth), low),
            pltpu.VMEM((groups, depth, wide), low),
            pltpu.VMEM((groups, 2, far, rows, wide), low),
            pltpu.VMEM((per, span, LANES), f32),
            pltpu.VMEM((per, seq_len, LANES), low),
            pltpu.VMEM((per, span, LANES), f32),
            pltpu.VMEM((seq_len, LANES), f32),
            pltpu.VMEM((seq_len, LANES), f32),
            pltpu.VMEM((2, 2, rows, wide), low),
            pltpu.VMEM((2, 2, rows, wide), low),
            pltpu.VMEM((2, 2, rows, wide), low),
            pltpu.VMEM((rows, wide), f32),
            dma((2, 3)),
            dma((micro, 7)),
            dma((2, pairs * micro)),
            dma((4 + 2 * micro * rows_of,)),
            dma((pairs, micro * rows_of, 3)),
            dma((groups, 2, far)),
            dma((groups, 2, far)),
            dma((2, 2, 2)),
            dma((1,)),
        ],
        compiler_params=pltpu.CompilerParams(
            collective_id=2, has_side_effects=True, vmem_limit_bytes=62 * 1024 * 1024
        ),
        name="mix_back",
    )(lengths, lse, diag, *qkvs, made_own, made_other, attn_in, mixed, normed)


def resid_back_kernel(kept, got, out_kept, out_got, resid_ref, cot, gain, w_own, w_other, grad_ref, attn_ref, own_ref, other_ref, out_ref, sum_ref):
    @pl.when(pl.program_id(0) == 0)
    def _():
        sum_ref[...] = jnp.zeros_like(sum_ref)

    wide = jnp.float32
    resid = resid_ref[...]
    out_ref[...] = (resid + (out_kept[...].astype(wide) + out_got[...].astype(wide))).astype(out_ref.dtype)
    grad = kept[...].astype(wide) + got[...].astype(wide)
    root = lax.rsqrt(jnp.mean(resid * resid, axis=-1, keepdims=True) + eps)
    sum_ref[...] += jnp.sum(grad * resid * root, axis=0, keepdims=True)
    scaled = grad * gain[...]
    shared = jnp.mean(scaled * resid, axis=-1, keepdims=True) * root * root * root
    total = cot[...].astype(wide) + scaled * root - resid * shared
    grad_ref[...] = total
    low = total.astype(attn_ref.dtype)
    attn_ref[...] = low
    own_ref[...] = dot32(low, w_own[...], NN).astype(own_ref.dtype)
    other_ref[...] = dot32(low, w_other[...], NN).astype(other_ref.dtype)


def resid_back(kept, got, out_kept, out_got, resid, cotangent, gain, w_own, w_other):
    groups, tile, depth = kept.shape
    cols = w_own.shape[1]
    tall = lambda width: pl.BlockSpec((None, tile, width), lambda g: (g, 0, 0))
    flat = lambda shape: pl.BlockSpec(shape, lambda g: (0, 0))
    low, wide = jnp.bfloat16, jnp.float32
    shape = lambda width, kind: jax.ShapeDtypeStruct((groups, tile, width), kind)
    return pl.pallas_call(
        resid_back_kernel,
        grid=(groups,),
        in_specs=[tall(depth)] * 6 + [flat((1, depth)), flat((depth, cols)), flat((depth, cols))],
        out_specs=[tall(depth), tall(depth), tall(cols), tall(cols), tall(depth), flat((1, depth))],
        out_shape=[
            shape(depth, wide), shape(depth, low), shape(cols, low), shape(cols, low), shape(depth, low),
            jax.ShapeDtypeStruct((1, depth), wide),
        ],
        compiler_params=pltpu.CompilerParams(vmem_limit_bytes=VMEM_LIMIT),
        name="resid_back",
    )(kept, got, out_kept, out_got, resid, cotangent, gain, w_own, w_other)


def input_back_kernel(own, there, w_own, w_other, tokens, grad_resid, gain, out_ref, sum_ref):
    @pl.when(pl.program_id(0) == 0)
    def _():
        sum_ref[...] = jnp.zeros_like(sum_ref)

    grad = dot32(own[...], w_own[...], NT) + dot32(there[...], w_other[...], NT)
    values = tokens[...].astype(jnp.float32)
    root = lax.rsqrt(jnp.mean(values * values, axis=-1, keepdims=True) + eps)
    sum_ref[...] += jnp.sum(grad * values * root, axis=0, keepdims=True)
    scaled = grad * gain[...]
    shared = jnp.mean(scaled * values, axis=-1, keepdims=True) * root * root * root
    out_ref[...] = grad_resid[...] + scaled * root - values * shared


def input_back(own, there, w_own, w_other, tokens, grad_resid, gain):
    groups, tile, depth = tokens.shape
    cols = own.shape[2]
    tall = lambda width: pl.BlockSpec((None, tile, width), lambda g: (g, 0, 0))
    flat = lambda shape: pl.BlockSpec(shape, lambda g: (0, 0))
    return pl.pallas_call(
        input_back_kernel,
        grid=(groups,),
        in_specs=[tall(cols), tall(cols), flat((depth, cols)), flat((depth, cols)), tall(depth), tall(depth), flat((1, depth))],
        out_specs=[tall(depth), flat((1, depth))],
        out_shape=[
            jax.ShapeDtypeStruct((groups, tile, depth), jnp.float32), jax.ShapeDtypeStruct((1, depth), jnp.float32)
        ],
        compiler_params=pltpu.CompilerParams(vmem_limit_bytes=VMEM_LIMIT),
        name="input_back",
    )(own, there, w_own, w_other, tokens, grad_resid, gain)


def small_sum_kernel(sizes, x_ref, o_ref, outbox, inbox, send_sems, recv_sems):
    partners = []
    for name, size in sizes:
        at, bit = lax.axis_index(name), 1
        while bit < size:
            partners.append({name: jnp.where(lax.rem(at // bit, 2) == 0, at + bit, at - bit)})
            bit *= 2
    barrier = pltpu.get_barrier_semaphore()
    for partner in partners:
        pl.semaphore_signal(barrier, inc=1, device_id=partner, device_id_type=MESH)
    pl.semaphore_wait(barrier, len(partners))
    o_ref[...] = x_ref[...]
    for at, partner in enumerate(partners):
        outbox[at] = o_ref[...]
        copy = pltpu.make_async_remote_copy(
            src_ref=outbox.at[at], dst_ref=inbox.at[at], send_sem=send_sems.at[at], recv_sem=recv_sems.at[at],
            device_id=partner, device_id_type=MESH,
        )
        copy.start()
        copy.wait()
        o_ref[...] += inbox[at]


def small_sum(values, sizes):
    rounds = sum(size.bit_length() - 1 for _, size in sizes)
    return pl.pallas_call(
        functools.partial(small_sum_kernel, sizes),
        in_specs=[pl.BlockSpec(memory_space=pltpu.VMEM)],
        out_specs=pl.BlockSpec(memory_space=pltpu.VMEM),
        out_shape=jax.ShapeDtypeStruct(values.shape, values.dtype),
        scratch_shapes=[
            pltpu.VMEM((rounds,) + values.shape, values.dtype),
            pltpu.VMEM((rounds,) + values.shape, values.dtype),
            pltpu.SemaphoreType.DMA((rounds,)),
            pltpu.SemaphoreType.DMA((rounds,)),
        ],
        compiler_params=pltpu.CompilerParams(collective_id=3, has_side_effects=True),
        name="small_sum",
    )(values)


class Ring:
    def __init__(self, count):
        order = ring_order(count)
        place = [0] * count
        for at, index in enumerate(order):
            place[index] = at
        self.count = count
        self.order = jnp.array(order, jnp.int32)
        self.here = jnp.array(place, jnp.int32)[lax.axis_index("dp")]
        self.ahead = [(order[i], order[(i + 1) % count]) for i in range(count)]
        self.behind = [(order[i], order[(i - 1) % count]) for i in range(count)]

    def owner(self, shift):
        return self.order[(self.here + shift) % self.count]

    def send(self, block, forward):
        return lax.ppermute(block, "dp", self.ahead if forward else self.behind)

    def gather(self, shard):
        rows, cols = shard.shape
        cut = cols // 2
        far = self.count // 2
        whole = jnp.zeros((self.count * rows, cols), shard.dtype)

        def put(whole, block, shift, column=0):
            return lax.dynamic_update_slice(whole, block, (self.owner(shift) * rows, column))

        whole = put(whole, shard, 0)
        ahead = behind = shard
        for step in range(1, far):
            ahead, behind = self.send(ahead, True), self.send(behind, False)
            whole = put(put(whole, ahead, -step), behind, step)
        last = (ahead, behind)
        ahead, behind = self.send(ahead[:, :cut], True), self.send(behind[:, cut:], False)
        whole = put(put(whole, ahead, -far), behind, far, cut)
        return whole, last

    def scatter(self, local, cols):
        cut = cols // 2
        far = self.count // 2
        most = local(self.owner(far))
        ahead, behind = self.send(most[:, :cut], True), self.send(most[:, cut:], False)
        for step in range(far - 1, 0, -1):
            mine = local(self.owner(step))
            other = local(self.owner(-step))
            if step == far - 1:
                ahead = jnp.concatenate([add_low(mine[:, :cut], ahead), mine[:, cut:]], axis=1)
                behind = jnp.concatenate([other[:, :cut], add_low(other[:, cut:], behind)], axis=1)
            else:
                ahead, behind = add_low(mine, ahead), add_low(other, behind)
            ahead, behind = self.send(ahead, True), self.send(behind, False)
        return local(self.owner(0)).astype(jnp.float32) + ahead.astype(jnp.float32) + behind.astype(jnp.float32)


def add_low(a, b):
    return (a.astype(jnp.float32) + b.astype(jnp.float32)).astype(jnp.bfloat16)


def body(
    tokens, cotangent, lengths, buckets, gain_one, gain_two, table,
    w_query, w_key, w_value, w_out, w_gate, w_up, w_down,
):
    micro, rows, local, width = tokens.shape
    seq_devices = lax.axis_size("seq")
    dp_devices = lax.axis_size("dp")
    seq_rank = lax.axis_index("seq")
    core = seq_rank % 2
    plane = seq_rank // 2
    planes = seq_devices // 2
    heads = table.shape[1]
    shard_rows, inner = w_query.shape
    head_dim = inner // heads
    half_inner = inner // 2
    hidden_units = w_gate.shape[1]
    pair_local = 2 * local
    seq_len = local * seq_devices
    first = core == 0
    core_pairs = [(i, i ^ 1) for i in range(seq_devices)]
    plane_groups = [[2 * p + c for p in range(planes)] for c in range(2)]
    ring = Ring(dp_devices)

    def swap_core(value):
        return lax.ppermute(value, "seq", core_pairs)

    def both_cores(own, other, axis):
        return jnp.concatenate([jnp.where(first, own, other), jnp.where(first, other, own)], axis=axis)

    def own_half(value, axis):
        return lax.dynamic_slice_in_dim(value, core * local, local, axis)

    def other_half(value, axis):
        return lax.dynamic_slice_in_dim(value, (1 - core) * local, local, axis)

    def core_columns(weight, split):
        low, high = weight[:, :split], weight[:, split:]
        high = jnp.pad(high, ((0, 0), (0, split - high.shape[1])))
        return jnp.where(first, low, high)

    chunk = 512
    chunks = -(-(hidden_units // 2) // chunk)
    split = chunks * chunk
    if split > hidden_units:
        split = hidden_units
    fused = planes == 2 and rows == 2 and half_inner % LANES == 0
    attn_parts = [core_columns(w, half_inner) for w in (w_query, w_key, w_value)]
    if fused:
        attn_parts = [w[:, p : p + LANES] for p in range(0, half_inner, LANES) for w in attn_parts]
    attn_shard = jnp.concatenate(attn_parts + [core_columns(w_out.T, half_inner)], axis=1)
    up_parts = [core_columns(w, split) for w in (w_gate, w_up, w_down.T)]
    chunk_shards = [
        jnp.concatenate([w[:, n * chunk : (n + 1) * chunk] for w in up_parts], axis=1) for n in range(chunks)
    ]

    small = jnp.concatenate([gain_one, gain_two, table.reshape(-1)])
    small = jnp.pad(small, (0, -small.shape[0] % LANES))
    small = jnp.pad(small[None], ((0, 15), (0, 0)))
    attn_weights, small, tokens_other, cotangent_other = gather_first(
        attn_shard, small, tokens, cotangent, dp_devices, planes
    )
    small = small.reshape(dp_devices, 16, -1)[:, 0].astype(jnp.float32)
    gain_first = small[:, :shard_rows].reshape(-1)
    gain_second = small[:, shard_rows : 2 * shard_rows].reshape(-1)
    full_table = small[:, 2 * shard_rows : 2 * shard_rows + table.size].reshape(-1, heads)
    last = attn_weights
    qkv_cols = 3 * half_inner
    there_weights = swap_core(attn_weights)
    qkv_weights = attn_weights[:, :qkv_cols]
    out_own, out_other = attn_weights[:, qkv_cols:], there_weights[:, qkv_cols:]
    out_pair = jnp.concatenate([out_own, out_other], axis=1)

    early = min(2, chunks - 1)
    ready = []
    for shard in chunk_shards[:early]:
        shard, last = lax.optimization_barrier((shard, last))
        ready.append(lax.all_gather(shard, "dp", axis=0, tiled=True))

    tokens_pair = both_cores(tokens, tokens_other, 2)
    down_in = both_cores(cotangent, cotangent_other, 2)

    core_heads = heads // 2
    head_splits = planes // rows
    item_heads = core_heads // head_splits
    item_cols = item_heads * head_dim
    padded_cols = -(-item_cols // LANES) * LANES
    padded_heads = padded_cols // head_dim
    item_row = plane // head_splits
    item_group = plane % head_splits
    head_start = core * core_heads + item_group * item_heads
    item_table = lax.dynamic_slice_in_dim(full_table, head_start, item_heads, 1)
    item_table = jnp.pad(item_table, ((0, 0), (0, padded_heads - item_heads)))
    levels = full_table.shape[0]
    bucket_hot = (buckets[:, None] == jnp.arange(levels)[None, :]).astype(jnp.float32)
    bucket_hot = jnp.pad(bucket_hot, ((0, 1), (0, 0)))
    diag = jnp.dot(item_table.T, bucket_hot.T, precision=highest)[:, None, :]

    def to_items(value, parts):
        if planes == 2 and rows == 2:
            mine = lax.dynamic_index_in_dim(value, plane, 0, keepdims=False)
            sent = lax.dynamic_index_in_dim(value, 1 - plane, 0, keepdims=False)
            got = lax.ppermute(sent, "seq", [(i, i ^ 2) for i in range(4)])
            low = plane == 0
            return jnp.concatenate([jnp.where(low, mine, got), jnp.where(low, got, mine)], axis=0)
        value = value.reshape(rows, pair_local, parts, head_splits, item_cols)
        value = value.transpose(0, 3, 1, 2, 4).reshape(planes, pair_local, parts * item_cols)
        value = lax.all_to_all(value, "seq", 0, 0, tiled=True, axis_index_groups=plane_groups)
        value = value.reshape(seq_len, parts, item_cols)
        value = jnp.pad(value, ((0, 0), (0, 0), (0, padded_cols - item_cols)))
        return value.reshape(seq_len, parts * padded_cols)

    def from_items(values):
        parts = len(values)
        if planes == 2 and rows == 2:
            value = jnp.concatenate(values, axis=1)
            mine = lax.dynamic_slice_in_dim(value, plane * pair_local, pair_local, 0)
            sent = lax.dynamic_slice_in_dim(value, (1 - plane) * pair_local, pair_local, 0)
            got = lax.ppermute(sent, "seq", [(i, i ^ 2) for i in range(4)])
            low = plane == 0
            return jnp.stack([jnp.where(low, mine, got), jnp.where(low, got, mine)])
        value = jnp.concatenate([v[:, :item_cols] for v in values], axis=1)
        value = value.reshape(planes, pair_local, parts * item_cols)
        value = lax.all_to_all(value, "seq", 0, 0, tiled=True, axis_index_groups=plane_groups)
        value = value.reshape(rows, head_splits, pair_local, parts, item_cols).transpose(0, 2, 3, 1, 4)
        return value.reshape(rows, pair_local, parts * half_inner)

    normed, roots, qkvs, lses, mixes, resids, normed_twos, item_lens = [], [], [], [], [], [], [], []
    for step in range(micro):
        rows_in = tokens_pair[step].astype(jnp.float32)
        root = lax.rsqrt(jnp.mean(rows_in * rows_in, axis=-1, keepdims=True) + eps)
        roots.append(root)
        normed.append((rows_in * root * gain_first).astype(jnp.bfloat16))
    for step in range(micro):
        made = jnp.einsum("rld,de->rle", normed[step], qkv_weights, preferred_element_type=jnp.float32)
        qkvs.append(to_items(made.astype(jnp.bfloat16), 3))
    for step in range(micro):
        item_len = lax.dynamic_slice_in_dim(lengths[step], item_row, 1, 0)
        item_lens.append(item_len)
        mixed, lse = attend(qkvs[step], diag, item_len, head_dim, fused)
        lses.append(lse)
        mixed_own = from_items([mixed])
        mixes.append(mixed_own)
        mixed_pair = jnp.concatenate([mixed_own, swap_core(mixed_own)], axis=2)
        resid = tokens_pair[step].astype(jnp.float32) + jnp.einsum(
            "rle,de->rld", mixed_pair, out_pair, preferred_element_type=jnp.float32
        )
        root = lax.rsqrt(jnp.mean(resid * resid, axis=-1, keepdims=True) + eps)
        normed_twos.append((resid * root * gain_second).astype(jnp.bfloat16))
        resids.append(own_half(resid, 1))

    def apart(qkvs, grads_items, lses, item_lens, attn_all, mixed_all, normed_all):
        grads_qkv, diag_sum = [], 0.0
        for step in range(micro):
            grad_q, grad_k, grad_v, grad_diag = attend_back(
                qkvs[step], grads_items[step], lses[step], diag, item_lens[step], head_dim
            )
            diag_sum = diag_sum + grad_diag[:item_heads, 0]
            grads_qkv.append(from_items([grad_q, grad_k, grad_v]))
        grads_all = jnp.concatenate([flat(v) for v in grads_qkv])
        attn_all = flat(both_cores(attn_all, swap_core(attn_all), 2))
        grad_attn = jnp.einsum("td,te->de", normed_all, grads_all, preferred_element_type=jnp.float32)
        grad_o = jnp.einsum("td,te->de", attn_all, mixed_all, preferred_element_type=jnp.float32)
        both = jnp.concatenate([grad_o, grad_attn], axis=1).astype(jnp.bfloat16)
        total = ring.scatter(
            lambda index: lax.dynamic_slice_in_dim(both, index * shard_rows, shard_rows, 0), 4 * half_inner
        )
        return grads_qkv, diag_sum, total

    flat = lambda value: value.reshape(-1, value.shape[-1])
    normed_two_all = jnp.concatenate([flat(v) for v in normed_twos])
    down_all = flat(down_in)
    back_kept, back_got, out_kept, out_got, chunk_totals = feed(
        normed_two_all, down_all, ready, chunk_shards[early:], dp_devices, planes, local
    )
    by_row = lambda value: value.reshape(micro * rows, local, value.shape[-1])
    grad_resid, attn_in, made_own, made_other, output, gain_two_sum = resid_back(
        back_kept, back_got, out_kept, out_got, jnp.concatenate(resids), by_row(cotangent), gain_second[None],
        out_own, out_other,
    )

    normed_all = jnp.concatenate([flat(v) for v in normed])
    mixed_all = jnp.concatenate([flat(v) for v in mixes])
    if fused:
        own, there, diag_sum, attn_totals, _ = mix_back(
            qkvs, made_own, made_other, attn_in, mixed_all, normed_all, jnp.concatenate(lses), diag,
            jnp.concatenate(item_lens), head_dim, dp_devices, planes,
        )
        input_grad, gain_one_sum = input_back(
            own, there, attn_weights, there_weights, by_row(tokens), grad_resid, gain_first[None]
        )
        diag_sum = diag_sum[:, 0]
    else:
        split_micro = lambda value: value.reshape(micro, rows, local, -1)
        grads_mixed = both_cores(split_micro(made_own), swap_core(split_micro(made_other)), 2)
        grads_qkv, diag_sum, attn_totals = apart(
            qkvs, [to_items(g, 1) for g in grads_mixed], lses, item_lens, split_micro(attn_in), mixed_all, normed_all
        )
        grads_qkv = jnp.stack(grads_qkv)
        own = by_row(own_half(grads_qkv, 2))
        there = swap_core(by_row(other_half(grads_qkv, 2)))
        input_grad, gain_one_sum = input_back(
            own, there, attn_weights, there_weights, by_row(tokens), grad_resid, gain_first[None]
        )
    item_grad = jnp.dot(diag_sum, bucket_hot, precision=highest)
    grad_table = lax.dynamic_update_slice(jnp.zeros((heads, levels), jnp.float32), item_grad, (head_start, 0))

    def finish(total):
        if planes == 2:
            low = total.astype(jnp.bfloat16)
            got = lax.ppermute(low, "seq", [(i, i ^ 2) for i in range(4)])
            total = low.astype(jnp.float32) + got.astype(jnp.float32)
        else:
            total = lax.psum(total, "seq", axis_index_groups=plane_groups)
        return total, swap_core(total)

    def whole_columns(own, other, size):
        low, high = jnp.where(first, own, other), jnp.where(first, other, own)
        return jnp.concatenate([low, high[:, : size - low.shape[1]]], axis=1)

    own, other = finish(attn_totals)
    if fused:
        grad_out = whole_columns(own[0], other[0], inner)
        grad_query, grad_key, grad_value = [
            whole_columns(
                jnp.concatenate(list(own[1:, :, part * LANES : (part + 1) * LANES]), axis=1),
                jnp.concatenate(list(other[1:, :, part * LANES : (part + 1) * LANES]), axis=1),
                inner,
            )
            for part in range(3)
        ]
    else:
        parts = [slice(i * half_inner, (i + 1) * half_inner) for i in range(4)]
        grad_out, grad_query, grad_key, grad_value = [whole_columns(own[:, p], other[:, p], inner) for p in parts]
    own, other = finish(chunk_totals)
    done = [(own[n], other[n]) for n in range(chunks)]
    parts = [slice(i * chunk, (i + 1) * chunk) for i in range(3)]
    grad_gate, grad_up, grad_down = [
        whole_columns(
            jnp.concatenate([own[:, p] for own, _ in done], axis=1),
            jnp.concatenate([other[:, p] for _, other in done], axis=1),
            hidden_units,
        )
        for p in parts
    ]

    dp_rank = lax.axis_index("dp")
    small = jnp.concatenate([gain_one_sum[0], gain_two_sum[0], grad_table.T.reshape(-1)])
    small = jnp.pad(small, (0, -small.shape[0] % (8 * LANES))).reshape(-1, LANES)
    small = small_sum(small, (("seq", seq_devices), ("dp", dp_devices))).reshape(-1)
    grad_gain_one = lax.dynamic_slice_in_dim(small, dp_rank * shard_rows, shard_rows, 0)
    grad_gain_two = lax.dynamic_slice_in_dim(small, width + dp_rank * shard_rows, shard_rows, 0)
    table_part = levels // dp_devices
    grad_table = lax.dynamic_slice_in_dim(small[2 * width : 2 * width + levels * heads].reshape(levels, heads), dp_rank * table_part, table_part, 0)

    return (
        output.reshape(tokens.shape), input_grad.reshape(tokens.shape), grad_gain_one, grad_gain_two, grad_table,
        grad_query, grad_key, grad_value, grad_out.T, grad_gate, grad_up, grad_down.T,
    )


def solution(mesh):
    weight, turned = P("dp", None), P(None, "dp")
    return jax.shard_map(
        body,
        mesh=mesh,
        in_specs=(
            P(None, "dp", "seq", None), P(None, "dp", "seq", None), P(None, "dp"), P(), P("dp"), P("dp"),
            weight, weight, weight, weight, turned, weight, weight, turned,
        ),
        out_specs=(
            P(None, "dp", "seq", None), P(None, "dp", "seq", None), P("dp"), P("dp"),
            weight, weight, weight, weight, turned, weight, weight, turned,
        ),
        check_vma=False,
    )
```

```python
import functools

import jax
import jax.numpy as jnp
from jax import lax
from jax.experimental import pallas as pl
from jax.experimental.pallas import tpu as pltpu
from jax.sharding import PartitionSpec as P

eps = 1e-06
masked_value = -1e30
highest = lax.Precision.HIGHEST
gelu_scale = 0.7978845608028654
gelu_cubic = 0.044715
LANES = 128
VMEM_LIMIT = 56 * 1024 * 1024
NT = (((1,), (1,)), ((), ()))
NN = (((1,), (0,)), ((), ()))
TN = (((0,), (0,)), ((), ()))


def dot32(a, b, dims):
    return lax.dot_general(a, b, dims, preferred_element_type=jnp.float32)


def toeplitz_strip(diag_row, span):
    wide = jnp.broadcast_to(diag_row, (LANES, span))
    return pltpu.roll(wide, span - (LANES - 1), 1, stride=1, stride_axis=0)


def with_mask_lane(key_pair, lanes, here, spare, length):
    rows = lax.broadcasted_iota(jnp.int32, key_pair.shape, 0)
    mask = jnp.where(rows < length, 0.0, masked_value).astype(key_pair.dtype)
    zero = jnp.zeros_like(key_pair)
    return jnp.where(here, key_pair, jnp.where(lanes == spare, mask, zero))


def attend_kernel(head_dim, block, len_ref, diag_ref, q_ref, k_ref, v_ref, mixed_ref, lse_ref, strip, keys):
    step = pl.program_id(1)
    seq_len = k_ref.shape[0]
    span = diag_ref.shape[-1]
    length = len_ref[0]
    per = LANES // head_dim
    lanes_k = lax.broadcasted_iota(jnp.int32, (seq_len, LANES), 1)
    lanes_q = lax.broadcasted_iota(jnp.int32, (block, LANES), 1)

    @pl.when(step == 0)
    def _():
        for head in range(per):
            strip[head] = toeplitz_strip(diag_ref[head], span)
            here = lanes_k // head_dim == head
            spare = ((head + 1) % per) * head_dim
            keys[head] = with_mask_lane(k_ref[...], lanes_k, here, spare, length)

    mixed = None
    for head in range(per):
        here = lanes_q // head_dim == head
        spare = ((head + 1) % per) * head_dim
        one = (lanes_q == spare).astype(q_ref.dtype)
        query = jnp.where(here, q_ref[...], one)
        raw = dot32(query, keys[head], NT)
        parts = []
        for sub in range(block // LANES):
            offset = seq_len - LANES - (step * block + sub * LANES)
            offset = pl.multiple_of(offset, LANES)
            parts.append(raw[sub * LANES : (sub + 1) * LANES] + strip[head, :, pl.ds(offset, seq_len)])
        scores = jnp.concatenate(parts, axis=0)
        top = jnp.max(scores, axis=1, keepdims=True)
        expo = jnp.exp(scores - top)
        total = jnp.sum(expo, axis=1, keepdims=True)
        made = dot32(expo.astype(jnp.bfloat16), v_ref[...], NN) / total
        mixed = made if mixed is None else jnp.where(here, made, mixed)
        lse = jnp.broadcast_to(top + jnp.log(total), (block, LANES))
        lse_ref[head] = lse.T[:1]
    mixed_ref[...] = mixed.astype(mixed_ref.dtype)


def attend(qkv, diag, length, head_dim, by_pair=False, block=256):
    seq_len, cols = qkv.shape[0], qkv.shape[1] // 3
    pairs = cols // LANES
    per = LANES // head_dim
    span = diag.shape[-1]
    at = (lambda part, p: 3 * p + part) if by_pair else (lambda part, p: part * pairs + p)
    flops = 2 * 2 * seq_len * seq_len * LANES * 2 * cols // head_dim
    return pl.pallas_call(
        functools.partial(attend_kernel, head_dim, block),
        grid=(pairs, seq_len // block),
        in_specs=[
            pl.BlockSpec(memory_space=pltpu.SMEM),
            pl.BlockSpec((per, 1, span), lambda p, b: (p, 0, 0)),
            pl.BlockSpec((block, LANES), lambda p, b: (b, at(0, p))),
            pl.BlockSpec((seq_len, LANES), lambda p, b: (0, at(1, p))),
            pl.BlockSpec((seq_len, LANES), lambda p, b: (0, at(2, p))),
        ],
        out_specs=[
            pl.BlockSpec((block, LANES), lambda p, b: (b, p)),
            pl.BlockSpec((per, 1, block), lambda p, b: (p, 0, b)),
        ],
        out_shape=[
            jax.ShapeDtypeStruct((seq_len, cols), jnp.bfloat16),
            jax.ShapeDtypeStruct((cols // head_dim, 1, seq_len), jnp.float32),
        ],
        scratch_shapes=[
            pltpu.VMEM((per, LANES, span), jnp.float32),
            pltpu.VMEM((per, seq_len, LANES), jnp.bfloat16),
        ],
        compiler_params=pltpu.CompilerParams(vmem_limit_bytes=VMEM_LIMIT),
        cost_estimate=pl.CostEstimate(flops=flops, bytes_accessed=8 * seq_len * cols, transcendentals=0),
        name="attend",
    )(length, diag, qkv, qkv, qkv)


def attend_back_kernel(
    head_dim, block, len_ref, diag_ref, q_ref, k_ref, v_ref, do_ref, lse_ref,
    dq_ref, dk_ref, dv_ref, dd_ref, strip, keys, acc_bias, acc_k, acc_v,
):
    step = pl.program_id(1)
    steps = pl.num_programs(1)
    seq_len = k_ref.shape[0]
    span = diag_ref.shape[-1]
    length = len_ref[0]
    per = LANES // head_dim
    lanes_k = lax.broadcasted_iota(jnp.int32, (seq_len, LANES), 1)
    lanes_q = lax.broadcasted_iota(jnp.int32, (block, LANES), 1)
    subs = block // LANES

    @pl.when(step == 0)
    def _():
        for head in range(per):
            strip[head] = toeplitz_strip(diag_ref[head], span).T
            here = lanes_k // head_dim == head
            spare = ((head + 1) % per) * head_dim
            keys[head] = with_mask_lane(k_ref[...], lanes_k, here, spare, length)
        acc_bias[...] = jnp.zeros_like(acc_bias)
        acc_k[...] = jnp.zeros_like(acc_k)
        acc_v[...] = jnp.zeros_like(acc_v)

    grad_query = None
    for head in range(per):
        here = lanes_q // head_dim == head
        spare = ((head + 1) % per) * head_dim
        zero = jnp.zeros_like(q_ref[...])
        one = (lanes_q == spare).astype(q_ref.dtype)
        query = jnp.where(here, q_ref[...], zero)
        grad = jnp.where(here, do_ref[...], zero)
        raw = dot32(keys[head], query + one, NT)
        grad_probs = dot32(v_ref[...], grad, NT)
        parts = []
        offsets = []
        for sub in range(subs):
            offset = seq_len - LANES - (step * block + sub * LANES)
            offset = pl.multiple_of(offset, LANES)
            offsets.append(offset)
            parts.append(raw[:, sub * LANES : (sub + 1) * LANES] + strip[head, pl.ds(offset, seq_len), :])
        scores = jnp.concatenate(parts, axis=1)
        probs = jnp.exp(scores - lse_ref[head])
        product = probs * grad_probs
        inner = jnp.sum(product, axis=0, keepdims=True)
        grad_scores = product - probs * inner
        for sub in range(subs):
            rows = pl.ds(offsets[sub], seq_len)
            acc_bias[head, rows, :] += grad_scores[:, sub * LANES : (sub + 1) * LANES]
        rounded = grad_scores.astype(jnp.bfloat16)
        acc_v[...] += dot32(probs.astype(jnp.bfloat16), grad, NN)
        acc_k[...] += dot32(rounded, query, NN)
        made = dot32(rounded, k_ref[...], TN)
        grad_query = made if grad_query is None else jnp.where(here, made, grad_query)
    dq_ref[...] = grad_query.astype(dq_ref.dtype)

    @pl.when(step == steps - 1)
    def _():
        dk_ref[...] = acc_k[...].astype(dk_ref.dtype)
        dv_ref[...] = acc_v[...].astype(dv_ref.dtype)
        row = lax.broadcasted_iota(jnp.int32, (LANES, LANES), 0)
        col = lax.broadcasted_iota(jnp.int32, (LANES, LANES), 1)
        flip = (row + col == LANES - 1).astype(jnp.float32)
        for head in range(per):
            turned = lax.dot_general(
                flip, acc_bias[head], NT, precision=lax.Precision.HIGHEST, preferred_element_type=jnp.float32
            )
            aligned = pltpu.roll(turned, 0, 1, stride=1, stride_axis=0)
            dd_ref[head] = jnp.sum(aligned, axis=0, keepdims=True)


def attend_back(qkv, grad_mixed, lse, diag, length, head_dim, block=256):
    seq_len, cols = qkv.shape[0], qkv.shape[1] // 3
    pairs = cols // LANES
    per = LANES // head_dim
    span = diag.shape[-1]
    flops = 5 * 2 * seq_len * seq_len * LANES * 2 * cols // head_dim
    whole = lambda p, b: (0, p)
    part = lambda p, b: (b, p)
    flat = jax.ShapeDtypeStruct((seq_len, cols), jnp.bfloat16)
    return pl.pallas_call(
        functools.partial(attend_back_kernel, head_dim, block),
        grid=(pairs, seq_len // block),
        in_specs=[
            pl.BlockSpec(memory_space=pltpu.SMEM),
            pl.BlockSpec((per, 1, span), lambda p, b: (p, 0, 0)),
            pl.BlockSpec((block, LANES), part),
            pl.BlockSpec((seq_len, LANES), lambda p, b: (0, pairs + p)),
            pl.BlockSpec((seq_len, LANES), lambda p, b: (0, 2 * pairs + p)),
            pl.BlockSpec((block, LANES), part),
            pl.BlockSpec((per, 1, block), lambda p, b: (p, 0, b)),
        ],
        out_specs=[
            pl.BlockSpec((block, LANES), part),
            pl.BlockSpec((seq_len, LANES), whole),
            pl.BlockSpec((seq_len, LANES), whole),
            pl.BlockSpec((per, 1, span), lambda p, b: (p, 0, 0)),
        ],
        out_shape=[flat, flat, flat, jax.ShapeDtypeStruct(diag.shape, jnp.float32)],
        scratch_shapes=[
            pltpu.VMEM((per, span, LANES), jnp.float32),
            pltpu.VMEM((per, seq_len, LANES), jnp.bfloat16),
            pltpu.VMEM((per, span, LANES), jnp.float32),
            pltpu.VMEM((seq_len, LANES), jnp.float32),
            pltpu.VMEM((seq_len, LANES), jnp.float32),
        ],
        compiler_params=pltpu.CompilerParams(vmem_limit_bytes=VMEM_LIMIT),
        cost_estimate=pl.CostEstimate(flops=flops, bytes_accessed=16 * seq_len * cols, transcendentals=0),
        name="attend_back",
    )(length, diag, qkv, qkv, qkv, grad_mixed, lse)


def gated_values(gate, up, grad):
    square = gate * gate
    turn = jnp.tanh(gelu_scale * gate * (1.0 + gelu_cubic * square))
    half = 0.5 * (1.0 + turn)
    act = gate * half
    slope = half + 0.5 * gate * (1.0 - turn * turn) * gelu_scale * (1.0 + 3.0 * gelu_cubic * square)
    low = jnp.bfloat16
    return (grad * up * slope).astype(low), (grad * act).astype(low), (act * up).astype(low)


def ring_order(count):
    if count % 4 or count < 8:
        return list(range(count))
    long, short = 4, count // 4
    walk = []
    for line in range(long):
        columns = range(1, short) if line % 2 == 0 else range(short - 1, 0, -1)
        walk += [line * short + column for column in columns]
    return walk + [line * short for line in range(long - 1, -1, -1)]


MESH = pl.DeviceIdType.MESH


def pick(options, at):
    value = jnp.int32(options[0])
    for index in range(1, len(options)):
        value = jnp.where(at == index, jnp.int32(options[index]), value)
    return value


class Links:
    def __init__(self, count, planes):
        order = ring_order(count)
        place = [0] * count
        for at, index in enumerate(order):
            place[index] = at
        self.count, self.order, self.planes = count, order, planes
        self.place = pick(place, lax.axis_index("dp"))
        seq = lax.axis_index("seq")
        self.core = seq % 2
        self.plane = seq // 2
        self.sibling = {"seq": self.plane * 2 + 1 - self.core}
        self.across = {"seq": (1 - self.plane) * 2 + self.core}
        self.diagonal = {"seq": (1 - self.plane) * 2 + 1 - self.core}
        self.ahead = {"dp": self.owner(1)}
        self.behind = {"dp": self.owner(-1)}

    def owner(self, shift):
        return pick(self.order, lax.rem(self.place + shift + self.count, self.count))

    def greet(self, diagonal=False):
        barrier = pltpu.get_barrier_semaphore()
        friends = [self.ahead, self.behind, self.sibling] + ([self.across] if self.planes == 2 else [])
        if diagonal:
            friends.append(self.diagonal)
        for friend in friends:
            pl.semaphore_signal(barrier, inc=1, device_id=friend, device_id_type=MESH)
        pl.semaphore_wait(barrier, len(friends))


class Gather:
    def __init__(self, links, shard, whole, sems, rows, share):
        self.links, self.shard, self.whole, self.sems, self.rows = links, shard, whole, sems, rows
        self.far = links.count // 2
        self.shared = links.planes == 2
        self.share = share
        self.size = rows - share if self.shared else rows
        self.cut = -(-(self.size // 2) // 16) * 16

    def base(self, shift):
        start = self.links.owner(shift) * self.rows
        if self.shared:
            start = start + self.links.plane * self.share
        return pl.multiple_of(start, 16)

    def ring_copy(self, step, forward):
        shift = (1 - step) if forward else (step - 1)
        offset, size = 0, self.size
        if step == self.far:
            offset, size = (0, self.cut) if forward else (self.cut, self.size - self.cut)
        place = self.whole.at[pl.ds(pl.multiple_of(self.base(shift) + offset, 16), size)]
        source = place
        if step == 1:
            first = self.links.plane * self.share if self.shared else 0
            source = self.shard.at[pl.ds(pl.multiple_of(first + offset, 16), size)]
        return pltpu.make_async_remote_copy(
            src_ref=source,
            dst_ref=place,
            send_sem=self.sems.at[0 if forward else 1, step],
            recv_sem=self.sems.at[2 if forward else 3, step],
            device_id=self.links.ahead if forward else self.links.behind,
            device_id_type=MESH,
        )

    def recv_copy(self, step, forward):
        shift = -step if forward else step
        offset, size = 0, self.size
        if step == self.far:
            offset, size = (0, self.cut) if forward else (self.cut, self.size - self.cut)
        place = self.whole.at[pl.ds(pl.multiple_of(self.base(shift) + offset, 16), size)]
        return pltpu.make_async_remote_copy(
            src_ref=place,
            dst_ref=place,
            send_sem=self.sems.at[0 if forward else 1, step],
            recv_sem=self.sems.at[2 if forward else 3, step],
            device_id=self.links.ahead if forward else self.links.behind,
            device_id_type=MESH,
        )

    def across_copy(self, slot, shift, receive):
        plane = 1 - self.links.plane if receive else self.links.plane
        start = self.links.owner(shift) * self.rows + plane * (self.rows - self.share)
        place = self.whole.at[pl.ds(pl.multiple_of(start, 16), self.share)]
        return pltpu.make_async_remote_copy(
            src_ref=place,
            dst_ref=place,
            send_sem=self.sems.at[4, slot],
            recv_sem=self.sems.at[5, slot],
            device_id=self.links.across,
            device_id_type=MESH,
        )

    def start(self):
        self.ring_copy(1, True).start()
        self.ring_copy(1, False).start()

    def advance(self, step):
        last = step == self.far
        for forward in (True, False):
            self.recv_copy(step, forward).wait_recv()
            if not last:
                self.ring_copy(step + 1, forward).start()
            if self.shared and not last:
                slot = 2 * step - 2 + (0 if forward else 1)
                self.across_copy(slot, -step if forward else step, False).start()
        if self.shared and last:
            self.across_copy(2 * step - 2, step, False).start()

    def slots(self):
        shifts = []
        for step in range(1, self.far):
            shifts += [(2 * step - 2, -step), (2 * step - 1, step)]
        return shifts + [(2 * self.far - 2, self.far)]

    def finish(self):
        for step in range(1, self.far + 1):
            self.ring_copy(step, True).wait_send()
            self.ring_copy(step, False).wait_send()
        if self.shared:
            for slot, shift in self.slots():
                self.across_copy(slot, shift, False).wait_send()
                self.across_copy(slot, shift, True).wait_recv()


def gather_kernel(
    count, planes, rows, shard, small, tokens, cotangent,
    whole, smalls, tokens_there, cotangent_there, items,
    sems, sems_small, sems_core, own, item_sems,
):
    links = Links(count, planes)
    micro = tokens.shape[0]
    split = planes == 2 and tokens.shape[1] == 2
    plane, rank = links.plane, 2 * links.plane + links.core
    keep = pltpu.make_async_copy(shard, whole.at[pl.ds(pl.multiple_of(links.owner(0) * rows, 16), rows)], own.at[0])
    keep_small = pltpu.make_async_copy(small, smalls.at[pl.ds(pl.multiple_of(links.owner(0) * 16, 16), 16)], own.at[1])
    starts = [keep, keep_small]
    if split:
        starts += [pltpu.make_async_copy(tokens.at[m, plane], items.at[m, rank], own.at[2 + m]) for m in range(micro)]
    for copy in starts:
        copy.start()
    links.greet()
    large = Gather(links, shard, whole, sems, rows, 16)
    little = SmallGather(links, small, smalls, sems_small)
    little.start()
    large.start()

    def item_copy(kind, m):
        source, place, device = (
            (tokens.at[m, 1 - plane], rank, links.across),
            (tokens.at[m, plane], rank, links.sibling),
            (items.at[m, rank_across], rank_across, links.sibling),
        )[kind]
        return pltpu.make_async_remote_copy(
            src_ref=source, dst_ref=items.at[m, place], send_sem=item_sems.at[kind, m, 0],
            recv_sem=item_sems.at[kind, m, 1], device_id=device, device_id_type=MESH,
        )

    rank_across = 2 * (1 - plane) + links.core
    if split:
        for kind in range(2):
            for m in range(micro):
                item_copy(kind, m).start()
    swaps = []
    for at, (source, target) in enumerate(((tokens, tokens_there), (cotangent, cotangent_there))):
        swaps.append(
            pltpu.make_async_remote_copy(
                src_ref=source, dst_ref=target, send_sem=sems_core.at[at, 0], recv_sem=sems_core.at[at, 1],
                device_id=links.sibling, device_id_type=MESH,
            )
        )
        swaps[-1].start()
    for step in range(1, large.far + 1):
        little.advance(step)
        large.advance(step)
    if split:
        for m in range(micro):
            item_copy(0, m).wait_recv()
            item_copy(2, m).start()
    for swap in swaps:
        swap.wait()
    little.finish()
    large.finish()
    if split:
        for m in range(micro):
            item_copy(0, m).wait_send()
            for kind in range(1, 3):
                item_copy(kind, m).wait()
    for copy in starts:
        copy.wait()


class SmallGather(Gather):
    def __init__(self, links, shard, whole, sems):
        self.links, self.shard, self.whole, self.sems, self.rows = links, shard, whole, sems, 16
        self.far, self.shared, self.size, self.cut = links.count // 2, False, 16, 16

    def start(self):
        self.ring_copy(1, True).start()
        self.ring_copy(1, False).start()

    def advance(self, step):
        self.recv_copy(step, True).wait_recv()
        if step < self.far:
            self.ring_copy(step + 1, True).start()
            self.recv_copy(step, False).wait_recv()
            if step + 1 < self.far:
                self.ring_copy(step + 1, False).start()

    def finish(self):
        for step in range(1, self.far + 1):
            self.ring_copy(step, True).wait_send()
            if step < self.far:
                self.ring_copy(step, False).wait_send()


def gather_first(shard, small, tokens, cotangent, count, planes):
    rows, cols = shard.shape
    micro, _, local, depth = tokens.shape
    anywhere = pl.BlockSpec(memory_space=pl.ANY)
    dma = pltpu.SemaphoreType.DMA
    return pl.pallas_call(
        functools.partial(gather_kernel, count, planes, rows),
        in_specs=[anywhere] * 4,
        out_specs=[anywhere] * 5,
        out_shape=[
            jax.ShapeDtypeStruct((count * rows, cols), shard.dtype),
            jax.ShapeDtypeStruct((count * 16, small.shape[1]), small.dtype),
            jax.ShapeDtypeStruct(tokens.shape, tokens.dtype),
            jax.ShapeDtypeStruct(cotangent.shape, cotangent.dtype),
            jax.ShapeDtypeStruct((micro, 2 * planes, local, depth), tokens.dtype),
        ],
        scratch_shapes=[dma((6, count)), dma((4, count)), dma((2, 2)), dma((2 + micro,)), dma((3, micro, 2))],
        compiler_params=pltpu.CompilerParams(collective_id=0, has_side_effects=True),
        name="gather_first",
    )(shard, small, tokens, cotangent)


class Scatter:
    def __init__(self, links, grads, inbox, totals, mine, came, made, total, send_sems, recv_sems, near_sems, total_sems, rows):
        self.links, self.grads, self.inbox, self.totals = links, grads, inbox, totals
        self.mine, self.came, self.made, self.total = mine, came, made, total
        self.send_sems, self.recv_sems, self.near_sems, self.total_sems = send_sems, recv_sems, near_sems, total_sems
        self.rows = rows
        self.base = 0
        self.far = links.count // 2
        self.cut = -(-(rows // 2) // 16) * 16
        self.spaces = made.shape[0]

    def part(self, step, way):
        if step > 1:
            return 0, self.rows
        return (0, self.cut) if way == 0 else (self.cut, self.rows - self.cut)

    def term(self, chunk, shift, offset, size):
        start = self.links.owner(shift) * self.rows + offset
        return self.grads.at[chunk + self.base, pl.ds(pl.multiple_of(start, 16), size)]

    def hop(self, chunk, step, way):
        offset, size = self.part(step, way)
        if step == 1:
            source = self.term(chunk, self.far, offset, size)
        else:
            source = self.made.at[lax.rem(chunk, self.spaces), way, pl.ds(offset, size)]
        return pltpu.make_async_remote_copy(
            src_ref=source,
            dst_ref=self.inbox.at[chunk, way, step - 1, pl.ds(offset, size)],
            send_sem=self.send_sems.at[chunk, way, step - 1],
            recv_sem=self.recv_sems.at[chunk, way, step - 1],
            device_id=self.links.behind if way else self.links.ahead,
            device_id_type=MESH,
        )

    def near(self, chunk, step, way):
        offset, size = self.part(step, way)
        space = lax.rem(chunk, self.spaces)
        shift = (step - self.far) if way else (self.far - step)
        copies = [
            pltpu.make_async_copy(
                self.inbox.at[chunk, way, step - 1, pl.ds(offset, size)],
                self.came.at[space, way, pl.ds(offset, size)],
                self.near_sems.at[space, way, 0],
            )
        ]
        if step < self.far or way == 0:
            copies.append(
                pltpu.make_async_copy(
                    self.term(chunk, shift, 0, self.rows), self.mine.at[space, way], self.near_sems.at[space, way, 1]
                )
            )
        return copies

    def start(self, chunk):
        for way in range(2):
            self.hop(chunk, 1, way).start()

    def fetch(self, chunk, step):
        for way in range(2):
            self.hop(chunk, step, way).wait_recv()
            for copy in self.near(chunk, step, way):
                copy.start()

    def pass_on(self, chunk, step):
        space = lax.rem(chunk, self.spaces)
        for way in range(2):
            for copy in self.near(chunk, step, way):
                copy.wait()
            self.hop(chunk, step, way).wait_send()
            offset, size = self.part(step, way)
            rows = pl.ds(offset, size)
            if size < self.rows:
                other = pl.ds(0 if way else size, self.rows - size)
                self.made[space, way, other] = self.mine[space, way, other]
            self.made[space, way, rows] = add_low(self.mine[space, way, rows], self.came[space, way, rows])
            self.hop(chunk, step + 1, way).start()

    def total_copy(self, chunk):
        return pltpu.make_async_copy(self.total, self.totals.at[chunk], self.total_sems.at[0])

    def close(self, chunk):
        space = lax.rem(chunk, self.spaces)
        for way in range(2):
            for copy in self.near(chunk, self.far, way):
                copy.wait()
            self.hop(chunk, self.far, way).wait_send()

        @pl.when(chunk > 0)
        def _():
            self.total_copy(chunk - 1).wait()

        total = self.mine[space, 0].astype(jnp.float32) + self.came[space, 0].astype(jnp.float32)
        self.total[...] = (total + self.came[space, 1].astype(jnp.float32)).astype(self.total.dtype)
        self.total_copy(chunk).start()


def feed_kernel(plan, *refs):
    count, planes, rows, chunks, early, inside, micro, tile, block, groups = plan
    late = chunks - early
    normed = refs[:micro]
    (down, *rest) = refs[micro:]
    ready, shards = rest[:early], rest[early:chunks]
    rest = rest[chunks:]
    back_kept, back_got, out_kept, out_got, totals, pieces, grads, inbox = rest[:8]
    wholes = rest[8 : 8 + late]
    (
        a_all, b_all, weights, piece, stage, mine, came, made, total, out_stage,
        in_sems, piece_sems, stage_sems, fetch_sems, keep_sems, give_sems, take_sems,
        send_sems, recv_sems, near_sems, total_sems, own_sems, *gather_sems,
    ) = rest[8 + late :]
    tokens, depth = a_all.shape
    width = weights.shape[2] // 3
    tiles, blocks = tokens // tile, depth // block
    per = tiles + blocks
    front = chunks * per
    links = Links(count, planes)
    far = count // 2

    loads = [pltpu.make_async_copy(down, b_all, in_sems.at[chunks])]
    for m in range(micro):
        share = tokens // micro
        loads.append(pltpu.make_async_copy(normed[m], a_all.at[pl.ds(m * share, share)], in_sems.at[chunks + 1 + m]))
    loads += [pltpu.make_async_copy(ready[n], weights.at[n], in_sems.at[n]) for n in range(early)]
    keeps = []
    for n in range(late):
        place = wholes[n].at[pl.ds(pl.multiple_of(links.owner(0) * rows, 16), rows)]
        keeps.append(pltpu.make_async_copy(shards[n], place, own_sems.at[n]))
    for copy in loads + keeps:
        copy.start()
    links.greet()
    gathers = [Gather(links, shards[n], wholes[n], gather_sems[n], rows, rows // 3) for n in range(late)]
    scatter = Scatter(
        links, grads, inbox, totals, mine, came, made, total, send_sems, recv_sems, near_sems, total_sems, rows
    )
    for copy in loads[: 1 + micro]:
        copy.wait()

    gap_gather = max(1, 16 // far)
    gap = max(2, 20 // far)

    def load_weights(n):
        source = ready[n] if n < early else wholes[n - early]
        return pltpu.make_async_copy(source, weights.at[n], in_sems.at[n])

    def piece_copy(n, t):
        place = pl.ds(pl.multiple_of(t * tile, 16), tile)
        return pltpu.make_async_copy(piece.at[place], pieces.at[n, place], piece_sems.at[t])

    def stage_copy(n, b):
        slot = lax.rem(b, 2)
        place = pl.ds(pl.multiple_of(b * block, 16), block)
        return pltpu.make_async_copy(stage.at[slot], grads.at[n, place], stage_sems.at[slot])

    def back_rows(g, half):
        start = (2 * g + half) * tile
        return pl.ds(pl.multiple_of(start, 16), tile)

    def fetch_copy(n, t):
        half = jnp.where(lax.rem(t, 2) == 0, 1 - links.core, links.core)
        slot = lax.rem(t, 2)
        target = pl.ds(pl.multiple_of((slot * chunks + n) * tile, 16), tile)
        return pltpu.make_async_copy(pieces.at[n, back_rows(t // 2, half)], piece.at[target], fetch_sems.at[slot, n])

    def give_copy(kind, g):
        target = (back_got, out_got)[kind]
        return pltpu.make_async_remote_copy(
            src_ref=out_stage.at[kind, 0], dst_ref=target.at[g], send_sem=give_sems.at[kind], recv_sem=take_sems.at[kind, g],
            device_id=links.sibling, device_id_type=MESH,
        )

    def keep_copy(kind, g):
        target = (back_kept, out_kept)[kind]
        return pltpu.make_async_copy(out_stage.at[kind, 1], target.at[g], keep_sems.at[kind])

    items_back = 4 * groups
    last_event = per * inside + 1 + gap * far
    total_items = max(front + items_back, last_event + 1)

    def item(i, carry):
        n, j = i // per, lax.rem(i, per)

        for k in range(late):
            base = k * per
            for step in range(far + 2):

                @pl.when(i == base + step * gap_gather)
                def _(k=k, step=step):
                    if step == 0:
                        gathers[k].start()
                    elif step <= far:
                        gathers[k].advance(step)
                    else:
                        gathers[k].finish()
                        keeps[k].wait()
                        load_weights(early + k).start()

        def event(offset, act):
            past = i - per - offset

            @pl.when((past >= 0) & (past < inside * per) & (lax.rem(past + per * 64, per) == 0))
            def _():
                act(past // per)

        def begin(chunk):
            for b in (blocks - 2, blocks - 1):
                stage_copy(chunk, b).wait()
            scatter.start(chunk)

        event(0, begin)
        for step in range(1, far + 1):
            event(step * gap - 1, lambda chunk, step=step: scatter.fetch(chunk, step))
            if step < far:
                event(step * gap, lambda chunk, step=step: scatter.pass_on(chunk, step))
            else:
                event(step * gap, scatter.close)

        @pl.when((i < front) & (j == 0))
        def _():
            for m in range(chunks):

                @pl.when(n == m)
                def _(m=m):
                    load_weights(m).wait()

        @pl.when((i < front) & (j < tiles))
        def _():
            @pl.when(n > 0)
            def _():
                piece_copy(n - 1, j).wait()

            place = pl.ds(pl.multiple_of(j * tile, 16), tile)
            a, d = a_all[place], b_all[place]
            gate = dot32(a, weights[n, :, :width], NN)
            up = dot32(a, weights[n, :, width : 2 * width], NN)
            grad = dot32(d, weights[n, :, 2 * width :], NN)
            d_gate, d_up, hidden = gated_values(gate, up, grad)
            piece[place, :width] = d_gate
            piece[place, width : 2 * width] = d_up
            piece[place, 2 * width :] = hidden
            piece_copy(n, j).start()

        @pl.when((i < front) & (j >= tiles))
        def _():
            b = j - tiles

            @pl.when(b >= 2)
            def _():
                stage_copy(n, b - 2).wait()

            place = pl.ds(pl.multiple_of(b * block, LANES), block)
            slot = lax.rem(b, 2)
            first = dot32(a_all[:, place], piece[:, : 2 * width], TN)
            stage[slot, :, : 2 * width] = first.astype(stage.dtype)
            second = dot32(b_all[:, place], piece[:, 2 * width :], TN)
            stage[slot, :, 2 * width :] = second.astype(stage.dtype)
            stage_copy(n, b).start()

        @pl.when(i == front)
        def _():
            if inside < chunks:
                for b in (blocks - 2, blocks - 1):
                    stage_copy(chunks - 1, b).wait()
            for t in range(tiles):
                piece_copy(chunks - 1, t).wait()
            for m in range(chunks):
                fetch_copy(m, 0).start()

        at = i - front
        t, kind_at = at // 2, lax.rem(at + 2 * per, 2)
        for kind in range(2):

            @pl.when((at >= 0) & (at < items_back) & (kind_at == kind))
            def _(kind=kind):
                slot, g = lax.rem(t, 2), t // 2
                if kind == 0:
                    for m in range(chunks):
                        fetch_copy(m, t).wait()

                    @pl.when(t + 1 < 2 * groups)
                    def _():
                        for m in range(chunks):
                            fetch_copy(m, t + 1).start()

                columns = slice(0, 2 * width) if kind == 0 else slice(2 * width, 3 * width)
                made_sum = None
                for m in range(chunks):
                    place = pl.ds(pl.multiple_of((slot * chunks + m) * tile, 16), tile)
                    term = dot32(piece[place, columns], weights[m, :, columns], NT)
                    made_sum = term if made_sum is None else made_sum + term

                @pl.when((t >= 2) & (slot == 0))
                def _():
                    give_copy(kind, g - 1).wait_send()

                @pl.when((t >= 2) & (slot == 1))
                def _():
                    keep_copy(kind, g - 1).wait()

                out_stage[kind, slot] = made_sum.astype(out_stage.dtype)

                @pl.when(slot == 0)
                def _():
                    give_copy(kind, g).start()

                @pl.when(slot == 1)
                def _():
                    keep_copy(kind, g).start()

        return carry

    lax.fori_loop(0, total_items, item, 0)
    scatter.total_copy(inside - 1).wait()
    for kind in range(2):
        give_copy(kind, groups - 1).wait_send()
        keep_copy(kind, groups - 1).wait()
        for g in range(groups):
            give_copy(kind, g).wait_recv()


def feed(normed, down, ready, shards, count, planes, tile, inside):
    tokens, depth = down.shape
    micro = len(normed)
    rows, cols = shards[0].shape
    early, chunks = len(ready), len(ready) + len(shards)
    far = count // 2
    block = 384
    groups = tokens // (2 * tile)
    spaces = 2 if far <= 4 else chunks
    plan = (count, planes, rows, chunks, early, inside, micro, tile, block, groups)
    anywhere = pl.BlockSpec(memory_space=pl.ANY)
    low = jnp.bfloat16
    part = jax.ShapeDtypeStruct((groups, tile, depth), low)
    shapes = [part] * 4 + [
        jax.ShapeDtypeStruct((inside, rows, cols), low),
        jax.ShapeDtypeStruct((chunks, tokens, cols), low),
        jax.ShapeDtypeStruct((chunks, depth, cols), low),
        jax.ShapeDtypeStruct((chunks, 2, far, rows, cols), low),
    ]
    shapes += [jax.ShapeDtypeStruct((depth, cols), low)] * len(shards)
    dma = pltpu.SemaphoreType.DMA
    made = pl.pallas_call(
        functools.partial(feed_kernel, plan),
        in_specs=[anywhere] * (1 + micro + chunks),
        out_specs=[anywhere] * len(shapes),
        out_shape=shapes,
        scratch_shapes=[
            pltpu.VMEM((tokens, depth), low),
            pltpu.VMEM((tokens, depth), low),
            pltpu.VMEM((chunks, depth, cols), low),
            pltpu.VMEM((tokens, cols), low),
            pltpu.VMEM((2, block, cols), low),
            pltpu.VMEM((spaces, 2, rows, cols), low),
            pltpu.VMEM((spaces, 2, rows, cols), low),
            pltpu.VMEM((spaces, 2, rows, cols), low),
            pltpu.VMEM((rows, cols), low),
            pltpu.VMEM((2, 2, tile, depth), low),
            dma((chunks + 1 + micro,)),
            dma((tokens // tile,)),
            dma((2,)),
            dma((2, chunks)),
            dma((2,)),
            dma((2,)),
            dma((2, groups)),
            dma((chunks, 2, far)),
            dma((chunks, 2, far)),
            dma((spaces, 2, 2)),
            dma((1,)),
            dma((len(shards),)),
        ]
        + [dma((6, count))] * len(shards),
        compiler_params=pltpu.CompilerParams(
            collective_id=1, has_side_effects=True, vmem_limit_bytes=62 * 1024 * 1024
        ),
        cost_estimate=pl.CostEstimate(
            flops=18 * tokens * depth * cols // 3 * chunks, bytes_accessed=10 * tokens * depth, transcendentals=0
        ),
        name="feed",
    )(*normed, down, *ready, *shards)
    return (*made[:5], made[6])


def mix_ahead_kernel(
    plan, len_ref, diag_ref, made, shard, shard_2, mixes, there, lse_ref, whole, whole_2,
    qkv_v, mix_v, strip, keys, in_sems, mix_sems, own_sems, gather_sems, gather_sems_2,
):
    count, planes, rows, head_dim, block = plan
    micro, seq_len, cols = made.shape
    pairs = cols // (3 * LANES)
    plane_len = seq_len // 2
    span = diag_ref.shape[-1]
    per, wide, steps = LANES // head_dim, 3 * LANES, seq_len // block
    units = micro * pairs
    links = Links(count, planes)
    plane = links.plane
    far = count // 2
    lanes_k = lax.broadcasted_iota(jnp.int32, (seq_len, LANES), 1)
    lanes_q = lax.broadcasted_iota(jnp.int32, (block, LANES), 1)

    def at_rows(start, size):
        return pl.ds(pl.multiple_of(start, 16), size)

    def unit_load(u):
        p, m = u // micro, lax.rem(u, micro)
        source = made.at[m, :, pl.ds(pl.multiple_of(p * wide, LANES), wide)]
        return pltpu.make_async_copy(source, qkv_v.at[lax.rem(u, 2)], in_sems.at[lax.rem(u, 2)])

    def columns(p):
        return pl.ds(pl.multiple_of(p * LANES, LANES), LANES)

    def mix_copies(u):
        p, m, slot = u // micro, lax.rem(u, micro), lax.rem(u, 2)
        mine = mix_v.at[slot, at_rows(plane * plane_len, plane_len)]
        near = pltpu.make_async_copy(mine, mixes.at[m, plane, :, columns(p)], mix_sems.at[0, slot])
        beside = pltpu.make_async_remote_copy(
            src_ref=mine, dst_ref=there.at[m, plane, :, columns(p)], send_sem=mix_sems.at[1, slot],
            recv_sem=mix_sems.at[2, u], device_id=links.sibling, device_id_type=MESH,
        )
        far_away = pltpu.make_async_remote_copy(
            src_ref=mix_v.at[slot, at_rows((1 - plane) * plane_len, plane_len)],
            dst_ref=mixes.at[m, plane, :, columns(p)], send_sem=mix_sems.at[3, slot],
            recv_sem=mix_sems.at[4, u], device_id=links.across, device_id_type=MESH,
        )
        return near, beside, far_away

    def forward_copy(u):
        p, m = u // micro, lax.rem(u, micro)
        return pltpu.make_async_remote_copy(
            src_ref=mixes.at[m, 1 - plane, :, columns(p)], dst_ref=there.at[m, 1 - plane, :, columns(p)],
            send_sem=mix_sems.at[5, u], recv_sem=mix_sems.at[6, u], device_id=links.sibling, device_id_type=MESH,
        )

    def forward(u):
        p, m = u // micro, lax.rem(u, micro)
        arrived = pltpu.make_async_remote_copy(
            src_ref=mixes.at[m, 1 - plane, :, columns(p)], dst_ref=mixes.at[m, 1 - plane, :, columns(p)],
            send_sem=mix_sems.at[3, 0], recv_sem=mix_sems.at[4, u], device_id=links.across, device_id_type=MESH,
        )
        arrived.wait_recv()
        forward_copy(u).start()

    pairs_of = ((shard, whole, gather_sems), (shard_2, whole_2, gather_sems_2))
    keeps = [
        pltpu.make_async_copy(source, target.at[at_rows(links.owner(0) * rows, rows)], own_sems.at[k])
        for k, (source, target, _) in enumerate(pairs_of)
    ]
    for keep in keeps:
        keep.start()
    unit_load(jnp.int32(0)).start()
    links.greet()
    gathers = [Gather(links, source, target, sems, rows, rows // 4) for source, target, sems in pairs_of]
    gathers[0].start()
    spacing = units * steps // (2 * far)

    def item(i, carry):
        u, b = i // steps, lax.rem(i, steps)
        p, m, slot = u // micro, lax.rem(u, micro), lax.rem(u, 2)

        for step in range(1, 2 * far):

            @pl.when(i == step * spacing)
            def _(step=step):
                if step <= far:
                    gathers[0].advance(step)
                if step == far - 1:
                    gathers[1].start()
                if step > far:
                    gathers[1].advance(step - far)

        @pl.when(b == 0)
        def _():
            unit_load(u).wait()

            @pl.when(u + 1 < units)
            def _():
                unit_load(u + 1).start()

            @pl.when(u >= 2)
            def _():
                near, beside, far_away = mix_copies(u - 2)
                near.wait()
                beside.wait_send()
                far_away.wait_send()
                forward(u - 2)

            @pl.when(m == 0)
            def _():
                for head in range(per):
                    strip[head] = toeplitz_strip(diag_ref[p * per + head], span)

            length = len_ref[m]
            for head in range(per):
                here = lanes_k // head_dim == head
                spare = ((head + 1) % per) * head_dim
                keys[head] = with_mask_lane(qkv_v[slot, :, LANES : 2 * LANES], lanes_k, here, spare, length)

        place = at_rows(b * block, block)
        q_now = qkv_v[slot, place, :LANES]
        mixed = None
        for head in range(per):
            here = lanes_q // head_dim == head
            spare = ((head + 1) % per) * head_dim
            query = jnp.where(here, q_now, (lanes_q == spare).astype(q_now.dtype))
            raw = dot32(query, keys[head], NT)
            parts = []
            for sub in range(block // LANES):
                offset = pl.multiple_of(seq_len - LANES - (b * block + sub * LANES), LANES)
                parts.append(raw[sub * LANES : (sub + 1) * LANES] + strip[head, :, pl.ds(offset, seq_len)])
            scores = jnp.concatenate(parts, axis=0)
            top = jnp.max(scores, axis=1, keepdims=True)
            expo = jnp.exp(scores - top)
            total = jnp.sum(expo, axis=1, keepdims=True)
            now = dot32(expo.astype(jnp.bfloat16), qkv_v[slot, :, 2 * LANES :], NN) / total
            mixed = now if mixed is None else jnp.where(here, now, mixed)
            lse = jnp.broadcast_to(top + jnp.log(total), (block, LANES))
            at = m * pairs * per + p * per + head
            lse_ref[at, :, pl.ds(pl.multiple_of(b * block, LANES), block)] = lse.T[:1]
        mix_v[slot, place] = mixed.astype(mix_v.dtype)

        @pl.when(b == steps - 1)
        def _():
            for copy in mix_copies(u):
                copy.start()

        return carry

    lax.fori_loop(0, units * steps, item, 0)
    for u in range(max(0, units - 2), units):
        near, beside, far_away = mix_copies(jnp.int32(u))
        near.wait()
        beside.wait_send()
        far_away.wait_send()
        forward(jnp.int32(u))
    gathers[1].advance(far)
    for gather, keep in zip(gathers, keeps):
        gather.finish()
        keep.wait()
    for u in range(units):
        at = jnp.int32(u)
        mix_copies(at)[1].wait_recv()
        forward_copy(at).wait()


def mix_ahead(made, diag, lengths, shards, rows_of, head_dim, count, planes, block=256):
    micro, seq_len, cols = made.shape
    pairs, per, span = cols // (3 * LANES), LANES // head_dim, diag.shape[-1]
    plane_len, units = seq_len // 2, micro * pairs
    rows, width = shards[0].shape
    plan = (count, planes, rows, head_dim, block)
    anywhere = pl.BlockSpec(memory_space=pl.ANY)
    near = pl.BlockSpec(memory_space=pltpu.VMEM)
    low, f32 = jnp.bfloat16, jnp.float32
    dma = pltpu.SemaphoreType.DMA
    return pl.pallas_call(
        functools.partial(mix_ahead_kernel, plan),
        in_specs=[pl.BlockSpec(memory_space=pltpu.SMEM), near, anywhere, anywhere, anywhere],
        out_specs=[anywhere, anywhere, near, anywhere, anywhere],
        out_shape=[
            jax.ShapeDtypeStruct((micro, rows_of, plane_len, cols // 3), low),
            jax.ShapeDtypeStruct((micro, rows_of, plane_len, cols // 3), low),
            jax.ShapeDtypeStruct((units * per, 1, seq_len), f32),
        ]
        + [jax.ShapeDtypeStruct((count * rows, width), low)] * 2,
        scratch_shapes=[
            pltpu.VMEM((2, seq_len, 3 * LANES), low),
            pltpu.VMEM((2, seq_len, LANES), low),
            pltpu.VMEM((per, LANES, span), f32),
            pltpu.VMEM((per, seq_len, LANES), low),
            dma((2,)),
            dma((7, units)),
            dma((2,)),
            dma((6, count)),
            dma((6, count)),
        ],
        compiler_params=pltpu.CompilerParams(
            collective_id=4, has_side_effects=True, vmem_limit_bytes=VMEM_LIMIT
        ),
        name="mix_ahead",
    )(lengths, diag, made, *shards)


def resid_ahead_kernel(core_ref, own, there, w_own, w_other, tokens, tokens_there, gain, resid_ref, normed_ref):
    resid = jnp.where(pl.program_id(1) == 1, tokens[...], tokens_there[...]).astype(jnp.float32)
    resid = resid + (dot32(own[...], w_own[...], NT) + dot32(there[...], w_other[...], NT))
    root = lax.rsqrt(jnp.mean(resid * resid, axis=-1, keepdims=True) + eps)
    resid_ref[...] = resid
    normed_ref[...] = (resid * root * gain[...]).astype(normed_ref.dtype)


def resid_ahead(mixes, there, w_own, w_other, tokens, tokens_there, gain, core_at):
    groups, tile, depth = tokens.shape
    cols, pair_len = mixes.shape[2], 2 * tile
    mine = pl.BlockSpec((None, tile, depth), lambda g, h, s: (g, 0, 0))
    tall = lambda width: pl.BlockSpec((None, tile, width), lambda g, h, s: (g, lax.rem(s[0] + 1 + h, 2), 0))
    flat = lambda shape: pl.BlockSpec(shape, lambda g, h, s: (0, 0))
    last = pl.BlockSpec((depth, cols), lambda g, h, s: (0, 3))
    return pl.pallas_call(
        resid_ahead_kernel,
        grid_spec=pltpu.PrefetchScalarGridSpec(
            num_scalar_prefetch=1,
            grid=(groups, 2),
            in_specs=[tall(cols), tall(cols), last, last, mine, mine, flat((1, depth))],
            out_specs=[mine, tall(depth)],
        ),
        out_shape=[
            jax.ShapeDtypeStruct((groups, tile, depth), jnp.float32),
            jax.ShapeDtypeStruct((groups, pair_len, depth), jnp.bfloat16),
        ],
        compiler_params=pltpu.CompilerParams(vmem_limit_bytes=VMEM_LIMIT),
        name="resid_ahead",
    )(core_at, mixes, there, w_own, w_other, tokens, tokens_there, gain)


def mix_back_kernel(plan, len_ref, lse_ref, diag_ref, *refs):
    count, planes, rows, micro, rows_of, head_dim, block, pairs = plan
    qkvs, mixed, normed, made_own, made_other, attn_in, last_grads = refs[:7]
    dqkv_own, dqkv_there, dd_ref, totals, attn_there, last_totals, last_inbox = refs[7:14]
    (
        qkv_v, do_v, sums_v, attn_v, mixed_v, normed_v, grads, inbox,
        strip, keys, acc_bias, acc_k, acc_v, mine, came, made, total,
        load_sems, do_sems, attn_sems, dqkv_sems, send_sems, recv_sems, near_sems, total_sems,
        mine_2, came_2, made_2, total_2, send_2, recv_2, near_2, total_sems_2,
    ) = refs[14:]
    seq_len = do_v.shape[1]
    span = diag_ref.shape[-1]
    plane_len = seq_len // 2
    local = attn_in.shape[1]
    steps = seq_len // block
    per = LANES // head_dim
    wide = 3 * LANES
    units = pairs * micro
    links = Links(count, planes)
    far = count // 2
    plane, core = links.plane, links.core
    lanes_k = lax.broadcasted_iota(jnp.int32, (seq_len, LANES), 1)
    lanes_q = lax.broadcasted_iota(jnp.int32, (block, LANES), 1)

    def at_rows(start, size):
        return pl.ds(pl.multiple_of(start, 16), size)

    def do_copies(m):
        at = lambda p, c: do_v.at[m, at_rows((2 * p + c) * local, local)]
        far = []
        for way, (source, row, device) in enumerate(
            (
                (made_other, plane, links.sibling),
                (made_own, 1 - plane, links.across),
                (made_other, 1 - plane, links.diagonal),
            )
        ):
            far.append(
                pltpu.make_async_remote_copy(
                    src_ref=source.at[m * rows_of + row], dst_ref=at(plane, core), send_sem=do_sems.at[m, way],
                    recv_sem=do_sems.at[m, 3 + way], device_id=device, device_id_type=MESH,
                )
            )
        return far, pltpu.make_async_copy(made_own.at[m * rows_of + plane], at(plane, core), do_sems.at[m, 6])

    def attn_far():
        return pltpu.make_async_remote_copy(
            src_ref=attn_in, dst_ref=attn_there, send_sem=attn_sems.at[0], recv_sem=attn_sems.at[1],
            device_id=links.sibling, device_id_type=MESH,
        )

    def attn_loads():
        copies = []
        for m in range(micro):
            for r in range(rows_of):
                for side in range(2):
                    source = (attn_in, attn_there)[side]
                    half = core if side == 0 else 1 - core
                    start = (m * rows_of + r) * 2 * local + half * local
                    at = (m * rows_of + r) * 2 + side
                    copies.append(
                        pltpu.make_async_copy(source.at[m * rows_of + r], attn_v.at[at_rows(start, local)], attn_sems.at[4 + at])
                    )
        return copies

    mixed_load = pltpu.make_async_copy(mixed, mixed_v, attn_sems.at[2])
    normed_load = pltpu.make_async_copy(normed, normed_v, attn_sems.at[3])

    def unit_loads(m, p, slot):
        return [
            pltpu.make_async_copy(
                qkvs.at[m, :, pl.ds(pl.multiple_of((3 * p + part) * LANES, LANES), LANES)],
                qkv_v.at[slot, part],
                load_sems.at[slot, part],
            )
            for part in range(3)
        ]

    def start_unit(u):
        for copy in unit_loads(lax.rem(u, micro), u // micro, lax.rem(u, 2)):
            copy.start()

    def give_copies(u):
        p, m = u // micro, lax.rem(u, micro)
        at = m * rows_of + plane
        target = lambda ref: ref.at[at, :, pl.ds(pl.multiple_of(p * wide, LANES), wide)]
        source = lambda q, c: sums_v.at[p, m, at_rows((2 * q + c) * local, local)]
        far = []
        for way, (q, c, ref, device) in enumerate(
            (
                (plane, 1 - core, dqkv_there, links.sibling),
                (1 - plane, core, dqkv_own, links.across),
                (1 - plane, 1 - core, dqkv_there, links.diagonal),
            )
        ):
            far.append(
                pltpu.make_async_remote_copy(
                    src_ref=source(q, c), dst_ref=target(ref), send_sem=dqkv_sems.at[u, way],
                    recv_sem=dqkv_sems.at[u, 3 + way], device_id=device, device_id_type=MESH,
                )
            )
        return far, pltpu.make_async_copy(source(plane, core), target(dqkv_own), dqkv_sems.at[u, 6])

    start_unit(jnp.int32(0))
    mixed_load.start()
    normed_load.start()
    for m in range(micro):
        do_copies(m)[1].start()
    links.greet(True)
    for m in range(micro):
        for copy in do_copies(m)[0]:
            copy.start()
    attn_far().start()
    scatter = Scatter(
        links, grads, inbox, totals, mine, came, made, total, send_sems, recv_sems, near_sems, total_sems, rows
    )

    last_scatter = Scatter(
        links, last_grads, last_inbox, last_totals, mine_2, came_2, made_2, total_2, send_2, recv_2, near_2,
        total_sems_2, last_totals.shape[1],
    )
    last_scatter.base = last_grads.shape[0] - 1
    last_gap = max(2, 20 // far)
    zero = jnp.int32(0)
    last_scatter.start(zero)

    def weight_grads(group, left, right):
        for at in range(left.shape[1] // 384):
            place = slice(at * 384, (at + 1) * 384)
            made_now = dot32(left[:, place], right, TN)
            grads[group, place] = made_now.astype(grads.dtype)
        scatter.start(jnp.int32(group))

    def grads_out():
        for copy in attn_loads():
            copy.wait()
        mixed_load.wait()
        weight_grads(0, attn_v, mixed_v[...])

    def grads_pair(p):
        if p == 0:
            normed_load.wait()
        right = sums_v[p].reshape(micro * seq_len, wide)
        weight_grads(1 + p, normed_v, right)

    per_pair = micro * steps
    work = pairs * per_pair
    begins = [4] + [per_pair * (p + 1) for p in range(pairs)]
    gap = 1
    last = begins[-1] + 2 * far * gap

    def item(i, carry):
        u, b = i // steps, lax.rem(i, steps)
        p, m = u // micro, lax.rem(u, micro)
        slot = lax.rem(u, 2)

        @pl.when(i == 3)
        def _():
            attn_far().wait_recv()
            for copy in attn_loads():
                copy.start()

        for step in range(1, far + 1):

            @pl.when(i == step * last_gap - 1)
            def _(step=step):
                last_scatter.fetch(zero, step)

            @pl.when(i == step * last_gap)
            def _(step=step):
                if step < far:
                    last_scatter.pass_on(zero, step)
                else:
                    last_scatter.close(zero)

        for group, begin in enumerate(begins):
            g = jnp.int32(group)

            @pl.when(i == begin)
            def _(group=group):
                grads_out() if group == 0 else grads_pair(group - 1)

            for step in range(1, far + 1):

                @pl.when(i == begin + (2 * step - 1) * gap)
                def _(g=g, step=step):
                    scatter.fetch(g, step)

                @pl.when(i == begin + 2 * step * gap)
                def _(g=g, step=step):
                    if step < far:
                        scatter.pass_on(g, step)
                    else:
                        scatter.close(g)

        @pl.when((i < work) & (b == 0))
        def _():
            for copy in unit_loads(m, p, slot):
                copy.wait()

            @pl.when(u + 1 < units)
            def _():
                start_unit(u + 1)

            for k in range(micro):

                @pl.when(u == k)
                def _(k=k):
                    far_copies, near_copy = do_copies(k)
                    near_copy.wait()
                    for copy in far_copies:
                        copy.wait_recv()

            @pl.when(m == 0)
            def _():
                for head in range(per):
                    strip[head] = toeplitz_strip(diag_ref[p * per + head], span).T
                acc_bias[...] = jnp.zeros_like(acc_bias)

            length = len_ref[m]
            for head in range(per):
                here = lanes_k // head_dim == head
                spare = ((head + 1) % per) * head_dim
                keys[head] = with_mask_lane(qkv_v[slot, 1], lanes_k, here, spare, length)
            acc_k[...] = jnp.zeros_like(acc_k)
            acc_v[...] = jnp.zeros_like(acc_v)

        @pl.when(i < work)
        def _():
            place = at_rows(b * block, block)
            q_now = qkv_v[slot, 0, place]
            do_now = do_v[m, place, pl.ds(pl.multiple_of(p * LANES, LANES), LANES)]
            grad_query = None
            for head in range(per):
                here = lanes_q // head_dim == head
                spare = ((head + 1) % per) * head_dim
                blank = jnp.zeros_like(q_now)
                one = (lanes_q == spare).astype(q_now.dtype)
                query = jnp.where(here, q_now, blank)
                grad = jnp.where(here, do_now, blank)
                raw = dot32(keys[head], query + one, NT)
                grad_probs = dot32(qkv_v[slot, 2], grad, NT)
                parts, offsets = [], []
                for sub in range(block // LANES):
                    offset = pl.multiple_of(seq_len - LANES - (b * block + sub * LANES), LANES)
                    offsets.append(offset)
                    parts.append(raw[:, sub * LANES : (sub + 1) * LANES] + strip[head, pl.ds(offset, seq_len), :])
                scores = jnp.concatenate(parts, axis=1)
                lse = lse_ref[m * pairs * per + p * per + head, :, pl.ds(pl.multiple_of(b * block, LANES), block)]
                probs = jnp.exp(scores - lse)
                product = probs * grad_probs
                inner = jnp.sum(product, axis=0, keepdims=True)
                grad_scores = product - probs * inner
                for sub, offset in enumerate(offsets):
                    acc_bias[head, pl.ds(offset, seq_len), :] += grad_scores[:, sub * LANES : (sub + 1) * LANES]
                rounded = grad_scores.astype(jnp.bfloat16)
                acc_v[...] += dot32(probs.astype(jnp.bfloat16), grad, NN)
                acc_k[...] += dot32(rounded, query, NN)
                made_now = dot32(rounded, qkv_v[slot, 1], TN)
                grad_query = made_now if grad_query is None else jnp.where(here, made_now, grad_query)
            sums_v[p, m, place, :LANES] = grad_query.astype(sums_v.dtype)

        @pl.when((i < work) & (b == steps - 1))
        def _():
            sums_v[p, m, :, LANES : 2 * LANES] = acc_k[...].astype(sums_v.dtype)
            sums_v[p, m, :, 2 * LANES :] = acc_v[...].astype(sums_v.dtype)
            far_copies, near_copy = give_copies(u)
            near_copy.start()
            for copy in far_copies:
                copy.start()

            @pl.when(m == micro - 1)
            def _():
                row = lax.broadcasted_iota(jnp.int32, (LANES, LANES), 0)
                col = lax.broadcasted_iota(jnp.int32, (LANES, LANES), 1)
                flip = (row + col == LANES - 1).astype(jnp.float32)
                for head in range(per):
                    turned = lax.dot_general(
                        flip, acc_bias[head], NT, precision=highest, preferred_element_type=jnp.float32
                    )
                    aligned = pltpu.roll(turned, 0, 1, stride=1, stride_axis=0)
                    dd_ref[p * per + head] = jnp.sum(aligned, axis=0, keepdims=True)

        return carry

    lax.fori_loop(0, last + 1, item, 0)
    scatter.total_copy(jnp.int32(pairs)).wait()
    last_scatter.total_copy(zero).wait()
    for m in range(micro):
        for copy in do_copies(m)[0]:
            copy.wait_send()
    attn_far().wait_send()
    for u in range(units):
        far_copies, near_copy = give_copies(jnp.int32(u))
        near_copy.wait()
        for copy in far_copies:
            copy.wait()


def mix_back(qkvs, made_own, made_other, attn_in, mixed, normed, last_grads, lse, diag, lengths, head_dim, count, planes, block=256):
    micro, seq_len, cols = qkvs.shape
    cols = cols // 3
    rows_of = attn_in.shape[0] // micro
    _, local, depth = attn_in.shape
    pairs, per, span = cols // LANES, LANES // head_dim, diag.shape[-1]
    tokens = normed.shape[0]
    chunk_cols = last_grads.shape[2]
    rows, wide, far = depth // count, 3 * LANES, count // 2
    groups = 1 + pairs
    spaces = 2 if far <= 4 else groups
    plan = (count, planes, rows, micro, rows_of, head_dim, block, pairs)
    anywhere = pl.BlockSpec(memory_space=pl.ANY)
    low, f32 = jnp.bfloat16, jnp.float32
    dma = pltpu.SemaphoreType.DMA
    return pl.pallas_call(
        functools.partial(mix_back_kernel, plan),
        in_specs=[pl.BlockSpec(memory_space=pltpu.SMEM)]
        + [pl.BlockSpec(memory_space=pltpu.VMEM)] * 2
        + [anywhere] * 7,
        out_specs=[anywhere, anywhere, pl.BlockSpec(memory_space=pltpu.VMEM)] + [anywhere] * 4,
        out_shape=[
            jax.ShapeDtypeStruct((micro * rows_of, local, 3 * cols), low),
            jax.ShapeDtypeStruct((micro * rows_of, local, 3 * cols), low),
            jax.ShapeDtypeStruct(diag.shape, f32),
            jax.ShapeDtypeStruct((groups, rows, wide), low),
            jax.ShapeDtypeStruct(attn_in.shape, low),
            jax.ShapeDtypeStruct((1, rows, chunk_cols), low),
            jax.ShapeDtypeStruct((1, 2, far, rows, chunk_cols), low),
        ],
        scratch_shapes=[
            pltpu.VMEM((2, 3, seq_len, LANES), low),
            pltpu.VMEM((micro, seq_len, cols), low),
            pltpu.VMEM((pairs, micro, seq_len, wide), low),
            pltpu.VMEM((tokens, depth), low),
            pltpu.VMEM((tokens, cols), low),
            pltpu.VMEM((tokens, depth), low),
            pltpu.VMEM((groups, depth, wide), low),
            pltpu.VMEM((groups, 2, far, rows, wide), low),
            pltpu.VMEM((per, span, LANES), f32),
            pltpu.VMEM((per, seq_len, LANES), low),
            pltpu.VMEM((per, span, LANES), f32),
            pltpu.VMEM((seq_len, LANES), f32),
            pltpu.VMEM((seq_len, LANES), f32),
            pltpu.VMEM((spaces, 2, rows, wide), low),
            pltpu.VMEM((spaces, 2, rows, wide), low),
            pltpu.VMEM((spaces, 2, rows, wide), low),
            pltpu.VMEM((rows, wide), low),
            dma((2, 3)),
            dma((micro, 7)),
            dma((4 + 2 * micro * rows_of,)),
            dma((pairs * micro, 7)),
            dma((groups, 2, far)),
            dma((groups, 2, far)),
            dma((spaces, 2, 2)),
            dma((1,)),
            pltpu.VMEM((1, 2, rows, chunk_cols), low),
            pltpu.VMEM((1, 2, rows, chunk_cols), low),
            pltpu.VMEM((1, 2, rows, chunk_cols), low),
            pltpu.VMEM((rows, chunk_cols), low),
            dma((1, 2, far)),
            dma((1, 2, far)),
            dma((1, 2, 2)),
            dma((1,)),
        ],
        compiler_params=pltpu.CompilerParams(
            collective_id=2, has_side_effects=True, vmem_limit_bytes=62 * 1024 * 1024
        ),
        name="mix_back",
    )(lengths, lse, diag, qkvs, mixed, normed, made_own, made_other, attn_in, last_grads)


def resid_back_kernel(kept, got, out_kept, out_got, resid_ref, cot, gain, w_own, w_other, grad_ref, attn_ref, own_ref, other_ref, out_ref, sum_ref):
    @pl.when(pl.program_id(0) == 0)
    def _():
        sum_ref[...] = jnp.zeros_like(sum_ref)

    wide = jnp.float32
    resid = resid_ref[...]
    out_ref[...] = (resid + (out_kept[...].astype(wide) + out_got[...].astype(wide))).astype(out_ref.dtype)
    grad = kept[...].astype(wide) + got[...].astype(wide)
    root = lax.rsqrt(jnp.mean(resid * resid, axis=-1, keepdims=True) + eps)
    sum_ref[...] += jnp.sum(grad * resid * root, axis=0, keepdims=True)
    scaled = grad * gain[...]
    shared = jnp.mean(scaled * resid, axis=-1, keepdims=True) * root * root * root
    total = cot[...].astype(wide) + scaled * root - resid * shared
    grad_ref[...] = total
    low = total.astype(attn_ref.dtype)
    attn_ref[...] = low
    own_ref[...] = dot32(low, w_own[...], NN).astype(own_ref.dtype)
    other_ref[...] = dot32(low, w_other[...], NN).astype(other_ref.dtype)


def resid_back(kept, got, out_kept, out_got, resid, cotangent, gain, w_own, w_other):
    groups, tile, depth = kept.shape
    cols = w_own.shape[1] // 4
    tall = lambda width: pl.BlockSpec((None, tile, width), lambda g: (g, 0, 0))
    flat = lambda shape: pl.BlockSpec(shape, lambda g: (0, 0))
    low, wide = jnp.bfloat16, jnp.float32
    shape = lambda width, kind: jax.ShapeDtypeStruct((groups, tile, width), kind)
    return pl.pallas_call(
        resid_back_kernel,
        grid=(groups,),
        in_specs=[tall(depth)] * 6 + [flat((1, depth))] + [pl.BlockSpec((depth, cols), lambda g: (0, 3))] * 2,
        out_specs=[tall(depth), tall(depth), tall(cols), tall(cols), tall(depth), flat((1, depth))],
        out_shape=[
            shape(depth, wide), shape(depth, low), shape(cols, low), shape(cols, low), shape(depth, low),
            jax.ShapeDtypeStruct((1, depth), wide),
        ],
        compiler_params=pltpu.CompilerParams(vmem_limit_bytes=VMEM_LIMIT),
        name="resid_back",
    )(kept, got, out_kept, out_got, resid, cotangent, gain, w_own, w_other)


def input_back_kernel(own, there, w_own, w_other, tokens, grad_resid, gain, out_ref, sum_ref):
    @pl.when(pl.program_id(0) == 0)
    def _():
        sum_ref[...] = jnp.zeros_like(sum_ref)

    grad = dot32(own[...], w_own[...], NT) + dot32(there[...], w_other[...], NT)
    values = tokens[...].astype(jnp.float32)
    root = lax.rsqrt(jnp.mean(values * values, axis=-1, keepdims=True) + eps)
    sum_ref[...] += jnp.sum(grad * values * root, axis=0, keepdims=True)
    scaled = grad * gain[...]
    shared = jnp.mean(scaled * values, axis=-1, keepdims=True) * root * root * root
    out_ref[...] = grad_resid[...] + scaled * root - values * shared


def input_back(own, there, w_own, w_other, tokens, grad_resid, gain):
    groups, tile, depth = tokens.shape
    cols = own.shape[2]
    tall = lambda width: pl.BlockSpec((None, tile, width), lambda g: (g, 0, 0))
    flat = lambda shape: pl.BlockSpec(shape, lambda g: (0, 0))
    return pl.pallas_call(
        input_back_kernel,
        grid=(groups,),
        in_specs=[tall(cols), tall(cols), flat((depth, cols)), flat((depth, cols)), tall(depth), tall(depth), flat((1, depth))],
        out_specs=[tall(depth), flat((1, depth))],
        out_shape=[
            jax.ShapeDtypeStruct((groups, tile, depth), jnp.float32), jax.ShapeDtypeStruct((1, depth), jnp.float32)
        ],
        compiler_params=pltpu.CompilerParams(vmem_limit_bytes=VMEM_LIMIT),
        name="input_back",
    )(own, there, w_own, w_other, tokens, grad_resid, gain)


def small_sum_kernel(sizes, x_ref, o_ref, outbox, inbox, send_sems, recv_sems):
    partners = []
    for name, size in sizes:
        at, bit = lax.axis_index(name), 1
        while bit < size:
            partners.append({name: jnp.where(lax.rem(at // bit, 2) == 0, at + bit, at - bit)})
            bit *= 2
    barrier = pltpu.get_barrier_semaphore()
    for partner in partners:
        pl.semaphore_signal(barrier, inc=1, device_id=partner, device_id_type=MESH)
    pl.semaphore_wait(barrier, len(partners))
    o_ref[...] = x_ref[...]
    for at, partner in enumerate(partners):
        outbox[at] = o_ref[...]
        copy = pltpu.make_async_remote_copy(
            src_ref=outbox.at[at], dst_ref=inbox.at[at], send_sem=send_sems.at[at], recv_sem=recv_sems.at[at],
            device_id=partner, device_id_type=MESH,
        )
        copy.start()
        copy.wait()
        o_ref[...] += inbox[at]


def small_sum(values, sizes):
    rounds = sum(size.bit_length() - 1 for _, size in sizes)
    return pl.pallas_call(
        functools.partial(small_sum_kernel, sizes),
        in_specs=[pl.BlockSpec(memory_space=pltpu.VMEM)],
        out_specs=pl.BlockSpec(memory_space=pltpu.VMEM),
        out_shape=jax.ShapeDtypeStruct(values.shape, values.dtype),
        scratch_shapes=[
            pltpu.VMEM((rounds,) + values.shape, values.dtype),
            pltpu.VMEM((rounds,) + values.shape, values.dtype),
            pltpu.SemaphoreType.DMA((rounds,)),
            pltpu.SemaphoreType.DMA((rounds,)),
        ],
        compiler_params=pltpu.CompilerParams(collective_id=3, has_side_effects=True),
        name="small_sum",
    )(values)


class Ring:
    def __init__(self, count):
        order = ring_order(count)
        place = [0] * count
        for at, index in enumerate(order):
            place[index] = at
        self.count = count
        self.order = jnp.array(order, jnp.int32)
        self.here = jnp.array(place, jnp.int32)[lax.axis_index("dp")]
        self.ahead = [(order[i], order[(i + 1) % count]) for i in range(count)]
        self.behind = [(order[i], order[(i - 1) % count]) for i in range(count)]

    def owner(self, shift):
        return self.order[(self.here + shift) % self.count]

    def send(self, block, forward):
        return lax.ppermute(block, "dp", self.ahead if forward else self.behind)

    def gather(self, shard):
        rows, cols = shard.shape
        cut = cols // 2
        far = self.count // 2
        whole = jnp.zeros((self.count * rows, cols), shard.dtype)

        def put(whole, block, shift, column=0):
            return lax.dynamic_update_slice(whole, block, (self.owner(shift) * rows, column))

        whole = put(whole, shard, 0)
        ahead = behind = shard
        for step in range(1, far):
            ahead, behind = self.send(ahead, True), self.send(behind, False)
            whole = put(put(whole, ahead, -step), behind, step)
        last = (ahead, behind)
        ahead, behind = self.send(ahead[:, :cut], True), self.send(behind[:, cut:], False)
        whole = put(put(whole, ahead, -far), behind, far, cut)
        return whole, last

    def scatter(self, local, cols):
        cut = cols // 2
        far = self.count // 2
        most = local(self.owner(far))
        ahead, behind = self.send(most[:, :cut], True), self.send(most[:, cut:], False)
        for step in range(far - 1, 0, -1):
            mine = local(self.owner(step))
            other = local(self.owner(-step))
            if step == far - 1:
                ahead = jnp.concatenate([add_low(mine[:, :cut], ahead), mine[:, cut:]], axis=1)
                behind = jnp.concatenate([other[:, :cut], add_low(other[:, cut:], behind)], axis=1)
            else:
                ahead, behind = add_low(mine, ahead), add_low(other, behind)
            ahead, behind = self.send(ahead, True), self.send(behind, False)
        return local(self.owner(0)).astype(jnp.float32) + ahead.astype(jnp.float32) + behind.astype(jnp.float32)


def add_low(a, b):
    return (a.astype(jnp.float32) + b.astype(jnp.float32)).astype(jnp.bfloat16)


def body(
    tokens, cotangent, lengths, buckets, gain_one, gain_two, table,
    w_query, w_key, w_value, w_out, w_gate, w_up, w_down,
):
    micro, rows, local, width = tokens.shape
    seq_devices = lax.axis_size("seq")
    dp_devices = lax.axis_size("dp")
    seq_rank = lax.axis_index("seq")
    core = seq_rank % 2
    plane = seq_rank // 2
    planes = seq_devices // 2
    heads = table.shape[1]
    shard_rows, inner = w_query.shape
    head_dim = inner // heads
    half_inner = inner // 2
    hidden_units = w_gate.shape[1]
    pair_local = 2 * local
    seq_len = local * seq_devices
    first = core == 0
    core_pairs = [(i, i ^ 1) for i in range(seq_devices)]
    plane_groups = [[2 * p + c for p in range(planes)] for c in range(2)]
    ring = Ring(dp_devices)

    def swap_core(value):
        return lax.ppermute(value, "seq", core_pairs)

    def both_cores(own, other, axis):
        return jnp.concatenate([jnp.where(first, own, other), jnp.where(first, other, own)], axis=axis)

    def own_half(value, axis):
        return lax.dynamic_slice_in_dim(value, core * local, local, axis)

    def other_half(value, axis):
        return lax.dynamic_slice_in_dim(value, (1 - core) * local, local, axis)

    def core_columns(weight, split):
        low, high = weight[:, :split], weight[:, split:]
        high = jnp.pad(high, ((0, 0), (0, split - high.shape[1])))
        return jnp.where(first, low, high)

    chunk = 512
    chunks = -(-(hidden_units // 2) // chunk)
    split = chunks * chunk
    if split > hidden_units:
        split = hidden_units
    fused = planes == 2 and rows == 2 and half_inner % LANES == 0
    attn_parts = [core_columns(w, half_inner) for w in (w_query, w_key, w_value)]
    if fused:
        attn_parts = [w[:, p : p + LANES] for p in range(0, half_inner, LANES) for w in attn_parts]
    attn_shard = jnp.concatenate(attn_parts + [core_columns(w_out.T, half_inner)], axis=1)
    up_parts = [core_columns(w, split) for w in (w_gate, w_up, w_down.T)]
    chunk_shards = [
        jnp.concatenate([w[:, n * chunk : (n + 1) * chunk] for w in up_parts], axis=1) for n in range(chunks)
    ]

    small = jnp.concatenate([gain_one, gain_two, table.reshape(-1)])
    small = jnp.pad(small, (0, -small.shape[0] % LANES))
    small = jnp.pad(small[None], ((0, 15), (0, 0)))
    attn_weights, small, tokens_other, cotangent_other, items = gather_first(
        attn_shard, small, tokens, cotangent, dp_devices, planes
    )
    small = small.reshape(dp_devices, 16, -1)[:, 0].astype(jnp.float32)
    gain_first = small[:, :shard_rows].reshape(-1)
    gain_second = small[:, shard_rows : 2 * shard_rows].reshape(-1)
    full_table = small[:, 2 * shard_rows : 2 * shard_rows + table.size].reshape(-1, heads)
    qkv_cols = 3 * half_inner
    there_weights = swap_core(attn_weights)
    qkv_weights = attn_weights[:, :qkv_cols]
    down_in = both_cores(cotangent, cotangent_other, 2)

    core_heads = heads // 2
    head_splits = planes // rows
    item_heads = core_heads // head_splits
    item_cols = item_heads * head_dim
    padded_cols = -(-item_cols // LANES) * LANES
    padded_heads = padded_cols // head_dim
    item_row = plane // head_splits
    item_group = plane % head_splits
    head_start = core * core_heads + item_group * item_heads
    item_table = lax.dynamic_slice_in_dim(full_table, head_start, item_heads, 1)
    item_table = jnp.pad(item_table, ((0, 0), (0, padded_heads - item_heads)))
    levels = full_table.shape[0]
    bucket_hot = (buckets[:, None] == jnp.arange(levels)[None, :]).astype(jnp.float32)
    bucket_hot = jnp.pad(bucket_hot, ((0, 1), (0, 0)))
    diag = jnp.dot(item_table.T, bucket_hot.T, precision=highest)[:, None, :]

    def to_items(value, parts):
        if planes == 2 and rows == 2:
            mine = lax.dynamic_index_in_dim(value, plane, 0, keepdims=False)
            sent = lax.dynamic_index_in_dim(value, 1 - plane, 0, keepdims=False)
            got = lax.ppermute(sent, "seq", [(i, i ^ 2) for i in range(4)])
            low = plane == 0
            return jnp.concatenate([jnp.where(low, mine, got), jnp.where(low, got, mine)], axis=0)
        value = value.reshape(rows, pair_local, parts, head_splits, item_cols)
        value = value.transpose(0, 3, 1, 2, 4).reshape(planes, pair_local, parts * item_cols)
        value = lax.all_to_all(value, "seq", 0, 0, tiled=True, axis_index_groups=plane_groups)
        value = value.reshape(seq_len, parts, item_cols)
        value = jnp.pad(value, ((0, 0), (0, 0), (0, padded_cols - item_cols)))
        return value.reshape(seq_len, parts * padded_cols)

    def from_items(values):
        parts = len(values)
        if planes == 2 and rows == 2:
            value = jnp.concatenate(values, axis=1)
            mine = lax.dynamic_slice_in_dim(value, plane * pair_local, pair_local, 0)
            sent = lax.dynamic_slice_in_dim(value, (1 - plane) * pair_local, pair_local, 0)
            got = lax.ppermute(sent, "seq", [(i, i ^ 2) for i in range(4)])
            low = plane == 0
            return jnp.stack([jnp.where(low, mine, got), jnp.where(low, got, mine)])
        value = jnp.concatenate([v[:, :item_cols] for v in values], axis=1)
        value = value.reshape(planes, pair_local, parts * item_cols)
        value = lax.all_to_all(value, "seq", 0, 0, tiled=True, axis_index_groups=plane_groups)
        value = value.reshape(rows, head_splits, pair_local, parts, item_cols).transpose(0, 2, 3, 1, 4)
        return value.reshape(rows, pair_local, parts * half_inner)

    rows_in = items.reshape(micro, 1, seq_len, width) if fused else both_cores(tokens, tokens_other, 2)
    rows_in = rows_in.astype(jnp.float32)
    root = lax.rsqrt(jnp.mean(rows_in * rows_in, axis=-1, keepdims=True) + eps)
    normed = lax.optimization_barrier((rows_in * root * gain_first).astype(jnp.bfloat16))
    made = jnp.einsum("mrld,de->mrle", normed, qkv_weights, preferred_element_type=jnp.float32).astype(jnp.bfloat16)
    item_lens = lax.dynamic_slice_in_dim(lengths, item_row, 1, 1)
    if fused:
        qkvs = made[:, 0]
        mixes, mixes_there, lses, *ready = mix_ahead(
            qkvs, diag, item_lens[:, 0], chunk_shards[:2], rows, head_dim, dp_devices, planes
        )
    else:
        qkvs = [to_items(made[step], 3) for step in range(micro)]
        pairs = [attend(qkvs[step], diag, item_lens[step], head_dim) for step in range(micro)]
        lses = [lse for _, lse in pairs]
        mixes = jnp.stack([from_items([mixed]) for mixed, _ in pairs])
        mixes_there = swap_core(mixes)
        ready = [lax.all_gather(shard, "dp", axis=0, tiled=True) for shard in chunk_shards[:2]]
    early = 2
    by_pair = lambda value: value.reshape(micro * rows, pair_local, value.shape[-1])
    by_row = lambda value: value.reshape(micro * rows, local, value.shape[-1])
    resids, normed_two = resid_ahead(
        by_pair(mixes), by_pair(mixes_there), attn_weights, there_weights, by_row(tokens), by_row(tokens_other),
        gain_second[None],
        core.astype(jnp.int32)[None],
    )

    def apart(qkvs, grads_items, lses, item_lens, attn_all, mixed_all, normed_all):
        grads_qkv, diag_sum = [], 0.0
        for step in range(micro):
            grad_q, grad_k, grad_v, grad_diag = attend_back(
                qkvs[step], grads_items[step], lses[step], diag, item_lens[step], head_dim
            )
            diag_sum = diag_sum + grad_diag[:item_heads, 0]
            grads_qkv.append(from_items([grad_q, grad_k, grad_v]))
        grads_all = jnp.concatenate([flat(v) for v in grads_qkv])
        attn_all = flat(both_cores(attn_all, swap_core(attn_all), 2))
        grad_attn = jnp.einsum("td,te->de", normed_all, grads_all, preferred_element_type=jnp.float32)
        grad_o = jnp.einsum("td,te->de", attn_all, mixed_all, preferred_element_type=jnp.float32)
        both = jnp.concatenate([grad_o, grad_attn], axis=1).astype(jnp.bfloat16)
        total = ring.scatter(
            lambda index: lax.dynamic_slice_in_dim(both, index * shard_rows, shard_rows, 0), 4 * half_inner
        )
        return grads_qkv, diag_sum, total

    flat = lambda value: value.reshape(-1, value.shape[-1])
    down_all = flat(down_in)
    inside = chunks - 1 if fused else chunks
    back_kept, back_got, out_kept, out_got, chunk_totals, chunk_grads = feed(
        [flat(normed_two)], down_all, ready, chunk_shards[early:], dp_devices, planes, local, inside
    )
    grad_resid, attn_in, made_own, made_other, output, gain_two_sum = resid_back(
        back_kept, back_got, out_kept, out_got, resids, by_row(cotangent), gain_second[None], attn_weights, there_weights
    )

    if fused:
        own, there, diag_sum, attn_totals, _, last_totals, _ = mix_back(
            qkvs, made_own, made_other, attn_in, flat(mixes), flat(normed), chunk_grads, lses, diag, item_lens[:, 0],
            head_dim, dp_devices, planes,
        )
        input_grad, gain_one_sum = input_back(
            own, there, attn_weights, there_weights, by_row(tokens), grad_resid, gain_first[None]
        )
        diag_sum = diag_sum[:, 0]
    else:
        split_micro = lambda value: value.reshape(micro, rows, local, -1)
        grads_mixed = both_cores(split_micro(made_own), swap_core(split_micro(made_other)), 2)
        grads_qkv, diag_sum, attn_totals = apart(
            qkvs, [to_items(g, 1) for g in grads_mixed], lses, item_lens, split_micro(attn_in), flat(mixes), flat(normed)
        )
        grads_qkv = jnp.stack(grads_qkv)
        own = by_row(own_half(grads_qkv, 2))
        there = swap_core(by_row(other_half(grads_qkv, 2)))
        input_grad, gain_one_sum = input_back(
            own, there, attn_weights, there_weights, by_row(tokens), grad_resid, gain_first[None]
        )
    item_grad = jnp.dot(diag_sum, bucket_hot, precision=highest)
    grad_table = lax.dynamic_update_slice(jnp.zeros((heads, levels), jnp.float32), item_grad, (head_start, 0))

    def finish(total):
        if planes == 2:
            low = total.astype(jnp.bfloat16)
            got = lax.ppermute(low, "seq", [(i, i ^ 2) for i in range(4)])
            total = low.astype(jnp.float32) + got.astype(jnp.float32)
        else:
            total = lax.psum(total.astype(jnp.float32), "seq", axis_index_groups=plane_groups)
        return total, swap_core(total)

    def whole_columns(own, other, size):
        low, high = jnp.where(first, own, other), jnp.where(first, other, own)
        return jnp.concatenate([low, high[:, : size - low.shape[1]]], axis=1)

    own, other = finish(attn_totals)
    if fused:
        grad_out = whole_columns(own[0], other[0], inner)
        grad_query, grad_key, grad_value = [
            whole_columns(
                jnp.concatenate(list(own[1:, :, part * LANES : (part + 1) * LANES]), axis=1),
                jnp.concatenate(list(other[1:, :, part * LANES : (part + 1) * LANES]), axis=1),
                inner,
            )
            for part in range(3)
        ]
    else:
        parts = [slice(i * half_inner, (i + 1) * half_inner) for i in range(4)]
        grad_out, grad_query, grad_key, grad_value = [whole_columns(own[:, p], other[:, p], inner) for p in parts]
    own, other = finish(chunk_totals)
    done = [(own[n], other[n]) for n in range(inside)]
    if fused:
        own, other = finish(last_totals)
        done.append((own[0], other[0]))
    parts = [slice(i * chunk, (i + 1) * chunk) for i in range(3)]
    grad_gate, grad_up, grad_down = [
        whole_columns(
            jnp.concatenate([own[:, p] for own, _ in done], axis=1),
            jnp.concatenate([other[:, p] for _, other in done], axis=1),
            hidden_units,
        )
        for p in parts
    ]

    dp_rank = lax.axis_index("dp")
    small = jnp.concatenate([gain_one_sum[0], gain_two_sum[0], grad_table.T.reshape(-1)])
    small = jnp.pad(small, (0, -small.shape[0] % (8 * LANES))).reshape(-1, LANES)
    small = small_sum(small, (("seq", seq_devices), ("dp", dp_devices))).reshape(-1)
    grad_gain_one = lax.dynamic_slice_in_dim(small, dp_rank * shard_rows, shard_rows, 0)
    grad_gain_two = lax.dynamic_slice_in_dim(small, width + dp_rank * shard_rows, shard_rows, 0)
    table_part = levels // dp_devices
    grad_table = lax.dynamic_slice_in_dim(small[2 * width : 2 * width + levels * heads].reshape(levels, heads), dp_rank * table_part, table_part, 0)

    return (
        output.reshape(tokens.shape), input_grad.reshape(tokens.shape), grad_gain_one, grad_gain_two, grad_table,
        grad_query, grad_key, grad_value, grad_out.T, grad_gate, grad_up, grad_down.T,
    )


def solution(mesh):
    weight, turned = P("dp", None), P(None, "dp")
    return jax.shard_map(
        body,
        mesh=mesh,
        in_specs=(
            P(None, "dp", "seq", None), P(None, "dp", "seq", None), P(None, "dp"), P(), P("dp"), P("dp"),
            weight, weight, weight, weight, turned, weight, weight, turned,
        ),
        out_specs=(
            P(None, "dp", "seq", None), P(None, "dp", "seq", None), P("dp"), P("dp"),
            weight, weight, weight, weight, turned, weight, weight, turned,
        ),
        check_vma=False,
    )
```

```python
import functools

import jax
import jax.numpy as jnp
from jax import lax
from jax.experimental import pallas as pl
from jax.experimental.pallas import tpu as pltpu
from jax.sharding import PartitionSpec as P

eps = 1e-06
masked_value = -1e30
highest = lax.Precision.HIGHEST
gelu_scale = 0.7978845608028654
gelu_cubic = 0.044715
LANES = 128
VMEM_LIMIT = 56 * 1024 * 1024
NT = (((1,), (1,)), ((), ()))
NN = (((1,), (0,)), ((), ()))
TN = (((0,), (0,)), ((), ()))


def dot32(a, b, dims):
    return lax.dot_general(a, b, dims, preferred_element_type=jnp.float32)


def toeplitz_strip(diag_row, span):
    wide = jnp.broadcast_to(diag_row, (LANES, span))
    return pltpu.roll(wide, span - (LANES - 1), 1, stride=1, stride_axis=0)


def with_mask_lane(key_pair, lanes, here, spare, length):
    rows = lax.broadcasted_iota(jnp.int32, key_pair.shape, 0)
    mask = jnp.where(rows < length, 0.0, masked_value).astype(key_pair.dtype)
    zero = jnp.zeros_like(key_pair)
    return jnp.where(here, key_pair, jnp.where(lanes == spare, mask, zero))


def attend_kernel(head_dim, block, len_ref, diag_ref, q_ref, k_ref, v_ref, mixed_ref, lse_ref, strip, keys):
    step = pl.program_id(1)
    seq_len = k_ref.shape[0]
    span = diag_ref.shape[-1]
    length = len_ref[0]
    per = LANES // head_dim
    lanes_k = lax.broadcasted_iota(jnp.int32, (seq_len, LANES), 1)
    lanes_q = lax.broadcasted_iota(jnp.int32, (block, LANES), 1)

    @pl.when(step == 0)
    def _():
        for head in range(per):
            strip[head] = toeplitz_strip(diag_ref[head], span)
            here = lanes_k // head_dim == head
            spare = ((head + 1) % per) * head_dim
            keys[head] = with_mask_lane(k_ref[...], lanes_k, here, spare, length)

    mixed = None
    for head in range(per):
        here = lanes_q // head_dim == head
        spare = ((head + 1) % per) * head_dim
        one = (lanes_q == spare).astype(q_ref.dtype)
        query = jnp.where(here, q_ref[...], one)
        raw = dot32(query, keys[head], NT)
        parts = []
        for sub in range(block // LANES):
            offset = seq_len - LANES - (step * block + sub * LANES)
            offset = pl.multiple_of(offset, LANES)
            parts.append(raw[sub * LANES : (sub + 1) * LANES] + strip[head, :, pl.ds(offset, seq_len)])
        scores = jnp.concatenate(parts, axis=0)
        top = jnp.max(scores, axis=1, keepdims=True)
        expo = jnp.exp(scores - top)
        total = jnp.sum(expo, axis=1, keepdims=True)
        made = dot32(expo.astype(jnp.bfloat16), v_ref[...], NN) / total
        mixed = made if mixed is None else jnp.where(here, made, mixed)
        lse = jnp.broadcast_to(top + jnp.log(total), (block, LANES))
        lse_ref[head] = lse.T[:1]
    mixed_ref[...] = mixed.astype(mixed_ref.dtype)


def attend(qkv, diag, length, head_dim, by_pair=False, block=256):
    seq_len, cols = qkv.shape[0], qkv.shape[1] // 3
    pairs = cols // LANES
    per = LANES // head_dim
    span = diag.shape[-1]
    at = (lambda part, p: 3 * p + part) if by_pair else (lambda part, p: part * pairs + p)
    flops = 2 * 2 * seq_len * seq_len * LANES * 2 * cols // head_dim
    return pl.pallas_call(
        functools.partial(attend_kernel, head_dim, block),
        grid=(pairs, seq_len // block),
        in_specs=[
            pl.BlockSpec(memory_space=pltpu.SMEM),
            pl.BlockSpec((per, 1, span), lambda p, b: (p, 0, 0)),
            pl.BlockSpec((block, LANES), lambda p, b: (b, at(0, p))),
            pl.BlockSpec((seq_len, LANES), lambda p, b: (0, at(1, p))),
            pl.BlockSpec((seq_len, LANES), lambda p, b: (0, at(2, p))),
        ],
        out_specs=[
            pl.BlockSpec((block, LANES), lambda p, b: (b, p)),
            pl.BlockSpec((per, 1, block), lambda p, b: (p, 0, b)),
        ],
        out_shape=[
            jax.ShapeDtypeStruct((seq_len, cols), jnp.bfloat16),
            jax.ShapeDtypeStruct((cols // head_dim, 1, seq_len), jnp.float32),
        ],
        scratch_shapes=[
            pltpu.VMEM((per, LANES, span), jnp.float32),
            pltpu.VMEM((per, seq_len, LANES), jnp.bfloat16),
        ],
        compiler_params=pltpu.CompilerParams(vmem_limit_bytes=VMEM_LIMIT),
        cost_estimate=pl.CostEstimate(flops=flops, bytes_accessed=8 * seq_len * cols, transcendentals=0),
        name="attend",
    )(length, diag, qkv, qkv, qkv)


def attend_back_kernel(
    head_dim, block, len_ref, diag_ref, q_ref, k_ref, v_ref, do_ref, lse_ref,
    dq_ref, dk_ref, dv_ref, dd_ref, strip, keys, acc_bias, acc_k, acc_v,
):
    step = pl.program_id(1)
    steps = pl.num_programs(1)
    seq_len = k_ref.shape[0]
    span = diag_ref.shape[-1]
    length = len_ref[0]
    per = LANES // head_dim
    lanes_k = lax.broadcasted_iota(jnp.int32, (seq_len, LANES), 1)
    lanes_q = lax.broadcasted_iota(jnp.int32, (block, LANES), 1)
    subs = block // LANES

    @pl.when(step == 0)
    def _():
        for head in range(per):
            strip[head] = toeplitz_strip(diag_ref[head], span).T
            here = lanes_k // head_dim == head
            spare = ((head + 1) % per) * head_dim
            keys[head] = with_mask_lane(k_ref[...], lanes_k, here, spare, length)
        acc_bias[...] = jnp.zeros_like(acc_bias)
        acc_k[...] = jnp.zeros_like(acc_k)
        acc_v[...] = jnp.zeros_like(acc_v)

    grad_query = None
    for head in range(per):
        here = lanes_q // head_dim == head
        spare = ((head + 1) % per) * head_dim
        zero = jnp.zeros_like(q_ref[...])
        one = (lanes_q == spare).astype(q_ref.dtype)
        query = jnp.where(here, q_ref[...], zero)
        grad = jnp.where(here, do_ref[...], zero)
        raw = dot32(keys[head], query + one, NT)
        grad_probs = dot32(v_ref[...], grad, NT)
        parts = []
        offsets = []
        for sub in range(subs):
            offset = seq_len - LANES - (step * block + sub * LANES)
            offset = pl.multiple_of(offset, LANES)
            offsets.append(offset)
            parts.append(raw[:, sub * LANES : (sub + 1) * LANES] + strip[head, pl.ds(offset, seq_len), :])
        scores = jnp.concatenate(parts, axis=1)
        probs = jnp.exp(scores - lse_ref[head])
        product = probs * grad_probs
        inner = jnp.sum(product, axis=0, keepdims=True)
        grad_scores = product - probs * inner
        for sub in range(subs):
            rows = pl.ds(offsets[sub], seq_len)
            acc_bias[head, rows, :] += grad_scores[:, sub * LANES : (sub + 1) * LANES]
        rounded = grad_scores.astype(jnp.bfloat16)
        acc_v[...] += dot32(probs.astype(jnp.bfloat16), grad, NN)
        acc_k[...] += dot32(rounded, query, NN)
        made = dot32(rounded, k_ref[...], TN)
        grad_query = made if grad_query is None else jnp.where(here, made, grad_query)
    dq_ref[...] = grad_query.astype(dq_ref.dtype)

    @pl.when(step == steps - 1)
    def _():
        dk_ref[...] = acc_k[...].astype(dk_ref.dtype)
        dv_ref[...] = acc_v[...].astype(dv_ref.dtype)
        row = lax.broadcasted_iota(jnp.int32, (LANES, LANES), 0)
        col = lax.broadcasted_iota(jnp.int32, (LANES, LANES), 1)
        flip = (row + col == LANES - 1).astype(jnp.float32)
        for head in range(per):
            turned = lax.dot_general(
                flip, acc_bias[head], NT, precision=lax.Precision.HIGHEST, preferred_element_type=jnp.float32
            )
            aligned = pltpu.roll(turned, 0, 1, stride=1, stride_axis=0)
            dd_ref[head] = jnp.sum(aligned, axis=0, keepdims=True)


def attend_back(qkv, grad_mixed, lse, diag, length, head_dim, block=256):
    seq_len, cols = qkv.shape[0], qkv.shape[1] // 3
    pairs = cols // LANES
    per = LANES // head_dim
    span = diag.shape[-1]
    flops = 5 * 2 * seq_len * seq_len * LANES * 2 * cols // head_dim
    whole = lambda p, b: (0, p)
    part = lambda p, b: (b, p)
    flat = jax.ShapeDtypeStruct((seq_len, cols), jnp.bfloat16)
    return pl.pallas_call(
        functools.partial(attend_back_kernel, head_dim, block),
        grid=(pairs, seq_len // block),
        in_specs=[
            pl.BlockSpec(memory_space=pltpu.SMEM),
            pl.BlockSpec((per, 1, span), lambda p, b: (p, 0, 0)),
            pl.BlockSpec((block, LANES), part),
            pl.BlockSpec((seq_len, LANES), lambda p, b: (0, pairs + p)),
            pl.BlockSpec((seq_len, LANES), lambda p, b: (0, 2 * pairs + p)),
            pl.BlockSpec((block, LANES), part),
            pl.BlockSpec((per, 1, block), lambda p, b: (p, 0, b)),
        ],
        out_specs=[
            pl.BlockSpec((block, LANES), part),
            pl.BlockSpec((seq_len, LANES), whole),
            pl.BlockSpec((seq_len, LANES), whole),
            pl.BlockSpec((per, 1, span), lambda p, b: (p, 0, 0)),
        ],
        out_shape=[flat, flat, flat, jax.ShapeDtypeStruct(diag.shape, jnp.float32)],
        scratch_shapes=[
            pltpu.VMEM((per, span, LANES), jnp.float32),
            pltpu.VMEM((per, seq_len, LANES), jnp.bfloat16),
            pltpu.VMEM((per, span, LANES), jnp.float32),
            pltpu.VMEM((seq_len, LANES), jnp.float32),
            pltpu.VMEM((seq_len, LANES), jnp.float32),
        ],
        compiler_params=pltpu.CompilerParams(vmem_limit_bytes=VMEM_LIMIT),
        cost_estimate=pl.CostEstimate(flops=flops, bytes_accessed=16 * seq_len * cols, transcendentals=0),
        name="attend_back",
    )(length, diag, qkv, qkv, qkv, grad_mixed, lse)


def gated_values(gate, up, grad):
    square = gate * gate
    turn = jnp.tanh(gelu_scale * gate * (1.0 + gelu_cubic * square))
    half = 0.5 * (1.0 + turn)
    act = gate * half
    slope = half + 0.5 * gate * (1.0 - turn * turn) * gelu_scale * (1.0 + 3.0 * gelu_cubic * square)
    low = jnp.bfloat16
    return (grad * up * slope).astype(low), (grad * act).astype(low), (act * up).astype(low)


def ring_order(count):
    if count % 4 or count < 8:
        return list(range(count))
    long, short = 4, count // 4
    walk = []
    for line in range(long):
        columns = range(1, short) if line % 2 == 0 else range(short - 1, 0, -1)
        walk += [line * short + column for column in columns]
    return walk + [line * short for line in range(long - 1, -1, -1)]


MESH = pl.DeviceIdType.MESH


def pick(options, at):
    value = jnp.int32(options[0])
    for index in range(1, len(options)):
        value = jnp.where(at == index, jnp.int32(options[index]), value)
    return value


class Links:
    def __init__(self, count, planes):
        order = ring_order(count)
        place = [0] * count
        for at, index in enumerate(order):
            place[index] = at
        self.count, self.order, self.planes = count, order, planes
        self.place = pick(place, lax.axis_index("dp"))
        seq = lax.axis_index("seq")
        self.core = seq % 2
        self.plane = seq // 2
        self.sibling = {"seq": self.plane * 2 + 1 - self.core}
        self.across = {"seq": (1 - self.plane) * 2 + self.core}
        self.diagonal = {"seq": (1 - self.plane) * 2 + 1 - self.core}
        self.ahead = {"dp": self.owner(1)}
        self.behind = {"dp": self.owner(-1)}

    def owner(self, shift):
        return pick(self.order, lax.rem(self.place + shift + self.count, self.count))

    def greet(self, diagonal=False):
        barrier = pltpu.get_barrier_semaphore()
        friends = [self.ahead, self.behind, self.sibling] + ([self.across] if self.planes == 2 else [])
        if diagonal:
            friends.append(self.diagonal)
        for friend in friends:
            pl.semaphore_signal(barrier, inc=1, device_id=friend, device_id_type=MESH)
        pl.semaphore_wait(barrier, len(friends))


class Gather:
    def __init__(self, links, shard, whole, sems, rows, share):
        self.links, self.shard, self.whole, self.sems, self.rows = links, shard, whole, sems, rows
        self.far = links.count // 2
        self.shared = links.planes == 2
        self.share = share
        self.size = rows - share if self.shared else rows
        self.cut = -(-(self.size // 2) // 16) * 16

    def base(self, shift):
        start = self.links.owner(shift) * self.rows
        if self.shared:
            start = start + self.links.plane * self.share
        return pl.multiple_of(start, 16)

    def ring_copy(self, step, forward):
        shift = (1 - step) if forward else (step - 1)
        offset, size = 0, self.size
        if step == self.far:
            offset, size = (0, self.cut) if forward else (self.cut, self.size - self.cut)
        place = self.whole.at[pl.ds(pl.multiple_of(self.base(shift) + offset, 16), size)]
        source = place
        if step == 1:
            first = self.links.plane * self.share if self.shared else 0
            source = self.shard.at[pl.ds(pl.multiple_of(first + offset, 16), size)]
        return pltpu.make_async_remote_copy(
            src_ref=source,
            dst_ref=place,
            send_sem=self.sems.at[0 if forward else 1, step],
            recv_sem=self.sems.at[2 if forward else 3, step],
            device_id=self.links.ahead if forward else self.links.behind,
            device_id_type=MESH,
        )

    def recv_copy(self, step, forward):
        shift = -step if forward else step
        offset, size = 0, self.size
        if step == self.far:
            offset, size = (0, self.cut) if forward else (self.cut, self.size - self.cut)
        place = self.whole.at[pl.ds(pl.multiple_of(self.base(shift) + offset, 16), size)]
        return pltpu.make_async_remote_copy(
            src_ref=place,
            dst_ref=place,
            send_sem=self.sems.at[0 if forward else 1, step],
            recv_sem=self.sems.at[2 if forward else 3, step],
            device_id=self.links.ahead if forward else self.links.behind,
            device_id_type=MESH,
        )

    def across_copy(self, slot, shift, receive):
        plane = 1 - self.links.plane if receive else self.links.plane
        start = self.links.owner(shift) * self.rows + plane * (self.rows - self.share)
        place = self.whole.at[pl.ds(pl.multiple_of(start, 16), self.share)]
        return pltpu.make_async_remote_copy(
            src_ref=place,
            dst_ref=place,
            send_sem=self.sems.at[4, slot],
            recv_sem=self.sems.at[5, slot],
            device_id=self.links.across,
            device_id_type=MESH,
        )

    def start(self):
        self.ring_copy(1, True).start()
        self.ring_copy(1, False).start()

    def advance(self, step):
        last = step == self.far
        for forward in (True, False):
            self.recv_copy(step, forward).wait_recv()
            if not last:
                self.ring_copy(step + 1, forward).start()
            if self.shared and not last:
                slot = 2 * step - 2 + (0 if forward else 1)
                self.across_copy(slot, -step if forward else step, False).start()
        if self.shared and last:
            self.across_copy(2 * step - 2, step, False).start()

    def slots(self):
        shifts = []
        for step in range(1, self.far):
            shifts += [(2 * step - 2, -step), (2 * step - 1, step)]
        return shifts + [(2 * self.far - 2, self.far)]

    def finish(self):
        for step in range(1, self.far + 1):
            self.ring_copy(step, True).wait_send()
            self.ring_copy(step, False).wait_send()
        if self.shared:
            for slot, shift in self.slots():
                self.across_copy(slot, shift, False).wait_send()
                self.across_copy(slot, shift, True).wait_recv()


def gather_kernel(
    count, planes, rows, shard, small, tokens, cotangent,
    whole, smalls, tokens_there, cotangent_there, items,
    sems, sems_small, sems_core, own, item_sems,
):
    links = Links(count, planes)
    micro = tokens.shape[0]
    split = planes == 2 and tokens.shape[1] == 2
    plane, rank = links.plane, 2 * links.plane + links.core
    keep = pltpu.make_async_copy(shard, whole.at[pl.ds(pl.multiple_of(links.owner(0) * rows, 16), rows)], own.at[0])
    keep_small = pltpu.make_async_copy(small, smalls.at[pl.ds(pl.multiple_of(links.owner(0) * 16, 16), 16)], own.at[1])
    starts = [keep, keep_small]
    if split:
        starts += [pltpu.make_async_copy(tokens.at[m, plane], items.at[m, rank], own.at[2 + m]) for m in range(micro)]
    for copy in starts:
        copy.start()
    links.greet()
    large = Gather(links, shard, whole, sems, rows, 16)
    little = SmallGather(links, small, smalls, sems_small)
    little.start()
    large.start()

    def item_copy(kind, m):
        source, place, device = (
            (tokens.at[m, 1 - plane], rank, links.across),
            (tokens.at[m, plane], rank, links.sibling),
            (items.at[m, rank_across], rank_across, links.sibling),
        )[kind]
        return pltpu.make_async_remote_copy(
            src_ref=source, dst_ref=items.at[m, place], send_sem=item_sems.at[kind, m, 0],
            recv_sem=item_sems.at[kind, m, 1], device_id=device, device_id_type=MESH,
        )

    rank_across = 2 * (1 - plane) + links.core
    if split:
        for kind in range(2):
            for m in range(micro):
                item_copy(kind, m).start()
    swaps = []
    for at, (source, target) in enumerate(((tokens, tokens_there), (cotangent, cotangent_there))):
        swaps.append(
            pltpu.make_async_remote_copy(
                src_ref=source, dst_ref=target, send_sem=sems_core.at[at, 0], recv_sem=sems_core.at[at, 1],
                device_id=links.sibling, device_id_type=MESH,
            )
        )
        swaps[-1].start()
    for step in range(1, large.far + 1):
        little.advance(step)
        large.advance(step)
    if split:
        for m in range(micro):
            item_copy(0, m).wait_recv()
            item_copy(2, m).start()
    for swap in swaps:
        swap.wait()
    little.finish()
    large.finish()
    if split:
        for m in range(micro):
            item_copy(0, m).wait_send()
            for kind in range(1, 3):
                item_copy(kind, m).wait()
    for copy in starts:
        copy.wait()


class SmallGather(Gather):
    def __init__(self, links, shard, whole, sems):
        self.links, self.shard, self.whole, self.sems, self.rows = links, shard, whole, sems, 16
        self.far, self.shared, self.size, self.cut = links.count // 2, False, 16, 16

    def start(self):
        self.ring_copy(1, True).start()
        self.ring_copy(1, False).start()

    def advance(self, step):
        self.recv_copy(step, True).wait_recv()
        if step < self.far:
            self.ring_copy(step + 1, True).start()
            self.recv_copy(step, False).wait_recv()
            if step + 1 < self.far:
                self.ring_copy(step + 1, False).start()

    def finish(self):
        for step in range(1, self.far + 1):
            self.ring_copy(step, True).wait_send()
            if step < self.far:
                self.ring_copy(step, False).wait_send()


def gather_first(shard, small, tokens, cotangent, count, planes):
    rows, cols = shard.shape
    micro, _, local, depth = tokens.shape
    anywhere = pl.BlockSpec(memory_space=pl.ANY)
    dma = pltpu.SemaphoreType.DMA
    return pl.pallas_call(
        functools.partial(gather_kernel, count, planes, rows),
        in_specs=[anywhere] * 4,
        out_specs=[anywhere] * 5,
        out_shape=[
            jax.ShapeDtypeStruct((count * rows, cols), shard.dtype),
            jax.ShapeDtypeStruct((count * 16, small.shape[1]), small.dtype),
            jax.ShapeDtypeStruct(tokens.shape, tokens.dtype),
            jax.ShapeDtypeStruct(cotangent.shape, cotangent.dtype),
            jax.ShapeDtypeStruct((micro, 2 * planes, local, depth), tokens.dtype),
        ],
        scratch_shapes=[dma((6, count)), dma((4, count)), dma((2, 2)), dma((2 + micro,)), dma((3, micro, 2))],
        compiler_params=pltpu.CompilerParams(collective_id=0, has_side_effects=True),
        name="gather_first",
    )(shard, small, tokens, cotangent)


class Scatter:
    def __init__(self, links, grads, inbox, totals, mine, came, made, total, send_sems, recv_sems, near_sems, total_sems, rows):
        self.links, self.grads, self.inbox, self.totals = links, grads, inbox, totals
        self.mine, self.came, self.made, self.total = mine, came, made, total
        self.send_sems, self.recv_sems, self.near_sems, self.total_sems = send_sems, recv_sems, near_sems, total_sems
        self.rows = rows
        self.base = 0
        self.far = links.count // 2
        self.cut = -(-(rows // 2) // 16) * 16
        self.spaces = made.shape[0]

    def part(self, step, way):
        if step > 1:
            return 0, self.rows
        return (0, self.cut) if way == 0 else (self.cut, self.rows - self.cut)

    def term(self, chunk, shift, offset, size):
        start = self.links.owner(shift) * self.rows + offset
        return self.grads.at[chunk + self.base, pl.ds(pl.multiple_of(start, 16), size)]

    def hop(self, chunk, step, way):
        offset, size = self.part(step, way)
        if step == 1:
            source = self.term(chunk, self.far, offset, size)
        else:
            source = self.made.at[lax.rem(chunk, self.spaces), way, pl.ds(offset, size)]
        return pltpu.make_async_remote_copy(
            src_ref=source,
            dst_ref=self.inbox.at[chunk, way, step - 1, pl.ds(offset, size)],
            send_sem=self.send_sems.at[chunk, way, step - 1],
            recv_sem=self.recv_sems.at[chunk, way, step - 1],
            device_id=self.links.behind if way else self.links.ahead,
            device_id_type=MESH,
        )

    def near(self, chunk, step, way):
        offset, size = self.part(step, way)
        space = lax.rem(chunk, self.spaces)
        shift = (step - self.far) if way else (self.far - step)
        copies = [
            pltpu.make_async_copy(
                self.inbox.at[chunk, way, step - 1, pl.ds(offset, size)],
                self.came.at[space, way, pl.ds(offset, size)],
                self.near_sems.at[space, way, 0],
            )
        ]
        if step < self.far or way == 0:
            copies.append(
                pltpu.make_async_copy(
                    self.term(chunk, shift, 0, self.rows), self.mine.at[space, way], self.near_sems.at[space, way, 1]
                )
            )
        return copies

    def start(self, chunk):
        for way in range(2):
            self.hop(chunk, 1, way).start()

    def fetch(self, chunk, step):
        for way in range(2):
            self.hop(chunk, step, way).wait_recv()
            for copy in self.near(chunk, step, way):
                copy.start()

    def pass_on(self, chunk, step):
        space = lax.rem(chunk, self.spaces)
        for way in range(2):
            for copy in self.near(chunk, step, way):
                copy.wait()
            self.hop(chunk, step, way).wait_send()
            offset, size = self.part(step, way)
            rows = pl.ds(offset, size)
            if size < self.rows:
                other = pl.ds(0 if way else size, self.rows - size)
                self.made[space, way, other] = self.mine[space, way, other]
            self.made[space, way, rows] = add_low(self.mine[space, way, rows], self.came[space, way, rows])
            self.hop(chunk, step + 1, way).start()

    def total_copy(self, chunk):
        return pltpu.make_async_copy(self.total, self.totals.at[chunk], self.total_sems.at[0])

    def close(self, chunk):
        space = lax.rem(chunk, self.spaces)
        for way in range(2):
            for copy in self.near(chunk, self.far, way):
                copy.wait()
            self.hop(chunk, self.far, way).wait_send()

        @pl.when(chunk > 0)
        def _():
            self.total_copy(chunk - 1).wait()

        total = self.mine[space, 0].astype(jnp.float32) + self.came[space, 0].astype(jnp.float32)
        self.total[...] = (total + self.came[space, 1].astype(jnp.float32)).astype(self.total.dtype)
        self.total_copy(chunk).start()


def feed_kernel(plan, *refs):
    count, planes, rows, chunks, early, inside, micro, tile, block, groups = plan
    late = chunks - early
    normed = refs[:micro]
    (down, *rest) = refs[micro:]
    ready, shards = rest[:early], rest[early:chunks]
    rest = rest[chunks:]
    back_kept, back_got, out_kept, out_got, totals, pieces, grads, inbox = rest[:8]
    wholes = rest[8 : 8 + late]
    (
        a_all, b_all, weights, piece, stage, mine, came, made, total, out_stage,
        in_sems, piece_sems, stage_sems, fetch_sems, keep_sems, give_sems, take_sems,
        send_sems, recv_sems, near_sems, total_sems, own_sems, *gather_sems,
    ) = rest[8 + late :]
    tokens, depth = a_all.shape
    width = weights.shape[2] // 3
    tiles, blocks = tokens // tile, depth // block
    per = tiles + blocks
    front = chunks * per
    links = Links(count, planes)
    far = count // 2

    loads = [pltpu.make_async_copy(down, b_all, in_sems.at[chunks])]
    for m in range(micro):
        share = tokens // micro
        loads.append(pltpu.make_async_copy(normed[m], a_all.at[pl.ds(m * share, share)], in_sems.at[chunks + 1 + m]))
    loads += [pltpu.make_async_copy(ready[n], weights.at[n], in_sems.at[n]) for n in range(early)]
    keeps = []
    for n in range(late):
        place = wholes[n].at[pl.ds(pl.multiple_of(links.owner(0) * rows, 16), rows)]
        keeps.append(pltpu.make_async_copy(shards[n], place, own_sems.at[n]))
    for copy in loads + keeps:
        copy.start()
    links.greet()
    gathers = [Gather(links, shards[n], wholes[n], gather_sems[n], rows, rows // 3) for n in range(late)]
    scatter = Scatter(
        links, grads, inbox, totals, mine, came, made, total, send_sems, recv_sems, near_sems, total_sems, rows
    )
    for copy in loads[: 1 + micro]:
        copy.wait()

    gap_gather = max(1, 16 // far)
    gap = max(2, 20 // far)

    def load_weights(n):
        source = ready[n] if n < early else wholes[n - early]
        return pltpu.make_async_copy(source, weights.at[n], in_sems.at[n])

    def piece_copy(n, t):
        place = pl.ds(pl.multiple_of(t * tile, 16), tile)
        return pltpu.make_async_copy(piece.at[place], pieces.at[n, place], piece_sems.at[t])

    def stage_copy(n, b):
        slot = lax.rem(b, 2)
        place = pl.ds(pl.multiple_of(b * block, 16), block)
        return pltpu.make_async_copy(stage.at[slot], grads.at[n, place], stage_sems.at[slot])

    def back_rows(g, half):
        start = (2 * g + half) * tile
        return pl.ds(pl.multiple_of(start, 16), tile)

    def fetch_copy(n, t):
        half = jnp.where(lax.rem(t, 2) == 0, 1 - links.core, links.core)
        slot = lax.rem(t, 2)
        target = pl.ds(pl.multiple_of((slot * chunks + n) * tile, 16), tile)
        return pltpu.make_async_copy(pieces.at[n, back_rows(t // 2, half)], piece.at[target], fetch_sems.at[slot, n])

    def give_copy(kind, g):
        target = (back_got, out_got)[kind]
        return pltpu.make_async_remote_copy(
            src_ref=out_stage.at[kind, 0], dst_ref=target.at[g], send_sem=give_sems.at[kind], recv_sem=take_sems.at[kind, g],
            device_id=links.sibling, device_id_type=MESH,
        )

    def keep_copy(kind, g):
        target = (back_kept, out_kept)[kind]
        return pltpu.make_async_copy(out_stage.at[kind, 1], target.at[g], keep_sems.at[kind])

    items_back = 4 * groups
    last_event = per * inside + 1 + gap * far
    total_items = max(front + items_back, last_event + 1)

    def item(i, carry):
        n, j = i // per, lax.rem(i, per)

        for k in range(late):
            base = k * per
            for step in range(far + 2):

                @pl.when(i == base + step * gap_gather)
                def _(k=k, step=step):
                    if step == 0:
                        gathers[k].start()
                    elif step <= far:
                        gathers[k].advance(step)
                    else:
                        gathers[k].finish()
                        keeps[k].wait()
                        load_weights(early + k).start()

        def event(offset, act):
            past = i - per - offset

            @pl.when((past >= 0) & (past < inside * per) & (lax.rem(past + per * 64, per) == 0))
            def _():
                act(past // per)

        def begin(chunk):
            for b in (blocks - 2, blocks - 1):
                stage_copy(chunk, b).wait()
            scatter.start(chunk)

        event(0, begin)
        for step in range(1, far + 1):
            event(step * gap - 1, lambda chunk, step=step: scatter.fetch(chunk, step))
            if step < far:
                event(step * gap, lambda chunk, step=step: scatter.pass_on(chunk, step))
            else:
                event(step * gap, scatter.close)

        @pl.when((i < front) & (j == 0))
        def _():
            for m in range(chunks):

                @pl.when(n == m)
                def _(m=m):
                    load_weights(m).wait()

        @pl.when((i < front) & (j < tiles))
        def _():
            @pl.when(n > 0)
            def _():
                piece_copy(n - 1, j).wait()

            place = pl.ds(pl.multiple_of(j * tile, 16), tile)
            a, d = a_all[place], b_all[place]
            gate = dot32(a, weights[n, :, :width], NN)
            up = dot32(a, weights[n, :, width : 2 * width], NN)
            grad = dot32(d, weights[n, :, 2 * width :], NN)
            d_gate, d_up, hidden = gated_values(gate, up, grad)
            piece[place, :width] = d_gate
            piece[place, width : 2 * width] = d_up
            piece[place, 2 * width :] = hidden
            piece_copy(n, j).start()

        @pl.when((i < front) & (j >= tiles))
        def _():
            b = j - tiles

            @pl.when(b >= 2)
            def _():
                stage_copy(n, b - 2).wait()

            place = pl.ds(pl.multiple_of(b * block, LANES), block)
            slot = lax.rem(b, 2)
            first = dot32(a_all[:, place], piece[:, : 2 * width], TN)
            stage[slot, :, : 2 * width] = first.astype(stage.dtype)
            second = dot32(b_all[:, place], piece[:, 2 * width :], TN)
            stage[slot, :, 2 * width :] = second.astype(stage.dtype)
            stage_copy(n, b).start()

        @pl.when(i == front)
        def _():
            if inside < chunks:
                for b in (blocks - 2, blocks - 1):
                    stage_copy(chunks - 1, b).wait()
            for t in range(tiles):
                piece_copy(chunks - 1, t).wait()
            for m in range(chunks):
                fetch_copy(m, 0).start()

        at = i - front
        t, kind_at = at // 2, lax.rem(at + 2 * per, 2)
        for kind in range(2):

            @pl.when((at >= 0) & (at < items_back) & (kind_at == kind))
            def _(kind=kind):
                slot, g = lax.rem(t, 2), t // 2
                if kind == 0:
                    for m in range(chunks):
                        fetch_copy(m, t).wait()

                    @pl.when(t + 1 < 2 * groups)
                    def _():
                        for m in range(chunks):
                            fetch_copy(m, t + 1).start()

                columns = slice(0, 2 * width) if kind == 0 else slice(2 * width, 3 * width)
                made_sum = None
                for m in range(chunks):
                    place = pl.ds(pl.multiple_of((slot * chunks + m) * tile, 16), tile)
                    term = dot32(piece[place, columns], weights[m, :, columns], NT)
                    made_sum = term if made_sum is None else made_sum + term

                @pl.when((t >= 2) & (slot == 0))
                def _():
                    give_copy(kind, g - 1).wait_send()

                @pl.when((t >= 2) & (slot == 1))
                def _():
                    keep_copy(kind, g - 1).wait()

                out_stage[kind, slot] = made_sum.astype(out_stage.dtype)

                @pl.when(slot == 0)
                def _():
                    give_copy(kind, g).start()

                @pl.when(slot == 1)
                def _():
                    keep_copy(kind, g).start()

        return carry

    lax.fori_loop(0, total_items, item, 0)
    scatter.total_copy(inside - 1).wait()
    for kind in range(2):
        give_copy(kind, groups - 1).wait_send()
        keep_copy(kind, groups - 1).wait()
        for g in range(groups):
            give_copy(kind, g).wait_recv()


def feed(normed, down, ready, shards, count, planes, tile, inside):
    tokens, depth = down.shape
    micro = len(normed)
    rows, cols = shards[0].shape
    early, chunks = len(ready), len(ready) + len(shards)
    far = count // 2
    block = 384
    groups = tokens // (2 * tile)
    spaces = 2 if far <= 4 else chunks
    plan = (count, planes, rows, chunks, early, inside, micro, tile, block, groups)
    anywhere = pl.BlockSpec(memory_space=pl.ANY)
    low = jnp.bfloat16
    part = jax.ShapeDtypeStruct((groups, tile, depth), low)
    shapes = [part] * 4 + [
        jax.ShapeDtypeStruct((inside, rows, cols), low),
        jax.ShapeDtypeStruct((chunks, tokens, cols), low),
        jax.ShapeDtypeStruct((chunks, depth, cols), low),
        jax.ShapeDtypeStruct((chunks, 2, far, rows, cols), low),
    ]
    shapes += [jax.ShapeDtypeStruct((depth, cols), low)] * len(shards)
    dma = pltpu.SemaphoreType.DMA
    made = pl.pallas_call(
        functools.partial(feed_kernel, plan),
        in_specs=[anywhere] * (1 + micro + chunks),
        out_specs=[anywhere] * len(shapes),
        out_shape=shapes,
        scratch_shapes=[
            pltpu.VMEM((tokens, depth), low),
            pltpu.VMEM((tokens, depth), low),
            pltpu.VMEM((chunks, depth, cols), low),
            pltpu.VMEM((tokens, cols), low),
            pltpu.VMEM((2, block, cols), low),
            pltpu.VMEM((spaces, 2, rows, cols), low),
            pltpu.VMEM((spaces, 2, rows, cols), low),
            pltpu.VMEM((spaces, 2, rows, cols), low),
            pltpu.VMEM((rows, cols), low),
            pltpu.VMEM((2, 2, tile, depth), low),
            dma((chunks + 1 + micro,)),
            dma((tokens // tile,)),
            dma((2,)),
            dma((2, chunks)),
            dma((2,)),
            dma((2,)),
            dma((2, groups)),
            dma((chunks, 2, far)),
            dma((chunks, 2, far)),
            dma((spaces, 2, 2)),
            dma((1,)),
            dma((len(shards),)),
        ]
        + [dma((6, count))] * len(shards),
        compiler_params=pltpu.CompilerParams(
            collective_id=1, has_side_effects=True, vmem_limit_bytes=62 * 1024 * 1024
        ),
        cost_estimate=pl.CostEstimate(
            flops=18 * tokens * depth * cols // 3 * chunks, bytes_accessed=10 * tokens * depth, transcendentals=0
        ),
        name="feed",
    )(*normed, down, *ready, *shards)
    return (*made[:5], made[6])


def mix_ahead_kernel(
    plan, len_ref, diag_ref, made, shard, shard_2, mixes, there, lse_ref, whole, whole_2,
    qkv_v, mix_v, strip, keys, in_sems, mix_sems, own_sems, gather_sems, gather_sems_2,
):
    count, planes, rows, head_dim, block = plan
    micro, seq_len, cols = made.shape
    pairs = cols // (3 * LANES)
    plane_len = seq_len // 2
    span = diag_ref.shape[-1]
    per, wide, steps = LANES // head_dim, 3 * LANES, seq_len // block
    units = micro * pairs
    links = Links(count, planes)
    plane = links.plane
    far = count // 2
    lanes_k = lax.broadcasted_iota(jnp.int32, (seq_len, LANES), 1)
    lanes_q = lax.broadcasted_iota(jnp.int32, (block, LANES), 1)

    def at_rows(start, size):
        return pl.ds(pl.multiple_of(start, 16), size)

    def unit_load(u):
        p, m = u // micro, lax.rem(u, micro)
        source = made.at[m, :, pl.ds(pl.multiple_of(p * wide, LANES), wide)]
        return pltpu.make_async_copy(source, qkv_v.at[lax.rem(u, 2)], in_sems.at[lax.rem(u, 2)])

    def columns(p):
        return pl.ds(pl.multiple_of(p * LANES, LANES), LANES)

    def mix_copies(u):
        p, m, slot = u // micro, lax.rem(u, micro), lax.rem(u, 2)
        mine = mix_v.at[slot, at_rows(plane * plane_len, plane_len)]
        near = pltpu.make_async_copy(mine, mixes.at[m, plane, :, columns(p)], mix_sems.at[0, slot])
        beside = pltpu.make_async_remote_copy(
            src_ref=mine, dst_ref=there.at[m, plane, :, columns(p)], send_sem=mix_sems.at[1, slot],
            recv_sem=mix_sems.at[2, u], device_id=links.sibling, device_id_type=MESH,
        )
        far_away = pltpu.make_async_remote_copy(
            src_ref=mix_v.at[slot, at_rows((1 - plane) * plane_len, plane_len)],
            dst_ref=mixes.at[m, plane, :, columns(p)], send_sem=mix_sems.at[3, slot],
            recv_sem=mix_sems.at[4, u], device_id=links.across, device_id_type=MESH,
        )
        return near, beside, far_away

    def forward_copy(u):
        p, m = u // micro, lax.rem(u, micro)
        return pltpu.make_async_remote_copy(
            src_ref=mixes.at[m, 1 - plane, :, columns(p)], dst_ref=there.at[m, 1 - plane, :, columns(p)],
            send_sem=mix_sems.at[5, u], recv_sem=mix_sems.at[6, u], device_id=links.sibling, device_id_type=MESH,
        )

    def forward(u):
        p, m = u // micro, lax.rem(u, micro)
        arrived = pltpu.make_async_remote_copy(
            src_ref=mixes.at[m, 1 - plane, :, columns(p)], dst_ref=mixes.at[m, 1 - plane, :, columns(p)],
            send_sem=mix_sems.at[3, 0], recv_sem=mix_sems.at[4, u], device_id=links.across, device_id_type=MESH,
        )
        arrived.wait_recv()
        forward_copy(u).start()

    pairs_of = ((shard, whole, gather_sems), (shard_2, whole_2, gather_sems_2))
    keeps = [
        pltpu.make_async_copy(source, target.at[at_rows(links.owner(0) * rows, rows)], own_sems.at[k])
        for k, (source, target, _) in enumerate(pairs_of)
    ]
    for keep in keeps:
        keep.start()
    unit_load(jnp.int32(0)).start()
    links.greet()
    gathers = [Gather(links, source, target, sems, rows, rows // 4) for source, target, sems in pairs_of]
    gathers[0].start()
    spacing = units * steps // (2 * far)

    def item(i, carry):
        u, b = i // steps, lax.rem(i, steps)
        p, m, slot = u // micro, lax.rem(u, micro), lax.rem(u, 2)

        for step in range(1, 2 * far):

            @pl.when(i == step * spacing)
            def _(step=step):
                if step <= far:
                    gathers[0].advance(step)
                if step == far - 1:
                    gathers[1].start()
                if step > far:
                    gathers[1].advance(step - far)

        @pl.when(b == 0)
        def _():
            unit_load(u).wait()

            @pl.when(u + 1 < units)
            def _():
                unit_load(u + 1).start()

            @pl.when(u >= 2)
            def _():
                near, beside, far_away = mix_copies(u - 2)
                near.wait()
                beside.wait_send()
                far_away.wait_send()
                forward(u - 2)

            @pl.when(m == 0)
            def _():
                for head in range(per):
                    strip[head] = toeplitz_strip(diag_ref[p * per + head], span)

            length = len_ref[m]
            for head in range(per):
                here = lanes_k // head_dim == head
                spare = ((head + 1) % per) * head_dim
                keys[head] = with_mask_lane(qkv_v[slot, :, LANES : 2 * LANES], lanes_k, here, spare, length)

        place = at_rows(b * block, block)
        q_now = qkv_v[slot, place, :LANES]
        mixed = None
        for head in range(per):
            here = lanes_q // head_dim == head
            spare = ((head + 1) % per) * head_dim
            query = jnp.where(here, q_now, (lanes_q == spare).astype(q_now.dtype))
            raw = dot32(query, keys[head], NT)
            parts = []
            for sub in range(block // LANES):
                offset = pl.multiple_of(seq_len - LANES - (b * block + sub * LANES), LANES)
                parts.append(raw[sub * LANES : (sub + 1) * LANES] + strip[head, :, pl.ds(offset, seq_len)])
            scores = jnp.concatenate(parts, axis=0)
            top = jnp.max(scores, axis=1, keepdims=True)
            expo = jnp.exp(scores - top)
            total = jnp.sum(expo, axis=1, keepdims=True)
            now = dot32(expo.astype(jnp.bfloat16), qkv_v[slot, :, 2 * LANES :], NN) / total
            mixed = now if mixed is None else jnp.where(here, now, mixed)
            lse = jnp.broadcast_to(top + jnp.log(total), (block, LANES))
            at = m * pairs * per + p * per + head
            lse_ref[at, :, pl.ds(pl.multiple_of(b * block, LANES), block)] = lse.T[:1]
        mix_v[slot, place] = mixed.astype(mix_v.dtype)

        @pl.when(b == steps - 1)
        def _():
            for copy in mix_copies(u):
                copy.start()

        return carry

    lax.fori_loop(0, units * steps, item, 0)
    for u in range(max(0, units - 2), units):
        near, beside, far_away = mix_copies(jnp.int32(u))
        near.wait()
        beside.wait_send()
        far_away.wait_send()
        forward(jnp.int32(u))
    gathers[1].advance(far)
    for gather, keep in zip(gathers, keeps):
        gather.finish()
        keep.wait()
    for u in range(units):
        at = jnp.int32(u)
        mix_copies(at)[1].wait_recv()
        forward_copy(at).wait()


def mix_ahead(made, diag, lengths, shards, rows_of, head_dim, count, planes, block=256):
    micro, seq_len, cols = made.shape
    pairs, per, span = cols // (3 * LANES), LANES // head_dim, diag.shape[-1]
    plane_len, units = seq_len // 2, micro * pairs
    rows, width = shards[0].shape
    plan = (count, planes, rows, head_dim, block)
    anywhere = pl.BlockSpec(memory_space=pl.ANY)
    near = pl.BlockSpec(memory_space=pltpu.VMEM)
    low, f32 = jnp.bfloat16, jnp.float32
    dma = pltpu.SemaphoreType.DMA
    return pl.pallas_call(
        functools.partial(mix_ahead_kernel, plan),
        in_specs=[pl.BlockSpec(memory_space=pltpu.SMEM), near, anywhere, anywhere, anywhere],
        out_specs=[anywhere, anywhere, near, anywhere, anywhere],
        out_shape=[
            jax.ShapeDtypeStruct((micro, rows_of, plane_len, cols // 3), low),
            jax.ShapeDtypeStruct((micro, rows_of, plane_len, cols // 3), low),
            jax.ShapeDtypeStruct((units * per, 1, seq_len), f32),
        ]
        + [jax.ShapeDtypeStruct((count * rows, width), low)] * 2,
        scratch_shapes=[
            pltpu.VMEM((2, seq_len, 3 * LANES), low),
            pltpu.VMEM((2, seq_len, LANES), low),
            pltpu.VMEM((per, LANES, span), f32),
            pltpu.VMEM((per, seq_len, LANES), low),
            dma((2,)),
            dma((7, units)),
            dma((2,)),
            dma((6, count)),
            dma((6, count)),
        ],
        compiler_params=pltpu.CompilerParams(
            collective_id=4, has_side_effects=True, vmem_limit_bytes=VMEM_LIMIT
        ),
        name="mix_ahead",
    )(lengths, diag, made, *shards)


def resid_ahead_kernel(core_ref, own, there, w_own, w_other, tokens, tokens_there, gain, resid_ref, normed_ref):
    resid = jnp.where(pl.program_id(1) == 1, tokens[...], tokens_there[...]).astype(jnp.float32)
    resid = resid + (dot32(own[...], w_own[...], NT) + dot32(there[...], w_other[...], NT))
    root = lax.rsqrt(jnp.mean(resid * resid, axis=-1, keepdims=True) + eps)
    resid_ref[...] = resid
    normed_ref[...] = (resid * root * gain[...]).astype(normed_ref.dtype)


def resid_ahead(mixes, there, w_own, w_other, tokens, tokens_there, gain, core_at):
    groups, tile, depth = tokens.shape
    cols, pair_len = mixes.shape[2], 2 * tile
    mine = pl.BlockSpec((None, tile, depth), lambda g, h, s: (g, 0, 0))
    tall = lambda width: pl.BlockSpec((None, tile, width), lambda g, h, s: (g, lax.rem(s[0] + 1 + h, 2), 0))
    flat = lambda shape: pl.BlockSpec(shape, lambda g, h, s: (0, 0))
    last = pl.BlockSpec((depth, cols), lambda g, h, s: (0, 3))
    return pl.pallas_call(
        resid_ahead_kernel,
        grid_spec=pltpu.PrefetchScalarGridSpec(
            num_scalar_prefetch=1,
            grid=(groups, 2),
            in_specs=[tall(cols), tall(cols), last, last, mine, mine, flat((1, depth))],
            out_specs=[mine, tall(depth)],
        ),
        out_shape=[
            jax.ShapeDtypeStruct((groups, tile, depth), jnp.float32),
            jax.ShapeDtypeStruct((groups, pair_len, depth), jnp.bfloat16),
        ],
        compiler_params=pltpu.CompilerParams(vmem_limit_bytes=VMEM_LIMIT),
        name="resid_ahead",
    )(core_at, mixes, there, w_own, w_other, tokens, tokens_there, gain)


def mix_back_kernel(plan, len_ref, lse_ref, diag_ref, *refs):
    count, planes, rows, micro, rows_of, head_dim, block, pairs = plan
    qkvs, mixed, normed, made_own, made_other, attn_in, last_grads = refs[:7]
    dqkv_own, dqkv_there, dd_ref, totals, attn_there, last_totals, last_inbox = refs[7:14]
    (
        qkv_v, do_v, sums_v, attn_v, mixed_v, normed_v, grads, inbox,
        strip, keys, acc_bias, acc_k, acc_v, mine, came, made, total,
        load_sems, do_sems, attn_sems, dqkv_sems, send_sems, recv_sems, near_sems, total_sems,
        mine_2, came_2, made_2, total_2, send_2, recv_2, near_2, total_sems_2,
    ) = refs[14:]
    seq_len = do_v.shape[1]
    span = diag_ref.shape[-1]
    plane_len = seq_len // 2
    local = attn_in.shape[1]
    steps = seq_len // block
    per = LANES // head_dim
    wide = 3 * LANES
    units = pairs * micro
    links = Links(count, planes)
    far = count // 2
    plane, core = links.plane, links.core
    lanes_k = lax.broadcasted_iota(jnp.int32, (seq_len, LANES), 1)
    lanes_q = lax.broadcasted_iota(jnp.int32, (block, LANES), 1)

    def at_rows(start, size):
        return pl.ds(pl.multiple_of(start, 16), size)

    def do_copies(m):
        at = lambda p, c: do_v.at[m, at_rows((2 * p + c) * local, local)]
        far = []
        for way, (source, row, device) in enumerate(
            (
                (made_other, plane, links.sibling),
                (made_own, 1 - plane, links.across),
                (made_other, 1 - plane, links.diagonal),
            )
        ):
            far.append(
                pltpu.make_async_remote_copy(
                    src_ref=source.at[m * rows_of + row], dst_ref=at(plane, core), send_sem=do_sems.at[m, way],
                    recv_sem=do_sems.at[m, 3 + way], device_id=device, device_id_type=MESH,
                )
            )
        return far, pltpu.make_async_copy(made_own.at[m * rows_of + plane], at(plane, core), do_sems.at[m, 6])

    def attn_far():
        return pltpu.make_async_remote_copy(
            src_ref=attn_in, dst_ref=attn_there, send_sem=attn_sems.at[0], recv_sem=attn_sems.at[1],
            device_id=links.sibling, device_id_type=MESH,
        )

    def attn_loads():
        copies = []
        for m in range(micro):
            for r in range(rows_of):
                for side in range(2):
                    source = (attn_in, attn_there)[side]
                    half = core if side == 0 else 1 - core
                    start = (m * rows_of + r) * 2 * local + half * local
                    at = (m * rows_of + r) * 2 + side
                    copies.append(
                        pltpu.make_async_copy(source.at[m * rows_of + r], attn_v.at[at_rows(start, local)], attn_sems.at[4 + at])
                    )
        return copies

    mixed_load = pltpu.make_async_copy(mixed, mixed_v, attn_sems.at[2])
    normed_load = pltpu.make_async_copy(normed, normed_v, attn_sems.at[3])

    def unit_loads(m, p, slot):
        return [
            pltpu.make_async_copy(
                qkvs.at[m, :, pl.ds(pl.multiple_of((3 * p + part) * LANES, LANES), LANES)],
                qkv_v.at[slot, part],
                load_sems.at[slot, part],
            )
            for part in range(3)
        ]

    def start_unit(u):
        for copy in unit_loads(lax.rem(u, micro), u // micro, lax.rem(u, 2)):
            copy.start()

    def give_copies(u):
        p, m = u // micro, lax.rem(u, micro)
        at = m * rows_of + plane
        target = lambda ref: ref.at[at, :, pl.ds(pl.multiple_of(p * wide, LANES), wide)]
        source = lambda q, c: sums_v.at[p, m, at_rows((2 * q + c) * local, local)]
        far = []
        for way, (q, c, ref, device) in enumerate(
            (
                (plane, 1 - core, dqkv_there, links.sibling),
                (1 - plane, core, dqkv_own, links.across),
                (1 - plane, 1 - core, dqkv_there, links.diagonal),
            )
        ):
            far.append(
                pltpu.make_async_remote_copy(
                    src_ref=source(q, c), dst_ref=target(ref), send_sem=dqkv_sems.at[u, way],
                    recv_sem=dqkv_sems.at[u, 3 + way], device_id=device, device_id_type=MESH,
                )
            )
        return far, pltpu.make_async_copy(source(plane, core), target(dqkv_own), dqkv_sems.at[u, 6])

    start_unit(jnp.int32(0))
    mixed_load.start()
    normed_load.start()
    for m in range(micro):
        do_copies(m)[1].start()
    links.greet(True)
    for m in range(micro):
        for copy in do_copies(m)[0]:
            copy.start()
    attn_far().start()
    scatter = Scatter(
        links, grads, inbox, totals, mine, came, made, total, send_sems, recv_sems, near_sems, total_sems, rows
    )

    last_scatter = Scatter(
        links, last_grads, last_inbox, last_totals, mine_2, came_2, made_2, total_2, send_2, recv_2, near_2,
        total_sems_2, last_totals.shape[1],
    )
    last_scatter.base = last_grads.shape[0] - 1
    last_gap = max(2, 20 // far)
    zero = jnp.int32(0)
    last_scatter.start(zero)

    def weight_grads(group, left, right):
        for at in range(left.shape[1] // 384):
            place = slice(at * 384, (at + 1) * 384)
            made_now = dot32(left[:, place], right, TN)
            grads[group, place] = made_now.astype(grads.dtype)
        scatter.start(jnp.int32(group))

    def grads_out():
        for copy in attn_loads():
            copy.wait()
        mixed_load.wait()
        weight_grads(0, attn_v, mixed_v[...])

    def grads_pair(p):
        if p == 0:
            normed_load.wait()
        right = sums_v[p].reshape(micro * seq_len, wide)
        weight_grads(1 + p, normed_v, right)

    per_pair = micro * steps
    work = pairs * per_pair
    begins = [4] + [per_pair * (p + 1) + 3 for p in range(pairs - 1)] + [work + 2]
    gap = max(1, 8 // far)
    last = begins[-1] + 2 * far * gap

    def item(i, carry):
        u, b = i // steps, lax.rem(i, steps)
        p, m = u // micro, lax.rem(u, micro)
        slot = lax.rem(u, 2)

        @pl.when(i == 3)
        def _():
            attn_far().wait_recv()
            for copy in attn_loads():
                copy.start()

        for step in range(1, far + 1):

            @pl.when(i == step * last_gap - 1)
            def _(step=step):
                last_scatter.fetch(zero, step)

            @pl.when(i == step * last_gap)
            def _(step=step):
                if step < far:
                    last_scatter.pass_on(zero, step)
                else:
                    last_scatter.close(zero)

        for group, begin in enumerate(begins):
            g = jnp.int32(group)

            @pl.when(i == begin)
            def _(group=group):
                grads_out() if group == 0 else grads_pair(group - 1)

            for step in range(1, far + 1):

                @pl.when(i == begin + (2 * step - 1) * gap)
                def _(g=g, step=step):
                    scatter.fetch(g, step)

                @pl.when(i == begin + 2 * step * gap)
                def _(g=g, step=step):
                    if step < far:
                        scatter.pass_on(g, step)
                    else:
                        scatter.close(g)

        @pl.when((i < work) & (b == 0))
        def _():
            for copy in unit_loads(m, p, slot):
                copy.wait()

            @pl.when(u + 1 < units)
            def _():
                start_unit(u + 1)

            for k in range(micro):

                @pl.when(u == k)
                def _(k=k):
                    far_copies, near_copy = do_copies(k)
                    near_copy.wait()
                    for copy in far_copies:
                        copy.wait_recv()

            @pl.when(m == 0)
            def _():
                for head in range(per):
                    strip[head] = toeplitz_strip(diag_ref[p * per + head], span).T
                acc_bias[...] = jnp.zeros_like(acc_bias)

            length = len_ref[m]
            for head in range(per):
                here = lanes_k // head_dim == head
                spare = ((head + 1) % per) * head_dim
                keys[head] = with_mask_lane(qkv_v[slot, 1], lanes_k, here, spare, length)
            acc_k[...] = jnp.zeros_like(acc_k)
            acc_v[...] = jnp.zeros_like(acc_v)

        @pl.when(i < work)
        def _():
            place = at_rows(b * block, block)
            q_now = qkv_v[slot, 0, place]
            do_now = do_v[m, place, pl.ds(pl.multiple_of(p * LANES, LANES), LANES)]
            grad_query = None
            for head in range(per):
                here = lanes_q // head_dim == head
                spare = ((head + 1) % per) * head_dim
                blank = jnp.zeros_like(q_now)
                one = (lanes_q == spare).astype(q_now.dtype)
                query = jnp.where(here, q_now, blank)
                grad = jnp.where(here, do_now, blank)
                raw = dot32(keys[head], query + one, NT)
                grad_probs = dot32(qkv_v[slot, 2], grad, NT)
                parts, offsets = [], []
                for sub in range(block // LANES):
                    offset = pl.multiple_of(seq_len - LANES - (b * block + sub * LANES), LANES)
                    offsets.append(offset)
                    parts.append(raw[:, sub * LANES : (sub + 1) * LANES] + strip[head, pl.ds(offset, seq_len), :])
                scores = jnp.concatenate(parts, axis=1)
                lse = lse_ref[m * pairs * per + p * per + head, :, pl.ds(pl.multiple_of(b * block, LANES), block)]
                probs = jnp.exp(scores - lse)
                product = probs * grad_probs
                inner = jnp.sum(product, axis=0, keepdims=True)
                grad_scores = product - probs * inner
                for sub, offset in enumerate(offsets):
                    acc_bias[head, pl.ds(offset, seq_len), :] += grad_scores[:, sub * LANES : (sub + 1) * LANES]
                rounded = grad_scores.astype(jnp.bfloat16)
                acc_v[...] += dot32(probs.astype(jnp.bfloat16), grad, NN)
                acc_k[...] += dot32(rounded, query, NN)
                made_now = dot32(rounded, qkv_v[slot, 1], TN)
                grad_query = made_now if grad_query is None else jnp.where(here, made_now, grad_query)
            sums_v[p, m, place, :LANES] = grad_query.astype(sums_v.dtype)

        @pl.when((i < work) & (b == steps - 1))
        def _():
            sums_v[p, m, :, LANES : 2 * LANES] = acc_k[...].astype(sums_v.dtype)
            sums_v[p, m, :, 2 * LANES :] = acc_v[...].astype(sums_v.dtype)
            far_copies, near_copy = give_copies(u)
            near_copy.start()
            for copy in far_copies:
                copy.start()

            @pl.when(m == micro - 1)
            def _():
                row = lax.broadcasted_iota(jnp.int32, (LANES, LANES), 0)
                col = lax.broadcasted_iota(jnp.int32, (LANES, LANES), 1)
                flip = (row + col == LANES - 1).astype(jnp.float32)
                for head in range(per):
                    turned = lax.dot_general(
                        flip, acc_bias[head], NT, precision=highest, preferred_element_type=jnp.float32
                    )
                    aligned = pltpu.roll(turned, 0, 1, stride=1, stride_axis=0)
                    dd_ref[p * per + head] = jnp.sum(aligned, axis=0, keepdims=True)

        return carry

    lax.fori_loop(0, last + 1, item, 0)
    scatter.total_copy(jnp.int32(pairs)).wait()
    last_scatter.total_copy(zero).wait()
    for m in range(micro):
        for copy in do_copies(m)[0]:
            copy.wait_send()
    attn_far().wait_send()
    for u in range(units):
        far_copies, near_copy = give_copies(jnp.int32(u))
        near_copy.wait()
        for copy in far_copies:
            copy.wait()


def mix_back(qkvs, made_own, made_other, attn_in, mixed, normed, last_grads, lse, diag, lengths, head_dim, count, planes, block=256):
    micro, seq_len, cols = qkvs.shape
    cols = cols // 3
    rows_of = attn_in.shape[0] // micro
    _, local, depth = attn_in.shape
    pairs, per, span = cols // LANES, LANES // head_dim, diag.shape[-1]
    tokens = normed.shape[0]
    chunk_cols = last_grads.shape[2]
    rows, wide, far = depth // count, 3 * LANES, count // 2
    groups = 1 + pairs
    spaces = 2 if far <= 4 else groups
    plan = (count, planes, rows, micro, rows_of, head_dim, block, pairs)
    anywhere = pl.BlockSpec(memory_space=pl.ANY)
    low, f32 = jnp.bfloat16, jnp.float32
    dma = pltpu.SemaphoreType.DMA
    return pl.pallas_call(
        functools.partial(mix_back_kernel, plan),
        in_specs=[pl.BlockSpec(memory_space=pltpu.SMEM)]
        + [pl.BlockSpec(memory_space=pltpu.VMEM)] * 2
        + [anywhere] * 7,
        out_specs=[anywhere, anywhere, pl.BlockSpec(memory_space=pltpu.VMEM)] + [anywhere] * 4,
        out_shape=[
            jax.ShapeDtypeStruct((micro * rows_of, local, 3 * cols), low),
            jax.ShapeDtypeStruct((micro * rows_of, local, 3 * cols), low),
            jax.ShapeDtypeStruct(diag.shape, f32),
            jax.ShapeDtypeStruct((groups, rows, wide), low),
            jax.ShapeDtypeStruct(attn_in.shape, low),
            jax.ShapeDtypeStruct((1, rows, chunk_cols), low),
            jax.ShapeDtypeStruct((1, 2, far, rows, chunk_cols), low),
        ],
        scratch_shapes=[
            pltpu.VMEM((2, 3, seq_len, LANES), low),
            pltpu.VMEM((micro, seq_len, cols), low),
            pltpu.VMEM((pairs, micro, seq_len, wide), low),
            pltpu.VMEM((tokens, depth), low),
            pltpu.VMEM((tokens, cols), low),
            pltpu.VMEM((tokens, depth), low),
            pltpu.VMEM((groups, depth, wide), low),
            pltpu.VMEM((groups, 2, far, rows, wide), low),
            pltpu.VMEM((per, span, LANES), f32),
            pltpu.VMEM((per, seq_len, LANES), low),
            pltpu.VMEM((per, span, LANES), f32),
            pltpu.VMEM((seq_len, LANES), f32),
            pltpu.VMEM((seq_len, LANES), f32),
            pltpu.VMEM((spaces, 2, rows, wide), low),
            pltpu.VMEM((spaces, 2, rows, wide), low),
            pltpu.VMEM((spaces, 2, rows, wide), low),
            pltpu.VMEM((rows, wide), low),
            dma((2, 3)),
            dma((micro, 7)),
            dma((4 + 2 * micro * rows_of,)),
            dma((pairs * micro, 7)),
            dma((groups, 2, far)),
            dma((groups, 2, far)),
            dma((spaces, 2, 2)),
            dma((1,)),
            pltpu.VMEM((1, 2, rows, chunk_cols), low),
            pltpu.VMEM((1, 2, rows, chunk_cols), low),
            pltpu.VMEM((1, 2, rows, chunk_cols), low),
            pltpu.VMEM((rows, chunk_cols), low),
            dma((1, 2, far)),
            dma((1, 2, far)),
            dma((1, 2, 2)),
            dma((1,)),
        ],
        compiler_params=pltpu.CompilerParams(
            collective_id=2, has_side_effects=True, vmem_limit_bytes=62 * 1024 * 1024
        ),
        name="mix_back",
    )(lengths, lse, diag, qkvs, mixed, normed, made_own, made_other, attn_in, last_grads)


def resid_back_kernel(kept, got, out_kept, out_got, resid_ref, cot, gain, w_own, w_other, grad_ref, attn_ref, own_ref, other_ref, out_ref, sum_ref):
    @pl.when(pl.program_id(0) == 0)
    def _():
        sum_ref[...] = jnp.zeros_like(sum_ref)

    wide = jnp.float32
    resid = resid_ref[...]
    out_ref[...] = (resid + (out_kept[...].astype(wide) + out_got[...].astype(wide))).astype(out_ref.dtype)
    grad = kept[...].astype(wide) + got[...].astype(wide)
    root = lax.rsqrt(jnp.mean(resid * resid, axis=-1, keepdims=True) + eps)
    sum_ref[...] += jnp.sum(grad * resid * root, axis=0, keepdims=True)
    scaled = grad * gain[...]
    shared = jnp.mean(scaled * resid, axis=-1, keepdims=True) * root * root * root
    total = cot[...].astype(wide) + scaled * root - resid * shared
    grad_ref[...] = total
    low = total.astype(attn_ref.dtype)
    attn_ref[...] = low
    own_ref[...] = dot32(low, w_own[...], NN).astype(own_ref.dtype)
    other_ref[...] = dot32(low, w_other[...], NN).astype(other_ref.dtype)


def resid_back(kept, got, out_kept, out_got, resid, cotangent, gain, w_own, w_other):
    groups, tile, depth = kept.shape
    cols = w_own.shape[1] // 4
    tall = lambda width: pl.BlockSpec((None, tile, width), lambda g: (g, 0, 0))
    flat = lambda shape: pl.BlockSpec(shape, lambda g: (0, 0))
    low, wide = jnp.bfloat16, jnp.float32
    shape = lambda width, kind: jax.ShapeDtypeStruct((groups, tile, width), kind)
    return pl.pallas_call(
        resid_back_kernel,
        grid=(groups,),
        in_specs=[tall(depth)] * 6 + [flat((1, depth))] + [pl.BlockSpec((depth, cols), lambda g: (0, 3))] * 2,
        out_specs=[tall(depth), tall(depth), tall(cols), tall(cols), tall(depth), flat((1, depth))],
        out_shape=[
            shape(depth, wide), shape(depth, low), shape(cols, low), shape(cols, low), shape(depth, low),
            jax.ShapeDtypeStruct((1, depth), wide),
        ],
        compiler_params=pltpu.CompilerParams(vmem_limit_bytes=VMEM_LIMIT),
        name="resid_back",
    )(kept, got, out_kept, out_got, resid, cotangent, gain, w_own, w_other)


def input_back_kernel(own, there, w_own, w_other, tokens, grad_resid, gain, out_ref, sum_ref):
    @pl.when(pl.program_id(0) == 0)
    def _():
        sum_ref[...] = jnp.zeros_like(sum_ref)

    grad = dot32(own[...], w_own[...], NT) + dot32(there[...], w_other[...], NT)
    values = tokens[...].astype(jnp.float32)
    root = lax.rsqrt(jnp.mean(values * values, axis=-1, keepdims=True) + eps)
    sum_ref[...] += jnp.sum(grad * values * root, axis=0, keepdims=True)
    scaled = grad * gain[...]
    shared = jnp.mean(scaled * values, axis=-1, keepdims=True) * root * root * root
    out_ref[...] = grad_resid[...] + scaled * root - values * shared


def input_back(own, there, w_own, w_other, tokens, grad_resid, gain):
    groups, tile, depth = tokens.shape
    cols = own.shape[2]
    tall = lambda width: pl.BlockSpec((None, tile, width), lambda g: (g, 0, 0))
    flat = lambda shape: pl.BlockSpec(shape, lambda g: (0, 0))
    return pl.pallas_call(
        input_back_kernel,
        grid=(groups,),
        in_specs=[tall(cols), tall(cols), flat((depth, cols)), flat((depth, cols)), tall(depth), tall(depth), flat((1, depth))],
        out_specs=[tall(depth), flat((1, depth))],
        out_shape=[
            jax.ShapeDtypeStruct((groups, tile, depth), jnp.float32), jax.ShapeDtypeStruct((1, depth), jnp.float32)
        ],
        compiler_params=pltpu.CompilerParams(vmem_limit_bytes=VMEM_LIMIT),
        name="input_back",
    )(own, there, w_own, w_other, tokens, grad_resid, gain)


def small_sum_kernel(sizes, x_ref, o_ref, outbox, inbox, send_sems, recv_sems):
    partners = []
    for name, size in sizes:
        at, bit = lax.axis_index(name), 1
        while bit < size:
            partners.append({name: jnp.where(lax.rem(at // bit, 2) == 0, at + bit, at - bit)})
            bit *= 2
    barrier = pltpu.get_barrier_semaphore()
    for partner in partners:
        pl.semaphore_signal(barrier, inc=1, device_id=partner, device_id_type=MESH)
    pl.semaphore_wait(barrier, len(partners))
    o_ref[...] = x_ref[...]
    for at, partner in enumerate(partners):
        outbox[at] = o_ref[...]
        copy = pltpu.make_async_remote_copy(
            src_ref=outbox.at[at], dst_ref=inbox.at[at], send_sem=send_sems.at[at], recv_sem=recv_sems.at[at],
            device_id=partner, device_id_type=MESH,
        )
        copy.start()
        copy.wait()
        o_ref[...] += inbox[at]


def small_sum(values, sizes):
    rounds = sum(size.bit_length() - 1 for _, size in sizes)
    return pl.pallas_call(
        functools.partial(small_sum_kernel, sizes),
        in_specs=[pl.BlockSpec(memory_space=pltpu.VMEM)],
        out_specs=pl.BlockSpec(memory_space=pltpu.VMEM),
        out_shape=jax.ShapeDtypeStruct(values.shape, values.dtype),
        scratch_shapes=[
            pltpu.VMEM((rounds,) + values.shape, values.dtype),
            pltpu.VMEM((rounds,) + values.shape, values.dtype),
            pltpu.SemaphoreType.DMA((rounds,)),
            pltpu.SemaphoreType.DMA((rounds,)),
        ],
        compiler_params=pltpu.CompilerParams(collective_id=3, has_side_effects=True),
        name="small_sum",
    )(values)


class Ring:
    def __init__(self, count):
        order = ring_order(count)
        place = [0] * count
        for at, index in enumerate(order):
            place[index] = at
        self.count = count
        self.order = jnp.array(order, jnp.int32)
        self.here = jnp.array(place, jnp.int32)[lax.axis_index("dp")]
        self.ahead = [(order[i], order[(i + 1) % count]) for i in range(count)]
        self.behind = [(order[i], order[(i - 1) % count]) for i in range(count)]

    def owner(self, shift):
        return self.order[(self.here + shift) % self.count]

    def send(self, block, forward):
        return lax.ppermute(block, "dp", self.ahead if forward else self.behind)

    def gather(self, shard):
        rows, cols = shard.shape
        cut = cols // 2
        far = self.count // 2
        whole = jnp.zeros((self.count * rows, cols), shard.dtype)

        def put(whole, block, shift, column=0):
            return lax.dynamic_update_slice(whole, block, (self.owner(shift) * rows, column))

        whole = put(whole, shard, 0)
        ahead = behind = shard
        for step in range(1, far):
            ahead, behind = self.send(ahead, True), self.send(behind, False)
            whole = put(put(whole, ahead, -step), behind, step)
        last = (ahead, behind)
        ahead, behind = self.send(ahead[:, :cut], True), self.send(behind[:, cut:], False)
        whole = put(put(whole, ahead, -far), behind, far, cut)
        return whole, last

    def scatter(self, local, cols):
        cut = cols // 2
        far = self.count // 2
        most = local(self.owner(far))
        ahead, behind = self.send(most[:, :cut], True), self.send(most[:, cut:], False)
        for step in range(far - 1, 0, -1):
            mine = local(self.owner(step))
            other = local(self.owner(-step))
            if step == far - 1:
                ahead = jnp.concatenate([add_low(mine[:, :cut], ahead), mine[:, cut:]], axis=1)
                behind = jnp.concatenate([other[:, :cut], add_low(other[:, cut:], behind)], axis=1)
            else:
                ahead, behind = add_low(mine, ahead), add_low(other, behind)
            ahead, behind = self.send(ahead, True), self.send(behind, False)
        return local(self.owner(0)).astype(jnp.float32) + ahead.astype(jnp.float32) + behind.astype(jnp.float32)


def add_low(a, b):
    return (a.astype(jnp.float32) + b.astype(jnp.float32)).astype(jnp.bfloat16)


def body(
    tokens, cotangent, lengths, buckets, gain_one, gain_two, table,
    w_query, w_key, w_value, w_out, w_gate, w_up, w_down,
):
    micro, rows, local, width = tokens.shape
    seq_devices = lax.axis_size("seq")
    dp_devices = lax.axis_size("dp")
    seq_rank = lax.axis_index("seq")
    core = seq_rank % 2
    plane = seq_rank // 2
    planes = seq_devices // 2
    heads = table.shape[1]
    shard_rows, inner = w_query.shape
    head_dim = inner // heads
    half_inner = inner // 2
    hidden_units = w_gate.shape[1]
    pair_local = 2 * local
    seq_len = local * seq_devices
    first = core == 0
    core_pairs = [(i, i ^ 1) for i in range(seq_devices)]
    plane_groups = [[2 * p + c for p in range(planes)] for c in range(2)]
    ring = Ring(dp_devices)

    def swap_core(value):
        return lax.ppermute(value, "seq", core_pairs)

    def both_cores(own, other, axis):
        return jnp.concatenate([jnp.where(first, own, other), jnp.where(first, other, own)], axis=axis)

    def own_half(value, axis):
        return lax.dynamic_slice_in_dim(value, core * local, local, axis)

    def other_half(value, axis):
        return lax.dynamic_slice_in_dim(value, (1 - core) * local, local, axis)

    def core_columns(weight, split):
        low, high = weight[:, :split], weight[:, split:]
        high = jnp.pad(high, ((0, 0), (0, split - high.shape[1])))
        return jnp.where(first, low, high)

    chunk = 512
    chunks = -(-(hidden_units // 2) // chunk)
    split = chunks * chunk
    if split > hidden_units:
        split = hidden_units
    fused = planes == 2 and rows == 2 and half_inner % LANES == 0
    attn_parts = [core_columns(w, half_inner) for w in (w_query, w_key, w_value)]
    if fused:
        attn_parts = [w[:, p : p + LANES] for p in range(0, half_inner, LANES) for w in attn_parts]
    attn_shard = jnp.concatenate(attn_parts + [core_columns(w_out.T, half_inner)], axis=1)
    up_parts = [core_columns(w, split) for w in (w_gate, w_up, w_down.T)]
    chunk_shards = [
        jnp.concatenate([w[:, n * chunk : (n + 1) * chunk] for w in up_parts], axis=1) for n in range(chunks)
    ]

    small = jnp.concatenate([gain_one, gain_two, table.reshape(-1)])
    small = jnp.pad(small, (0, -small.shape[0] % LANES))
    small = jnp.pad(small[None], ((0, 15), (0, 0)))
    attn_weights, small, tokens_other, cotangent_other, items = gather_first(
        attn_shard, small, tokens, cotangent, dp_devices, planes
    )
    small = small.reshape(dp_devices, 16, -1)[:, 0].astype(jnp.float32)
    gain_first = small[:, :shard_rows].reshape(-1)
    gain_second = small[:, shard_rows : 2 * shard_rows].reshape(-1)
    full_table = small[:, 2 * shard_rows : 2 * shard_rows + table.size].reshape(-1, heads)
    qkv_cols = 3 * half_inner
    there_weights = swap_core(attn_weights)
    qkv_weights = attn_weights[:, :qkv_cols]
    down_in = both_cores(cotangent, cotangent_other, 2)

    core_heads = heads // 2
    head_splits = planes // rows
    item_heads = core_heads // head_splits
    item_cols = item_heads * head_dim
    padded_cols = -(-item_cols // LANES) * LANES
    padded_heads = padded_cols // head_dim
    item_row = plane // head_splits
    item_group = plane % head_splits
    head_start = core * core_heads + item_group * item_heads
    item_table = lax.dynamic_slice_in_dim(full_table, head_start, item_heads, 1)
    item_table = jnp.pad(item_table, ((0, 0), (0, padded_heads - item_heads)))
    levels = full_table.shape[0]
    bucket_hot = (buckets[:, None] == jnp.arange(levels)[None, :]).astype(jnp.float32)
    bucket_hot = jnp.pad(bucket_hot, ((0, 1), (0, 0)))
    diag = jnp.dot(item_table.T, bucket_hot.T, precision=highest)[:, None, :]

    def to_items(value, parts):
        if planes == 2 and rows == 2:
            mine = lax.dynamic_index_in_dim(value, plane, 0, keepdims=False)
            sent = lax.dynamic_index_in_dim(value, 1 - plane, 0, keepdims=False)
            got = lax.ppermute(sent, "seq", [(i, i ^ 2) for i in range(4)])
            low = plane == 0
            return jnp.concatenate([jnp.where(low, mine, got), jnp.where(low, got, mine)], axis=0)
        value = value.reshape(rows, pair_local, parts, head_splits, item_cols)
        value = value.transpose(0, 3, 1, 2, 4).reshape(planes, pair_local, parts * item_cols)
        value = lax.all_to_all(value, "seq", 0, 0, tiled=True, axis_index_groups=plane_groups)
        value = value.reshape(seq_len, parts, item_cols)
        value = jnp.pad(value, ((0, 0), (0, 0), (0, padded_cols - item_cols)))
        return value.reshape(seq_len, parts * padded_cols)

    def from_items(values):
        parts = len(values)
        if planes == 2 and rows == 2:
            value = jnp.concatenate(values, axis=1)
            mine = lax.dynamic_slice_in_dim(value, plane * pair_local, pair_local, 0)
            sent = lax.dynamic_slice_in_dim(value, (1 - plane) * pair_local, pair_local, 0)
            got = lax.ppermute(sent, "seq", [(i, i ^ 2) for i in range(4)])
            low = plane == 0
            return jnp.stack([jnp.where(low, mine, got), jnp.where(low, got, mine)])
        value = jnp.concatenate([v[:, :item_cols] for v in values], axis=1)
        value = value.reshape(planes, pair_local, parts * item_cols)
        value = lax.all_to_all(value, "seq", 0, 0, tiled=True, axis_index_groups=plane_groups)
        value = value.reshape(rows, head_splits, pair_local, parts, item_cols).transpose(0, 2, 3, 1, 4)
        return value.reshape(rows, pair_local, parts * half_inner)

    rows_in = items.reshape(micro, 1, seq_len, width) if fused else both_cores(tokens, tokens_other, 2)
    rows_in = rows_in.astype(jnp.float32)
    root = lax.rsqrt(jnp.mean(rows_in * rows_in, axis=-1, keepdims=True) + eps)
    normed = lax.optimization_barrier((rows_in * root * gain_first).astype(jnp.bfloat16))
    made = jnp.einsum("mrld,de->mrle", normed, qkv_weights, preferred_element_type=jnp.float32).astype(jnp.bfloat16)
    item_lens = lax.dynamic_slice_in_dim(lengths, item_row, 1, 1)
    if fused:
        qkvs = made[:, 0]
        mixes, mixes_there, lses, *ready = mix_ahead(
            qkvs, diag, item_lens[:, 0], chunk_shards[:2], rows, head_dim, dp_devices, planes
        )
    else:
        qkvs = [to_items(made[step], 3) for step in range(micro)]
        pairs = [attend(qkvs[step], diag, item_lens[step], head_dim) for step in range(micro)]
        lses = [lse for _, lse in pairs]
        mixes = jnp.stack([from_items([mixed]) for mixed, _ in pairs])
        mixes_there = swap_core(mixes)
        ready = [lax.all_gather(shard, "dp", axis=0, tiled=True) for shard in chunk_shards[:2]]
    early = 2
    by_pair = lambda value: value.reshape(micro * rows, pair_local, value.shape[-1])
    by_row = lambda value: value.reshape(micro * rows, local, value.shape[-1])
    resids, normed_two = resid_ahead(
        by_pair(mixes), by_pair(mixes_there), attn_weights, there_weights, by_row(tokens), by_row(tokens_other),
        gain_second[None],
        core.astype(jnp.int32)[None],
    )

    def apart(qkvs, grads_items, lses, item_lens, attn_all, mixed_all, normed_all):
        grads_qkv, diag_sum = [], 0.0
        for step in range(micro):
            grad_q, grad_k, grad_v, grad_diag = attend_back(
                qkvs[step], grads_items[step], lses[step], diag, item_lens[step], head_dim
            )
            diag_sum = diag_sum + grad_diag[:item_heads, 0]
            grads_qkv.append(from_items([grad_q, grad_k, grad_v]))
        grads_all = jnp.concatenate([flat(v) for v in grads_qkv])
        attn_all = flat(both_cores(attn_all, swap_core(attn_all), 2))
        grad_attn = jnp.einsum("td,te->de", normed_all, grads_all, preferred_element_type=jnp.float32)
        grad_o = jnp.einsum("td,te->de", attn_all, mixed_all, preferred_element_type=jnp.float32)
        both = jnp.concatenate([grad_o, grad_attn], axis=1).astype(jnp.bfloat16)
        total = ring.scatter(
            lambda index: lax.dynamic_slice_in_dim(both, index * shard_rows, shard_rows, 0), 4 * half_inner
        )
        return grads_qkv, diag_sum, total

    flat = lambda value: value.reshape(-1, value.shape[-1])
    down_all = flat(down_in)
    inside = chunks - 1 if fused else chunks
    back_kept, back_got, out_kept, out_got, chunk_totals, chunk_grads = feed(
        [flat(normed_two)], down_all, ready, chunk_shards[early:], dp_devices, planes, local, inside
    )
    grad_resid, attn_in, made_own, made_other, output, gain_two_sum = resid_back(
        back_kept, back_got, out_kept, out_got, resids, by_row(cotangent), gain_second[None], attn_weights, there_weights
    )

    if fused:
        own, there, diag_sum, attn_totals, _, last_totals, _ = mix_back(
            qkvs, made_own, made_other, attn_in, flat(mixes), flat(normed), chunk_grads, lses, diag, item_lens[:, 0],
            head_dim, dp_devices, planes,
        )
        input_grad, gain_one_sum = input_back(
            own, there, attn_weights, there_weights, by_row(tokens), grad_resid, gain_first[None]
        )
        diag_sum = diag_sum[:, 0]
    else:
        split_micro = lambda value: value.reshape(micro, rows, local, -1)
        grads_mixed = both_cores(split_micro(made_own), swap_core(split_micro(made_other)), 2)
        grads_qkv, diag_sum, attn_totals = apart(
            qkvs, [to_items(g, 1) for g in grads_mixed], lses, item_lens, split_micro(attn_in), flat(mixes), flat(normed)
        )
        grads_qkv = jnp.stack(grads_qkv)
        own = by_row(own_half(grads_qkv, 2))
        there = swap_core(by_row(other_half(grads_qkv, 2)))
        input_grad, gain_one_sum = input_back(
            own, there, attn_weights, there_weights, by_row(tokens), grad_resid, gain_first[None]
        )
    item_grad = jnp.dot(diag_sum, bucket_hot, precision=highest)
    grad_table = lax.dynamic_update_slice(jnp.zeros((heads, levels), jnp.float32), item_grad, (head_start, 0))

    def finish(total):
        if planes == 2:
            low = total.astype(jnp.bfloat16)
            got = lax.ppermute(low, "seq", [(i, i ^ 2) for i in range(4)])
            total = low.astype(jnp.float32) + got.astype(jnp.float32)
        else:
            total = lax.psum(total.astype(jnp.float32), "seq", axis_index_groups=plane_groups)
        return total, swap_core(total)

    def whole_columns(own, other, size):
        low, high = jnp.where(first, own, other), jnp.where(first, other, own)
        return jnp.concatenate([low, high[:, : size - low.shape[1]]], axis=1)

    own, other = finish(attn_totals)
    if fused:
        grad_out = whole_columns(own[0], other[0], inner)
        grad_query, grad_key, grad_value = [
            whole_columns(
                jnp.concatenate(list(own[1:, :, part * LANES : (part + 1) * LANES]), axis=1),
                jnp.concatenate(list(other[1:, :, part * LANES : (part + 1) * LANES]), axis=1),
                inner,
            )
            for part in range(3)
        ]
    else:
        parts = [slice(i * half_inner, (i + 1) * half_inner) for i in range(4)]
        grad_out, grad_query, grad_key, grad_value = [whole_columns(own[:, p], other[:, p], inner) for p in parts]
    own, other = finish(chunk_totals)
    done = [(own[n], other[n]) for n in range(inside)]
    if fused:
        own, other = finish(last_totals)
        done.append((own[0], other[0]))
    parts = [slice(i * chunk, (i + 1) * chunk) for i in range(3)]
    grad_gate, grad_up, grad_down = [
        whole_columns(
            jnp.concatenate([own[:, p] for own, _ in done], axis=1),
            jnp.concatenate([other[:, p] for _, other in done], axis=1),
            hidden_units,
        )
        for p in parts
    ]

    dp_rank = lax.axis_index("dp")
    small = jnp.concatenate([gain_one_sum[0], gain_two_sum[0], grad_table.T.reshape(-1)])
    small = jnp.pad(small, (0, -small.shape[0] % (8 * LANES))).reshape(-1, LANES)
    small = small_sum(small, (("seq", seq_devices), ("dp", dp_devices))).reshape(-1)
    grad_gain_one = lax.dynamic_slice_in_dim(small, dp_rank * shard_rows, shard_rows, 0)
    grad_gain_two = lax.dynamic_slice_in_dim(small, width + dp_rank * shard_rows, shard_rows, 0)
    table_part = levels // dp_devices
    grad_table = lax.dynamic_slice_in_dim(small[2 * width : 2 * width + levels * heads].reshape(levels, heads), dp_rank * table_part, table_part, 0)

    return (
        output.reshape(tokens.shape), input_grad.reshape(tokens.shape), grad_gain_one, grad_gain_two, grad_table,
        grad_query, grad_key, grad_value, grad_out.T, grad_gate, grad_up, grad_down.T,
    )


def solution(mesh):
    weight, turned = P("dp", None), P(None, "dp")
    return jax.shard_map(
        body,
        mesh=mesh,
        in_specs=(
            P(None, "dp", "seq", None), P(None, "dp", "seq", None), P(None, "dp"), P(), P("dp"), P("dp"),
            weight, weight, weight, weight, turned, weight, weight, turned,
        ),
        out_specs=(
            P(None, "dp", "seq", None), P(None, "dp", "seq", None), P("dp"), P("dp"),
            weight, weight, weight, weight, turned, weight, weight, turned,
        ),
        check_vma=False,
    )
```
